32 devices in a mesh: row: 2 (over x), col: 16 (over z, y, core).
Axes of the slice: x: 2, y: 2, z: 4, core: 2. Of those that a mesh axis runs over, the one named last changes fastest.
Arguments:
- sub_vectors: bfloat16 [8192, 2048], P('row', 'col'), may hold values from -6 to 6
- merge_factor: bfloat16 [128, 8192], P('row', 'col'), may hold values from -0.0625 to 0.0625
- reflectors: bfloat16 [16, 1024, 256], P('col'), may hold values from -0.1875 to 0.1875
- wy_factors: bfloat16 [16, 256, 256], P('col'), may hold values from -0.1875 to 0.1875
- owners: int32 [6], replicated, may hold values from 0 to 15, as said below
- offsets: int32 [6], replicated, may hold values from 0 to 1024, as said below
Outputs:
- eigenvectors: bfloat16 [128, 2048], P(('row', 'col'))
The draws below stay inside these ranges and needn't reach their ends.
Inputs may be any that keep to these rules, and one draw needn't show every extreme that they name: Distinct owners; 0 and 15 each own a group. `offsets`: some group starts at 0 and some at 1024.
All inputs are finite; a program needn't handle non-finite values.
Results may differ from the reference program's by a relative error of at most 0.0011.
Values may be sent and summed in bfloat16 or wider, within the bound.
No kernel may reach another device: no remote copies, remote signals or barrier semaphores. Data moves between devices by JAX's collectives and lax.ppermute only.
A program may use at most 64 MiB of HBM per device.

```python
import jax
import jax.numpy as jnp
from jax import lax

C = 8192
GL = 1024
NB = 256
GROUPS = 6
W = 128
R = 2048
SLOTS = 16


def draw_owners(key, part):
    base = jax.random.fold_in(key, 11)
    first_key, second_key = jax.random.split(base, 2)
    inner = 1 + jax.random.permutation(first_key, SLOTS - 2)[:GROUPS - 2]
    values = jnp.concatenate([jnp.array([0, SLOTS - 1], jnp.int32), inner.astype(jnp.int32)])
    order = jax.random.permutation(second_key, GROUPS)
    return values[order]


def draw_offsets(key, part):
    base = jax.random.fold_in(key, 23)
    first_key, second_key = jax.random.split(base, 2)
    inner = jax.random.randint(first_key, (GROUPS - 2,), 0, R - GL + 1).astype(jnp.int32)
    values = jnp.concatenate([jnp.array([0, R - GL], jnp.int32), inner])
    order = jax.random.permutation(second_key, GROUPS)
    return values[order]


def block_scale(own_key, extent, shards, smallest, high):
    loudness, own = 1.0, jax.random.fold_in(own_key, 6)
    for position, blocks in shards:
        draws = jnp.exp(jax.random.uniform(jax.random.fold_in(own, position), (blocks,), jnp.float32, smallest / len(shards), high / len(shards)))
        loudness = loudness * jnp.repeat(draws, extent[position] // blocks).reshape([-1 if axis == position else 1 for axis in range(len(extent))])
    return loudness


def gaussian(key, dims, scale, limit, cuts=(), held_as=jnp.bfloat16):
    values = jax.random.normal(key, dims, jnp.float32) * scale
    if len(cuts) > 0:
        values = block_scale(key, dims, cuts, -0.22, 0.18) * values
    return jnp.clip(values, min=-limit, max=limit).astype(held_as)


def setup_inputs(seed: int = 0) -> dict:
    key_list = jax.random.split(jax.random.key(seed), 7)
    return {
        "sub_vectors": gaussian(key_list[0], (C, R), 1.0, 6.0, ((0, 2), (1, 16))),
        "merge_factor": gaussian(key_list[1], (W, C), C ** -0.5, 0.0625, ((0, 2), (1, 16))),
        "reflectors": gaussian(key_list[2], (SLOTS, GL, NB), GL ** -0.5, 0.1875, ((0, 16),)),
        "wy_factors": gaussian(key_list[3], (SLOTS, NB, NB), (4 * NB) ** -0.5, 0.1875, ((0, 16),)),
        "owners": draw_owners(jax.random.fold_in(key_list[6], 71), 0),
        "offsets": draw_offsets(jax.random.fold_in(key_list[6], 71), 0),
    }


def reference(sub_vectors, merge_factor, reflectors, wy_factors, owners, offsets):
    merged = jnp.dot(merge_factor, sub_vectors, preferred_element_type=jnp.float32)
    vectors = merged
    for group_index in range(GROUPS):
        owner_now = owners[group_index].astype(jnp.int32)
        offset_now = offsets[group_index].astype(jnp.int32)
        basis = lax.dynamic_index_in_dim(reflectors, owner_now, 0, keepdims=False).astype(jnp.float32)
        factor = lax.dynamic_index_in_dim(wy_factors, owner_now, 0, keepdims=False).astype(jnp.float32)
        block = lax.dynamic_slice_in_dim(vectors, offset_now, GL, 1)
        weights = jnp.dot(block, basis, precision=lax.Precision.HIGHEST)
        scaled = jnp.dot(weights, factor.T, precision=lax.Precision.HIGHEST)
        block = block - jnp.dot(scaled, basis.T, precision=lax.Precision.HIGHEST)
        vectors = lax.dynamic_update_slice_in_dim(vectors, block, offset_now, 1)
    return vectors.astype(jnp.bfloat16)
```

```python
import jax
import jax.numpy as jnp
from jax import lax
from jax.sharding import PartitionSpec as P

GROUPS = 6


def gather_factor(merge_factor, rows, cols):
    share = cols // rows
    width = merge_factor.shape[1]
    pairs = []
    for r in range(rows):
        for c in range(cols):
            pairs.append((r * cols + c, (c // share) * cols + share * r + c % share))
    held = lax.ppermute(merge_factor, ("row", "col"), pairs)[None]
    me = lax.axis_index("col")
    bits = [1 << k for k in reversed(range(cols.bit_length() - 1))]
    for bit in bits:
        other = lax.ppermute(held, "col", [(c, c ^ bit) for c in range(cols)])
        upper = (me & bit) != 0
        first = jnp.where(upper, other, held)
        second = jnp.where(upper, held, other)
        held = jnp.concatenate([first, second], 0)
    steps = len(bits)
    shape = [2] * steps
    held = held.reshape(shape + list(merge_factor.shape))
    order = [bits[::-1].index(b) for b in sorted(bits, reverse=True)]
    held = held.transpose(order + [steps, steps + 1])
    held = held.reshape(rows, share, merge_factor.shape[0], width)
    return held.transpose(0, 2, 1, 3).reshape(rows * merge_factor.shape[0], share * width)


def local(rows, cols, sub_vectors, merge_factor, reflectors, wy_factors, owners, offsets):
    me = lax.axis_index("col")
    mine = jnp.concatenate([reflectors[0], wy_factors[0]], 0)
    low = jnp.full_like(mine, -jnp.inf)
    spread = jnp.stack([jnp.where(owners[g] == me, mine, low) for g in range(GROUPS)])
    spread = lax.pmax(spread, ("row", "col"))

    factor_part = gather_factor(merge_factor, rows, cols)
    merged = jnp.dot(factor_part, sub_vectors, preferred_element_type=jnp.float32)
    parts = rows * cols
    each = merged.shape[0] // parts
    pieces = lax.all_to_all(
        merged.reshape(parts, each, merged.shape[1]), ("row", "col"), 0, 0
    )
    pieces = pieces.reshape(rows, cols, each, merged.shape[1]).sum(0)
    vectors = pieces.transpose(1, 0, 2).reshape(each, cols * merged.shape[1])

    group_rows = reflectors.shape[1]
    for group_index in range(GROUPS):
        offset_now = offsets[group_index]
        basis_full = spread[group_index, :group_rows].astype(jnp.float32)
        factor_full = spread[group_index, group_rows:].astype(jnp.float32)
        block = lax.dynamic_slice_in_dim(vectors, offset_now, group_rows, 1)
        weights = jnp.dot(block, basis_full, precision=lax.Precision.HIGHEST)
        scaled = jnp.dot(weights, factor_full.T, precision=lax.Precision.HIGHEST)
        block = block - jnp.dot(scaled, basis_full.T, precision=lax.Precision.HIGHEST)
        vectors = lax.dynamic_update_slice_in_dim(vectors, block, offset_now, 1)
    return vectors.astype(jnp.bfloat16)


def solution(mesh):
    rows, cols = mesh.shape["row"], mesh.shape["col"]

    def body(*args):
        return local(rows, cols, *args)

    in_specs = (
        P("row", "col"),
        P("row", "col"),
        P("col", None, None),
        P("col", None, None),
        P(),
        P(),
    )
    out_specs = P(("row", "col"), None)
    return jax.shard_map(body, mesh=mesh, in_specs=in_specs, out_specs=out_specs, check_vma=False)
```

```python
import functools

import jax
import jax.numpy as jnp
from jax import lax
from jax.experimental import pallas as pl
from jax.experimental.pallas import tpu as pltpu
from jax.sharding import PartitionSpec as P

GROUPS = 6
PHASES = ((0, 1, 2), (3, 4, 5))
INNER = 4
VMEM = pl.BlockSpec(memory_space=pltpu.VMEM)
SMEM = pl.BlockSpec(memory_space=pltpu.SMEM)
ANY = pl.BlockSpec(memory_space=pl.ANY)
LIMIT = pltpu.CompilerParams(vmem_limit_bytes=40 * 1024 * 1024)


def pack_kernel(place, basis, factor, *outs):
    row_bit, inner = place[0], place[1]
    pv, pt = basis.shape[0] // (2 * INNER), factor.shape[0] // (2 * INNER)
    for mask, out in enumerate(outs):
        e = row_bit * INNER + jnp.bitwise_xor(inner, mask)
        out[:pv, :] = basis[pl.ds(pl.multiple_of(e * pv, pv), pv), :]
        out[pv:, :] = factor[pl.ds(pl.multiple_of(e * pt, pt), pt), :]


def pick_kernel(place, owners, *refs):
    n_phase = len(PHASES)
    held, outs, sems = refs[: -n_phase - 1], refs[-n_phase - 1 : -1], refs[-1]
    inner, outer = place[1], place[2]

    def copy(ref, near, group, phase, slot):
        return pltpu.make_async_copy(ref.at[near], outs[phase].at[slot], sems.at[group])

    for phase, groups in enumerate(PHASES):
        for slot, group in enumerate(groups):
            owner = owners[group]
            far = jnp.bitwise_xor(owner // INNER, outer)
            near = jnp.bitwise_xor(owner % INNER, inner)
            for mask, ref in enumerate(held):

                @pl.when(far == mask)
                def _():
                    copy(ref, near, group, phase, slot).start()

    for phase, groups in enumerate(PHASES):
        for slot, group in enumerate(groups):
            copy(held[0], 0, group, phase, slot).wait()


def merge_kernel(share, place, sub, *refs):
    held, out = refs[:-1], refs[-1]
    inner, outer = place[1], place[2]
    deep, tall = held[0].shape[2], held[0].shape[1]
    out[...] = jnp.zeros_like(out)
    for near, ref in enumerate(held):
        for far in range(ref.shape[0]):
            j = jnp.bitwise_xor(outer, far) * INNER + jnp.bitwise_xor(inner, near)
            high, low = j // share, j % share
            rows = pl.ds(pl.multiple_of(high * tall, tall), tall)
            part = jnp.dot(
                ref[far],
                sub[pl.ds(pl.multiple_of(low * deep, deep), deep), :],
                preferred_element_type=jnp.float32,
            )
            out[rows, :] = out[rows, :] + part


def two_terms(x):
    high = x.astype(jnp.bfloat16)
    low = (x - high.astype(jnp.float32)).astype(jnp.bfloat16)
    return jnp.concatenate([high, low], 0)


def both(products):
    half = products.shape[0] // 2
    return products[:half] + products[half:]


def chain_kernel(groups, masks, first, last, cols, place, offsets, start, *refs):
    held, out, basis_all, factor_all = refs[:-3], refs[-3], refs[-2], refs[-1]
    e = place[0] * INNER + place[1]
    slices = 2 * INNER
    pv, pt = basis_all.shape[1] // slices, factor_all.shape[1] // slices
    for mask, ref in zip(masks, held):
        at = jnp.bitwise_xor(e, mask)
        basis_all[:, pl.ds(pl.multiple_of(at * pv, pv), pv), :] = ref[:, :pv, :]
        factor_all[:, pl.ds(pl.multiple_of(at * pt, pt), pt), :] = ref[:, pv:, :]
    if first:
        pieces = start[...]
        n, each, width = pieces.shape
        pieces = pieces.reshape(n // cols, cols, each, width).sum(0)
        x = jnp.concatenate([pieces[c] for c in range(cols)], 1)
        x = jnp.concatenate([x] + [jnp.zeros_like(x)] * (8 // each - 1), 0)
    else:
        x = start[...]
    wide = x.shape[1]
    group_rows = basis_all.shape[1]
    before = jnp.int32(0)
    for slot, group in enumerate(groups):
        offset = offsets[group]
        x = pltpu.roll(x, lax.rem(before - offset + wide, wide), 1)
        before = offset
        block = x[:, :group_rows]
        weights = both(
            jnp.dot(two_terms(block), basis_all[slot], preferred_element_type=jnp.float32)
        )
        scaled = both(
            lax.dot_general(
                two_terms(weights), factor_all[slot], (((1,), (1,)), ((), ())),
                preferred_element_type=jnp.float32,
            )
        )
        change = both(
            lax.dot_general(
                two_terms(scaled), basis_all[slot], (((1,), (1,)), ((), ())),
                preferred_element_type=jnp.float32,
            )
        )
        x = jnp.concatenate([block - change, x[:, group_rows:]], 1)
    x = pltpu.roll(x, before, 1)
    if last:
        out[...] = x[: out.shape[0]].astype(out.dtype)
    else:
        out[...] = x


def local(rows, cols, sub_vectors, merge_factor, reflectors, wy_factors, owners, offsets):
    outers = cols // INNER
    share = cols // rows
    row, col = lax.axis_index("row"), lax.axis_index("col")
    row_bit, inner, outer = row % 2, col % INNER, col // INNER
    place = jnp.stack([row_bit, inner, outer]).astype(jnp.int32)

    def near(x, mask):
        return lax.ppermute(x, "col", [(c, c ^ mask) for c in range(cols)])

    def far(x, mask):
        return near(x, mask * INNER)

    def across(x):
        return lax.ppermute(x, "row", [(r, r ^ 1) for r in range(rows)])

    basis, factor = reflectors[0], wy_factors[0]
    group_rows, reflect = basis.shape
    pv, pt = group_rows // (2 * INNER), reflect // (2 * INNER)

    pairs = [
        (r * cols + c, (c // share) * cols + share * r + c % share)
        for r in range(rows)
        for c in range(cols)
    ]
    mine = lax.ppermute(merge_factor, ("row", "col"), pairs)
    packed = pl.pallas_call(
        pack_kernel,
        out_shape=[jax.ShapeDtypeStruct((pv + pt, reflect), basis.dtype)] * INNER,
        in_specs=[SMEM, VMEM, VMEM],
        out_specs=[VMEM] * INNER,
        name="pack",
    )(place, basis, factor)
    plane = jnp.stack([packed[0]] + [near(packed[m], m) for m in range(1, INNER)])

    m_outer = jnp.stack([mine] + [far(mine, m) for m in range(1, outers)])
    v_outer = [plane] + [far(plane, m) for m in range(1, outers)]

    m_held = [m_outer, None, near(m_outer, 2), None]
    m_held[1], m_held[3] = near(m_held[0], 1), near(m_held[2], 1)
    wanted = merge_factor.shape[0] * rows
    merged = pl.pallas_call(
        functools.partial(merge_kernel, share),
        out_shape=jax.ShapeDtypeStruct((wanted, sub_vectors.shape[1]), jnp.float32),
        in_specs=[SMEM, VMEM] + [VMEM] * INNER,
        out_specs=VMEM,
        compiler_params=LIMIT,
        name="merge",
    )(place, sub_vectors, *m_held)
    parts = rows * cols
    each = wanted // parts
    state = lax.all_to_all(merged.reshape(parts, each, merged.shape[1]), ("row", "col"), 0, 0)

    picked = pl.pallas_call(
        pick_kernel,
        out_shape=[
            jax.ShapeDtypeStruct((len(groups), pv + pt, reflect), basis.dtype)
            for groups in PHASES
        ],
        in_specs=[SMEM, SMEM] + [ANY] * outers,
        out_specs=[ANY] * len(PHASES),
        scratch_shapes=[pltpu.SemaphoreType.DMA((GROUPS,))],
        name="pick",
    )(place, owners, *v_outer)

    wide = cols * sub_vectors.shape[1]
    for phase, groups in enumerate(PHASES):
        last = phase == len(PHASES) - 1
        own = picked[phase]
        by_row, by_col = across(own), near(own, 2)
        corner = near(by_row, 2) if phase % 2 == 0 else across(by_col)
        held = [own, by_row, by_col, corner]
        masks = [0, INNER, 2, INNER + 2]
        held = held + [near(x, 1) for x in held]
        masks = masks + [m ^ 1 for m in masks]
        state = pl.pallas_call(
            functools.partial(chain_kernel, groups, masks, phase == 0, last, cols),
            out_shape=jax.ShapeDtypeStruct(
                (each, wide) if last else (8, wide), jnp.bfloat16 if last else jnp.float32
            ),
            in_specs=[SMEM, SMEM, VMEM] + [VMEM] * len(held),
            out_specs=VMEM,
            scratch_shapes=[
                pltpu.VMEM((len(groups), group_rows, reflect), basis.dtype),
                pltpu.VMEM((len(groups), reflect, reflect), basis.dtype),
            ],
            compiler_params=LIMIT,
            name=f"chain{phase}",
        )(place, offsets, state, *held)
    return state


def solution(mesh):
    rows, cols = mesh.shape["row"], mesh.shape["col"]
    in_specs = (
        P("row", "col"),
        P("row", "col"),
        P("col", None, None),
        P("col", None, None),
        P(),
        P(),
    )
    out_specs = P(("row", "col"), None)
    return jax.shard_map(
        functools.partial(local, rows, cols),
        mesh=mesh,
        in_specs=in_specs,
        out_specs=out_specs,
        check_vma=False,
    )
```

```python
import functools

import jax
import jax.numpy as jnp
from jax import lax
from jax.experimental import pallas as pl
from jax.experimental.pallas import tpu as pltpu
from jax.sharding import PartitionSpec as P

GROUPS = 6
PHASES = ((0, 1, 2), (3, 4, 5))
NEAR = 4
FAR = 4
SLICES = 2 * NEAR * FAR
LANES = 128
VMEM = pl.BlockSpec(memory_space=pltpu.VMEM)
SMEM = pl.BlockSpec(memory_space=pltpu.SMEM)
ANY = pl.BlockSpec(memory_space=pl.ANY)
LIMIT = pltpu.CompilerParams(vmem_limit_bytes=40 * 1024 * 1024)


def slice_index():
    row, col = lax.axis_index("row"), lax.axis_index("col")
    return lax.rem(row, 2) * (NEAR * FAR) + lax.rem(col, NEAR * FAR)


def aligned(index, size):
    return pl.ds(pl.multiple_of(index * size, size), size)


def pack_kernel(basis_hbm, factor_hbm, *refs):
    outs, (basis, factor, sems) = refs[:-3], refs[-3:]
    half = basis.shape[0]
    row_bit = lax.rem(lax.axis_index("row"), 2)
    first = pltpu.make_async_copy(basis_hbm.at[aligned(row_bit, half)], basis, sems.at[0])
    second = pltpu.make_async_copy(factor_hbm, factor, sems.at[1])
    first.start()
    second.start()
    first.wait()
    second.wait()
    mine = slice_index()
    pv = half // (NEAR * FAR)
    lanes = basis.shape[1] // LANES
    tall = factor.shape[0] * lanes // SLICES
    for mask, out in enumerate(outs):
        e = jnp.bitwise_xor(mine, mask)
        rows = aligned(lax.rem(e, NEAR * FAR), pv)
        for k in range(lanes):
            out[k * pv : (k + 1) * pv, :] = basis[rows, k * LANES : (k + 1) * LANES]
        out[lanes * pv :, :] = factor[aligned(e // lanes, tall), aligned(lax.rem(e, lanes), LANES)]


def pick_kernel(owners, *refs):
    held, outs = refs[: -len(PHASES)], refs[-len(PHASES) :]
    col = lax.axis_index("col")
    for phase, groups in enumerate(PHASES):
        for slot, group in enumerate(groups):
            want = jnp.bitwise_xor(owners[group], col)
            piece = held[0][...]
            for mask in range(1, len(held)):
                piece = jnp.where(want == mask, held[mask][...], piece)
            outs[phase][slot] = piece


def merge_kernel(rows, cols, sub, *refs):
    held, outs, total = refs[:NEAR], refs[NEAR:-1], refs[-1]
    row, col = lax.axis_index("row"), lax.axis_index("col")
    share = cols // rows
    deep, tall = held[0].shape[2], held[0].shape[1]
    total[...] = jnp.zeros_like(total)
    for near, ref in enumerate(held):
        for far in range(ref.shape[0]):
            j = jnp.bitwise_xor(col, far * NEAR + near)
            part = jnp.dot(
                ref[far], sub[aligned(lax.rem(j, share), deep), :],
                preferred_element_type=jnp.float32,
            )
            at = aligned(j // share, tall)
            total[at, :] = total[at, :] + part
    each = outs[0].shape[1]
    for row_mask, out in enumerate(outs):
        for col_mask in range(cols):
            to = jnp.bitwise_xor(row, row_mask) * cols + jnp.bitwise_xor(col, col_mask)
            out[col_mask] = total[pl.ds(to * each, each), :]


def add_kernel(*refs):
    count = refs[0].shape[0]
    held, outs = refs[:-count], refs[-count:]
    for mask, out in enumerate(outs):
        piece = held[0][mask]
        for ref in held[1:]:
            piece = piece + ref[mask]
        out[...] = piece


def two_terms(x):
    high = x.astype(jnp.bfloat16)
    low = (x - high.astype(jnp.float32)).astype(jnp.bfloat16)
    return jnp.concatenate([high, low], 0)


def both(products):
    half = products.shape[0] // 2
    return products[:half] + products[half:]


def chain_kernel(groups, masks, first, last, offsets, *refs):
    n_state = len(refs) - len(masks) - (4 if first else 3)
    starts, held = refs[:n_state], refs[n_state : n_state + len(masks)]
    out, basis_all, factor_all = refs[n_state + len(masks) :][:3]
    mine = slice_index()
    lanes = basis_all.shape[2] // LANES
    pv = basis_all.shape[1] // SLICES
    tall = factor_all.shape[1] * lanes // SLICES
    for mask, ref in zip(masks, held):
        for far in range(FAR):
            e = jnp.bitwise_xor(mine, mask + far * NEAR)
            for k in range(lanes):
                basis_all[:, aligned(e, pv), k * LANES : (k + 1) * LANES] = ref[
                    far, :, k * pv : (k + 1) * pv, :
                ]
            factor_all[:, aligned(e // lanes, tall), aligned(lax.rem(e, lanes), LANES)] = ref[
                far, :, lanes * pv :, :
            ]
    if first:
        state = refs[-1]
        state[...] = jnp.zeros_like(state)
        col = lax.axis_index("col")
        for mask, ref in enumerate(starts):
            state[jnp.bitwise_xor(col, mask), : ref.shape[0], :] = ref[...]
        x = jnp.concatenate([state[c] for c in range(state.shape[0])], 1)
    else:
        x = starts[0][...]
    wide = x.shape[1]
    group_rows = basis_all.shape[1]
    before = jnp.int32(0)
    for slot, group in enumerate(groups):
        offset = offsets[group]
        x = pltpu.roll(x, lax.rem(before - offset + wide, wide), 1)
        before = offset
        block = x[:, :group_rows]
        weights = both(
            jnp.dot(two_terms(block), basis_all[slot], preferred_element_type=jnp.float32)
        )
        scaled = both(
            lax.dot_general(
                two_terms(weights), factor_all[slot], (((1,), (1,)), ((), ())),
                preferred_element_type=jnp.float32,
            )
        )
        change = both(
            lax.dot_general(
                two_terms(scaled), basis_all[slot], (((1,), (1,)), ((), ())),
                preferred_element_type=jnp.float32,
            )
        )
        x = jnp.concatenate([block - change, x[:, group_rows:]], 1)
    x = pltpu.roll(x, before, 1)
    if last:
        out[...] = x[: out.shape[0]].astype(out.dtype)
    else:
        out[...] = x


def local(rows, cols, sub_vectors, merge_factor, reflectors, wy_factors, owners, offsets):
    share = cols // rows

    def over_col(x, mask):
        return lax.ppermute(x, "col", [(c, c ^ mask) for c in range(cols)])

    def over_row(x, mask):
        return lax.ppermute(x, "row", [(r, r ^ mask) for r in range(rows)])

    basis, factor = reflectors[0], wy_factors[0]
    group_rows, reflect = basis.shape
    dtype = basis.dtype
    lanes = reflect // LANES
    tall = (group_rows + reflect) * lanes // SLICES

    pairs = [
        (r * cols + c, (c // share) * cols + share * r + c % share)
        for r in range(rows)
        for c in range(cols)
    ]
    mine = lax.ppermute(merge_factor, ("row", "col"), pairs)

    packed = pl.pallas_call(
        pack_kernel,
        out_shape=[jax.ShapeDtypeStruct((tall, LANES), dtype)] * (NEAR * FAR),
        in_specs=[ANY, ANY],
        out_specs=[VMEM] * (NEAR * FAR),
        scratch_shapes=[
            pltpu.VMEM((group_rows // 2, reflect), dtype),
            pltpu.VMEM(factor.shape, dtype),
            pltpu.SemaphoreType.DMA((2,)),
        ],
        name="pack",
    )(basis, factor)
    slices = [packed[0]] + [over_col(packed[m % (NEAR * FAR)], m) for m in range(1, cols)]

    m_far = jnp.stack([mine] + [over_col(mine, m) for m in range(NEAR, cols, NEAR)])
    m_two = over_col(m_far, 2)
    m_held = [m_far, over_col(m_far, 1), m_two, over_col(m_two, 1)]
    wanted, width = merge_factor.shape[0] * rows, sub_vectors.shape[1]
    each = wanted // (rows * cols)
    parts = pl.pallas_call(
        functools.partial(merge_kernel, rows, cols),
        out_shape=[jax.ShapeDtypeStruct((cols, each, width), jnp.float32)] * rows,
        in_specs=[VMEM] + [VMEM] * NEAR,
        out_specs=[VMEM] * rows,
        scratch_shapes=[pltpu.VMEM((wanted, width), jnp.float32)],
        compiler_params=LIMIT,
        name="merge",
    )(sub_vectors, *m_held)
    parts = [parts[0]] + [over_row(parts[m], m) for m in range(1, rows)]
    pieces = pl.pallas_call(
        add_kernel,
        out_shape=[jax.ShapeDtypeStruct((each, width), jnp.float32)] * cols,
        in_specs=[VMEM] * rows,
        out_specs=[VMEM] * cols,
        name="add",
    )(*parts)
    state = [pieces[0]] + [over_col(pieces[m], m) for m in range(1, cols)]

    picked = pl.pallas_call(
        pick_kernel,
        out_shape=[
            jax.ShapeDtypeStruct((len(groups), tall, LANES), dtype) for groups in PHASES
        ],
        in_specs=[SMEM] + [VMEM] * cols,
        out_specs=[VMEM] * len(PHASES),
        name="pick",
    )(owners, *slices)

    wide = cols * width
    for phase, groups in enumerate(PHASES):
        first, last = phase == 0, phase == len(PHASES) - 1
        own = picked[phase]
        own = jnp.stack([own] + [over_col(own, m * NEAR) for m in range(1, FAR)])
        by_row, by_col = over_row(own, 1), over_col(own, 2)
        corner = over_col(by_row, 2) if phase % 2 == 0 else over_row(by_col, 1)
        held = [own, by_row, by_col, corner]
        masks = [0, NEAR * FAR, 2, NEAR * FAR + 2]
        held = held + [over_col(x, 1) for x in held]
        masks = masks + [m + 1 for m in masks]
        out = pl.pallas_call(
            functools.partial(chain_kernel, groups, masks, first, last),
            out_shape=jax.ShapeDtypeStruct(
                (each, wide) if last else (8, wide), jnp.bfloat16 if last else jnp.float32
            ),
            in_specs=[SMEM] + [VMEM] * (len(state) + len(held)),
            out_specs=VMEM,
            scratch_shapes=[
                pltpu.VMEM((len(groups), group_rows, reflect), dtype),
                pltpu.VMEM((len(groups), reflect, reflect), dtype),
            ]
            + ([pltpu.VMEM((cols, 8, width), jnp.float32)] if first else []),
            compiler_params=LIMIT,
            name=f"chain{phase}",
        )(offsets, *state, *held)
        state = [out]
    return out


def solution(mesh):
    rows, cols = mesh.shape["row"], mesh.shape["col"]
    in_specs = (
        P("row", "col"),
        P("row", "col"),
        P("col", None, None),
        P("col", None, None),
        P(),
        P(),
    )
    out_specs = P(("row", "col"), None)
    return jax.shard_map(
        functools.partial(local, rows, cols),
        mesh=mesh,
        in_specs=in_specs,
        out_specs=out_specs,
        check_vma=False,
    )
```

```python
import functools

import jax
import jax.numpy as jnp
from jax import lax
from jax.experimental import pallas as pl
from jax.experimental.pallas import tpu as pltpu
from jax.sharding import PartitionSpec as P

GROUPS = 6
PHASES = ((0, 1, 2), (3, 4, 5))
NEAR = 4
FAR = 4
SLICES = 2 * NEAR * FAR
LANES = 128
VMEM = pl.BlockSpec(memory_space=pltpu.VMEM)
SMEM = pl.BlockSpec(memory_space=pltpu.SMEM)
ANY = pl.BlockSpec(memory_space=pl.ANY)
LIMIT = pltpu.CompilerParams(vmem_limit_bytes=40 * 1024 * 1024)


def slice_index():
    row, col = lax.axis_index("row"), lax.axis_index("col")
    return lax.rem(row, 2) * (NEAR * FAR) + lax.rem(col, NEAR * FAR)


def aligned(index, size):
    return pl.ds(pl.multiple_of(index * size, size), size)


def pack_kernel(basis_hbm, factor_hbm, *refs):
    outs, (basis, factor, sems) = refs[:-3], refs[-3:]
    half = basis.shape[0]
    row_bit = lax.rem(lax.axis_index("row"), 2)
    first = pltpu.make_async_copy(basis_hbm.at[aligned(row_bit, half)], basis, sems.at[0])
    second = pltpu.make_async_copy(factor_hbm, factor, sems.at[1])
    first.start()
    second.start()
    first.wait()
    second.wait()
    mine = slice_index()
    pv = half // (NEAR * FAR)
    lanes = basis.shape[1] // LANES
    tall = factor.shape[0] * lanes // SLICES
    for near, out in enumerate(outs):
        for far in range(FAR):
            e = jnp.bitwise_xor(mine, far * NEAR + near)
            rows = aligned(lax.rem(e, NEAR * FAR), pv)
            for k in range(lanes):
                out[far, k * pv : (k + 1) * pv, :] = basis[rows, k * LANES : (k + 1) * LANES]
            out[far, lanes * pv :, :] = factor[
                aligned(e // lanes, tall), aligned(lax.rem(e, lanes), LANES)
            ]


def turn_kernel(*refs):
    count = refs[-1].shape[0]
    held, outs = refs[:count], refs[count:]
    for a, ref in enumerate(held):
        for b, out in enumerate(outs):
            out[a] = ref[b]


def turn(arrays):
    shape, dtype = arrays[0].shape, arrays[0].dtype
    return pl.pallas_call(
        turn_kernel,
        out_shape=[jax.ShapeDtypeStruct((len(arrays),) + shape[1:], dtype)] * shape[0],
        in_specs=[VMEM] * len(arrays),
        out_specs=[VMEM] * shape[0],
        name="turn",
    )(*arrays)


def pick_kernel(owners, *refs):
    held, outs = refs[: -len(PHASES)], refs[-len(PHASES) :]
    col = lax.axis_index("col")
    for phase, groups in enumerate(PHASES):
        for slot, group in enumerate(groups):
            want = jnp.bitwise_xor(owners[group], col)
            near, far = lax.rem(want, NEAR), want // NEAR
            piece = held[0][near]
            for mask in range(1, len(held)):
                piece = jnp.where(far == mask, held[mask][near], piece)
            outs[phase][slot] = piece


def merge_kernel(rows, cols, sub, *refs):
    held, outs, total = refs[:NEAR], refs[NEAR:-1], refs[-1]
    row, col = lax.axis_index("row"), lax.axis_index("col")
    share = cols // rows
    deep, tall = held[0].shape[2], held[0].shape[1]
    total[...] = jnp.zeros_like(total)
    for near, ref in enumerate(held):
        for index in range(ref.shape[0]):
            far, row_mask = index // rows, index % rows
            j = jnp.bitwise_xor(lax.rem(col, share), far * NEAR + near)
            part = jnp.dot(ref[index], sub[aligned(j, deep), :], preferred_element_type=jnp.float32)
            at = aligned(jnp.bitwise_xor(row, row_mask), tall)
            total[at, :] = total[at, :] + part
    each = outs[0].shape[1]
    for row_mask, out in enumerate(outs):
        for col_mask in range(cols):
            to = jnp.bitwise_xor(row, row_mask) * cols + jnp.bitwise_xor(col, col_mask)
            out[col_mask] = total[pl.ds(to * each, each), :]


def add_kernel(*refs):
    count = refs[0].shape[0] // NEAR
    held, outs = refs[:-count], refs[-count:]
    for far, out in enumerate(outs):
        at = slice(far * NEAR, (far + 1) * NEAR)
        piece = held[0][at]
        for ref in held[1:]:
            piece = piece + ref[at]
        out[...] = piece


def two_terms(x):
    high = x.astype(jnp.bfloat16)
    low = (x - high.astype(jnp.float32)).astype(jnp.bfloat16)
    return jnp.concatenate([high, low], 0)


def both(products):
    half = products.shape[0] // 2
    return products[:half] + products[half:]


def chain_kernel(groups, masks, first, last, offsets, *refs):
    n_state = len(refs) - len(masks) - (4 if first else 3)
    starts, held = refs[:n_state], refs[n_state : n_state + len(masks)]
    out, basis_all, factor_all = refs[n_state + len(masks) :][:3]
    mine = slice_index()
    lanes = basis_all.shape[2] // LANES
    pv = basis_all.shape[1] // SLICES
    tall = factor_all.shape[1] * lanes // SLICES
    for own_masks, ref in zip(masks, held):
        for index, mask in enumerate(own_masks):
            e = jnp.bitwise_xor(mine, mask)
            for k in range(lanes):
                basis_all[:, aligned(e, pv), k * LANES : (k + 1) * LANES] = ref[
                    index, :, k * pv : (k + 1) * pv, :
                ]
            factor_all[:, aligned(e // lanes, tall), aligned(lax.rem(e, lanes), LANES)] = ref[
                index, :, lanes * pv :, :
            ]
    if first:
        state = refs[-1]
        state[...] = jnp.zeros_like(state)
        col = lax.axis_index("col")
        for near, ref in enumerate(starts):
            for far in range(ref.shape[0]):
                at = jnp.bitwise_xor(col, far * NEAR + near)
                state[at, : ref.shape[1], :] = ref[far]
        x = jnp.concatenate([state[c] for c in range(state.shape[0])], 1)
    else:
        x = starts[0][...]
    wide = x.shape[1]
    group_rows = basis_all.shape[1]
    before = jnp.int32(0)
    for slot, group in enumerate(groups):
        offset = offsets[group]
        x = pltpu.roll(x, lax.rem(before - offset + wide, wide), 1)
        before = offset
        block = x[:, :group_rows]
        weights = both(
            jnp.dot(two_terms(block), basis_all[slot], preferred_element_type=jnp.float32)
        )
        scaled = both(
            lax.dot_general(
                two_terms(weights), factor_all[slot], (((1,), (1,)), ((), ())),
                preferred_element_type=jnp.float32,
            )
        )
        change = both(
            lax.dot_general(
                two_terms(scaled), basis_all[slot], (((1,), (1,)), ((), ())),
                preferred_element_type=jnp.float32,
            )
        )
        x = jnp.concatenate([block - change, x[:, group_rows:]], 1)
    x = pltpu.roll(x, before, 1)
    if last:
        out[...] = x[: out.shape[0]].astype(out.dtype)
    else:
        out[...] = x


def local(rows, cols, sub_vectors, merge_factor, reflectors, wy_factors, owners, offsets):
    share = cols // rows

    def over_col(x, mask):
        return lax.ppermute(x, "col", [(c, c ^ mask) for c in range(cols)])

    def over_row(x, mask):
        return lax.ppermute(x, "row", [(r, r ^ mask) for r in range(rows)])

    basis, factor = reflectors[0], wy_factors[0]
    group_rows, reflect = basis.shape
    dtype = basis.dtype
    lanes = reflect // LANES
    tall = (group_rows + reflect) * lanes // SLICES

    packed = pl.pallas_call(
        pack_kernel,
        out_shape=[jax.ShapeDtypeStruct((FAR, tall, LANES), dtype)] * NEAR,
        in_specs=[ANY, ANY],
        out_specs=[VMEM] * NEAR,
        scratch_shapes=[
            pltpu.VMEM((group_rows // 2, reflect), dtype),
            pltpu.VMEM(factor.shape, dtype),
            pltpu.SemaphoreType.DMA((2,)),
        ],
        name="pack",
    )(basis, factor)
    slices = turn([packed[0]] + [over_col(packed[m], m) for m in range(1, NEAR)])
    slices = [slices[0]] + [over_col(slices[m % FAR], m * NEAR) for m in range(1, cols // NEAR)]
    picked = pl.pallas_call(
        pick_kernel,
        out_shape=[
            jax.ShapeDtypeStruct((len(groups), tall, LANES), dtype) for groups in PHASES
        ],
        in_specs=[SMEM] + [VMEM] * len(slices),
        out_specs=[VMEM] * len(PHASES),
        name="pick",
    )(owners, *slices)

    row, top = lax.axis_index("row"), lax.axis_index("col") // share
    across = [merge_factor] + [over_col(merge_factor, m * share) for m in range(1, rows)]

    def for_row(mask):
        index = top ^ row ^ mask
        block = across[0]
        for k in range(1, rows):
            block = jnp.where(index == k, across[k], block)
        return block

    m_held = jnp.stack([for_row(0)] + [over_row(for_row(m), m) for m in range(1, rows)])
    bit = share // 2
    while bit >= NEAR:
        m_held = jnp.concatenate([m_held, over_col(m_held, bit)])
        bit //= 2
    m_two = over_col(m_held, 2)
    m_held = [m_held, over_col(m_held, 1), m_two, over_col(m_two, 1)]
    wanted, width = merge_factor.shape[0] * rows, sub_vectors.shape[1]
    each = wanted // (rows * cols)
    parts = pl.pallas_call(
        functools.partial(merge_kernel, rows, cols),
        out_shape=[jax.ShapeDtypeStruct((cols, each, width), jnp.float32)] * rows,
        in_specs=[VMEM] + [VMEM] * NEAR,
        out_specs=[VMEM] * rows,
        scratch_shapes=[pltpu.VMEM((wanted, width), jnp.float32)],
        compiler_params=LIMIT,
        name="merge",
    )(sub_vectors, *m_held)
    parts = [parts[0]] + [over_row(parts[m], m) for m in range(1, rows)]
    pieces = pl.pallas_call(
        add_kernel,
        out_shape=[jax.ShapeDtypeStruct((NEAR, each, width), jnp.float32)] * (cols // NEAR),
        in_specs=[VMEM] * rows,
        out_specs=[VMEM] * (cols // NEAR),
        name="add",
    )(*parts)
    state = turn([pieces[0]] + [over_col(pieces[m], m * NEAR) for m in range(1, cols // NEAR)])
    state = [state[0]] + [over_col(state[m], m) for m in range(1, NEAR)]

    wide = cols * width
    x_bit, y_bit, core_bit = NEAR * FAR, 2, 1
    own_masks = [m * NEAR for m in range(FAR)]
    corner_masks = [m + x_bit + y_bit for m in own_masks]
    for phase, groups in enumerate(PHASES):
        first, last = phase == 0, phase == len(PHASES) - 1
        own = picked[phase]
        own = jnp.stack([own] + [over_col(own, m) for m in own_masks[1:]])
        by_row, by_col = over_row(own, 1), over_col(own, y_bit)
        corner = jnp.concatenate(
            [over_col(by_row[: FAR // 2], y_bit), over_row(by_col[FAR // 2 :], 1)]
        )
        sides = jnp.concatenate([by_row, by_col])
        held = [own, sides, corner]
        masks = [
            own_masks,
            [m + x_bit for m in own_masks] + [m + y_bit for m in own_masks],
            corner_masks,
        ]
        held = held + [over_col(x, core_bit) for x in held]
        masks = masks + [[m + core_bit for m in ms] for ms in masks]
        out = pl.pallas_call(
            functools.partial(chain_kernel, groups, masks, first, last),
            out_shape=jax.ShapeDtypeStruct(
                (each, wide) if last else (8, wide), jnp.bfloat16 if last else jnp.float32
            ),
            in_specs=[SMEM] + [VMEM] * (len(state) + len(held)),
            out_specs=VMEM,
            scratch_shapes=[
                pltpu.VMEM((len(groups), group_rows, reflect), dtype),
                pltpu.VMEM((len(groups), reflect, reflect), dtype),
            ]
            + ([pltpu.VMEM((cols, 8, width), jnp.float32)] if first else []),
            compiler_params=LIMIT,
            name=f"chain{phase}",
        )(offsets, *state, *held)
        state = [out]
    return out


def solution(mesh):
    rows, cols = mesh.shape["row"], mesh.shape["col"]
    in_specs = (
        P("row", "col"),
        P("row", "col"),
        P("col", None, None),
        P("col", None, None),
        P(),
        P(),
    )
    out_specs = P(("row", "col"), None)
    return jax.shard_map(
        functools.partial(local, rows, cols),
        mesh=mesh,
        in_specs=in_specs,
        out_specs=out_specs,
        check_vma=False,
    )
```

```python
import functools

import jax
import jax.numpy as jnp
from jax import lax
from jax.experimental import pallas as pl
from jax.experimental.pallas import tpu as pltpu
from jax.sharding import PartitionSpec as P

GROUPS = 6
NEAR = 4
FAR = 4
SLICES = 2 * NEAR * FAR
LANES = 128
VMEM = pl.BlockSpec(memory_space=pltpu.VMEM)
SMEM = pl.BlockSpec(memory_space=pltpu.SMEM)
ANY = pl.BlockSpec(memory_space=pl.ANY)
LIMIT = pltpu.CompilerParams(vmem_limit_bytes=40 * 1024 * 1024)


def slice_index():
    row, col = lax.axis_index("row"), lax.axis_index("col")
    return lax.rem(row, 2) * (NEAR * FAR) + lax.rem(col, NEAR * FAR)


def aligned(index, size):
    return pl.ds(pl.multiple_of(index * size, size), size)


def pack_kernel(basis_hbm, factor_hbm, out, basis, factor, sems):
    half = basis.shape[0]
    row_bit = lax.rem(lax.axis_index("row"), 2)
    first = pltpu.make_async_copy(basis_hbm.at[aligned(row_bit, half)], basis, sems.at[0])
    second = pltpu.make_async_copy(factor_hbm, factor, sems.at[1])
    first.start()
    second.start()
    first.wait()
    second.wait()
    pv = half // (NEAR * FAR)
    lanes = basis.shape[1] // LANES
    tall = factor.shape[0] * lanes // SLICES
    for col in range(out.shape[0]):
        c = col % (NEAR * FAR)
        e = row_bit * (NEAR * FAR) + c
        for k in range(lanes):
            out[col, k * pv : (k + 1) * pv, :] = basis[
                c * pv : (c + 1) * pv, k * LANES : (k + 1) * LANES
            ]
        out[col, lanes * pv :, :] = factor[
            aligned(e // lanes, tall), (c % lanes) * LANES : (c % lanes + 1) * LANES
        ]


def pick_kernel(owners, held, out):
    for group in range(GROUPS):
        out[group] = held[owners[group]]


def merge_kernel(rows, cols, sub, *refs):
    held, total = refs[:NEAR], refs[NEAR]
    row, col = lax.axis_index("row"), lax.axis_index("col")
    share = cols // rows
    deep, tall = held[0].shape[2], held[0].shape[1]
    total[...] = jnp.zeros_like(total)
    for near, ref in enumerate(held):
        for index in range(ref.shape[0]):
            far, row_mask = index // rows, index % rows
            j = jnp.bitwise_xor(lax.rem(col, share), far * NEAR + near)
            part = jnp.dot(ref[index], sub[aligned(j, deep), :], preferred_element_type=jnp.float32)
            at = aligned(jnp.bitwise_xor(row, row_mask), tall)
            total[at, :] = total[at, :] + part


def two_terms(x):
    high = x.astype(jnp.bfloat16)
    low = (x - high.astype(jnp.float32)).astype(jnp.bfloat16)
    return jnp.concatenate([high, low], 0)


def both(products):
    half = products.shape[0] // 2
    return products[:half] + products[half:]


def chain_kernel(cols, masks, offsets, start, *refs):
    held, (out, basis_all, factor_all) = refs[: len(masks)], refs[len(masks) :]
    mine = slice_index()
    lanes = basis_all.shape[2] // LANES
    pv = basis_all.shape[1] // SLICES
    tall = factor_all.shape[1] * lanes // SLICES
    for own_masks, ref in zip(masks, held):
        for index, mask in enumerate(own_masks):
            e = jnp.bitwise_xor(mine, mask)
            for k in range(lanes):
                basis_all[:, aligned(e, pv), k * LANES : (k + 1) * LANES] = ref[
                    index, :, k * pv : (k + 1) * pv, :
                ]
            factor_all[:, aligned(e // lanes, tall), aligned(lax.rem(e, lanes), LANES)] = ref[
                index, :, lanes * pv :, :
            ]
    n, each, width = start.shape
    pieces = start[...].reshape(n // cols, cols, each, width).sum(0)
    x = jnp.concatenate([pieces[c] for c in range(cols)], 1)
    x = jnp.concatenate([x] + [jnp.zeros_like(x)] * (8 // each - 1), 0)
    wide = x.shape[1]
    group_rows = basis_all.shape[1]
    before = jnp.int32(0)
    for slot in range(GROUPS):
        offset = offsets[slot]
        x = pltpu.roll(x, lax.rem(before - offset + wide, wide), 1)
        before = offset
        block = x[:, :group_rows]
        weights = both(
            jnp.dot(two_terms(block), basis_all[slot], preferred_element_type=jnp.float32)
        )
        scaled = both(
            lax.dot_general(
                two_terms(weights), factor_all[slot], (((1,), (1,)), ((), ())),
                preferred_element_type=jnp.float32,
            )
        )
        change = both(
            lax.dot_general(
                two_terms(scaled), basis_all[slot], (((1,), (1,)), ((), ())),
                preferred_element_type=jnp.float32,
            )
        )
        x = jnp.concatenate([block - change, x[:, group_rows:]], 1)
    x = pltpu.roll(x, before, 1)
    out[...] = x[: out.shape[0]].astype(out.dtype)


def local(rows, cols, sub_vectors, merge_factor, reflectors, wy_factors, owners, offsets):
    share = cols // rows

    def over_col(x, mask):
        return lax.ppermute(x, "col", [(c, c ^ mask) for c in range(cols)])

    def over_row(x, mask):
        return lax.ppermute(x, "row", [(r, r ^ mask) for r in range(rows)])

    basis, factor = reflectors[0], wy_factors[0]
    group_rows, reflect = basis.shape
    dtype = basis.dtype
    lanes = reflect // LANES
    tall = (group_rows + reflect) * lanes // SLICES

    packed = pl.pallas_call(
        pack_kernel,
        out_shape=jax.ShapeDtypeStruct((cols, tall, LANES), dtype),
        in_specs=[ANY, ANY],
        out_specs=VMEM,
        scratch_shapes=[
            pltpu.VMEM((group_rows // 2, reflect), dtype),
            pltpu.VMEM(factor.shape, dtype),
            pltpu.SemaphoreType.DMA((2,)),
        ],
        name="pack",
    )(basis, factor)
    packed, merge_factor = lax.optimization_barrier((packed, merge_factor))
    slices = lax.all_to_all(packed, "col", 0, 0)
    picked = pl.pallas_call(
        pick_kernel,
        out_shape=jax.ShapeDtypeStruct((GROUPS, tall, LANES), dtype),
        in_specs=[SMEM, VMEM],
        out_specs=VMEM,
        name="pick",
    )(owners, slices)

    row, top = lax.axis_index("row"), lax.axis_index("col") // share
    across = [merge_factor] + [over_col(merge_factor, m * share) for m in range(1, rows)]

    def for_row(mask):
        index = top ^ row ^ mask
        block = across[0]
        for k in range(1, rows):
            block = jnp.where(index == k, across[k], block)
        return block

    m_held = jnp.stack([for_row(0)] + [over_row(for_row(m), m) for m in range(1, rows)])
    bit = share // 2
    while bit >= NEAR:
        m_held = jnp.concatenate([m_held, over_col(m_held, bit)])
        bit //= 2
    m_two = over_col(m_held, 2)
    m_held = [m_held, over_col(m_held, 1), m_two, over_col(m_two, 1)]
    wanted, width = merge_factor.shape[0] * rows, sub_vectors.shape[1]
    each = wanted // (rows * cols)
    merged = pl.pallas_call(
        functools.partial(merge_kernel, rows, cols),
        out_shape=jax.ShapeDtypeStruct((wanted, width), jnp.float32),
        in_specs=[VMEM] + [VMEM] * NEAR,
        out_specs=VMEM,
        compiler_params=LIMIT,
        name="merge",
    )(sub_vectors, *m_held)
    state = lax.all_to_all(merged.reshape(rows * cols, each, width), ("row", "col"), 0, 0)

    x_bit, y_bit, core_bit = NEAR * FAR, 2, 1
    own_masks = [m * NEAR for m in range(FAR)]
    own = jnp.stack([picked] + [over_col(picked, m) for m in own_masks[1:]])
    by_row, by_col = over_row(own, 1), over_col(own, y_bit)
    corner = jnp.concatenate(
        [over_col(by_row[: FAR // 2], y_bit), over_row(by_col[FAR // 2 :], 1)]
    )
    sides = jnp.concatenate([by_row, by_col])
    held = [own, sides, corner]
    masks = [
        own_masks,
        [m + x_bit for m in own_masks] + [m + y_bit for m in own_masks],
        [m + x_bit + y_bit for m in own_masks],
    ]
    held = held + [over_col(x, core_bit) for x in held]
    masks = masks + [[m + core_bit for m in ms] for ms in masks]
    return pl.pallas_call(
        functools.partial(chain_kernel, cols, masks),
        out_shape=jax.ShapeDtypeStruct((each, cols * width), jnp.bfloat16),
        in_specs=[SMEM, VMEM] + [VMEM] * len(held),
        out_specs=VMEM,
        scratch_shapes=[
            pltpu.VMEM((GROUPS, group_rows, reflect), dtype),
            pltpu.VMEM((GROUPS, reflect, reflect), dtype),
        ],
        compiler_params=LIMIT,
        name="chain",
    )(offsets, state, *held)


def solution(mesh):
    rows, cols = mesh.shape["row"], mesh.shape["col"]
    in_specs = (
        P("row", "col"),
        P("row", "col"),
        P("col", None, None),
        P("col", None, None),
        P(),
        P(),
    )
    out_specs = P(("row", "col"), None)
    return jax.shard_map(
        functools.partial(local, rows, cols),
        mesh=mesh,
        in_specs=in_specs,
        out_specs=out_specs,
        check_vma=False,
    )
```

```python
import functools

import jax
import jax.numpy as jnp
from jax import lax
from jax.experimental import pallas as pl
from jax.experimental.pallas import tpu as pltpu
from jax.sharding import PartitionSpec as P

GROUPS = 6
COLOURS = 3
NEAR = 4
FAR = 4
SLICES = 2 * NEAR * FAR
LANES = 128
VMEM = pl.BlockSpec(memory_space=pltpu.VMEM)
SMEM = pl.BlockSpec(memory_space=pltpu.SMEM)
ANY = pl.BlockSpec(memory_space=pl.ANY)
LIMIT = pltpu.CompilerParams(vmem_limit_bytes=40 * 1024 * 1024)


def slice_index():
    row, col = lax.axis_index("row"), lax.axis_index("col")
    return lax.rem(row, 2) * (NEAR * FAR) + lax.rem(col, NEAR * FAR)


def aligned(index, size):
    return pl.ds(pl.multiple_of(index * size, size), size)


def pack_kernel(basis_hbm, factor_hbm, out, basis, factor, sems):
    half = basis.shape[0]
    row_bit = lax.rem(lax.axis_index("row"), 2)
    first = pltpu.make_async_copy(basis_hbm.at[aligned(row_bit, half)], basis, sems.at[0])
    second = pltpu.make_async_copy(factor_hbm, factor, sems.at[1])
    first.start()
    second.start()
    first.wait()
    second.wait()
    pv = half // (NEAR * FAR)
    lanes = basis.shape[1] // LANES
    tall = factor.shape[0] * lanes // SLICES
    for col in range(out.shape[0]):
        c = col % (NEAR * FAR)
        e = row_bit * (NEAR * FAR) + c
        for k in range(lanes):
            out[col, k * pv : (k + 1) * pv, :] = basis[
                c * pv : (c + 1) * pv, k * LANES : (k + 1) * LANES
            ]
        out[col, lanes * pv :, :] = factor[
            aligned(e // lanes, tall), (c % lanes) * LANES : (c % lanes + 1) * LANES
        ]


def pick_kernel(owners, held, out):
    each = GROUPS // COLOURS
    for group in range(GROUPS):
        out[group // each, group % each] = held[owners[group]]


def merge_kernel(rows, cols, sub, *refs):
    held, total = refs[:NEAR], refs[NEAR]
    row, col = lax.axis_index("row"), lax.axis_index("col")
    share = cols // rows
    deep, tall = held[0].shape[2], held[0].shape[1]
    total[...] = jnp.zeros_like(total)
    for near, ref in enumerate(held):
        for index in range(ref.shape[0]):
            far, row_mask = index // rows, index % rows
            j = jnp.bitwise_xor(lax.rem(col, share), far * NEAR + near)
            part = jnp.dot(ref[index], sub[aligned(j, deep), :], preferred_element_type=jnp.float32)
            at = aligned(jnp.bitwise_xor(row, row_mask), tall)
            total[at, :] = total[at, :] + part


def two_terms(x):
    high = x.astype(jnp.bfloat16)
    low = (x - high.astype(jnp.float32)).astype(jnp.bfloat16)
    return jnp.concatenate([high, low], 0)


def both(products):
    half = products.shape[0] // 2
    return products[:half] + products[half:]


def chain_kernel(cols, groups, masks, first, last, offsets, start, *refs):
    held, (out, basis_all, factor_all) = refs[: len(masks)], refs[len(masks) :]
    mine = slice_index()
    lanes = basis_all.shape[2] // LANES
    pv = basis_all.shape[1] // SLICES
    tall = factor_all.shape[1] * lanes // SLICES
    for own_masks, ref in zip(masks, held):
        for index, mask in enumerate(own_masks):
            e = jnp.bitwise_xor(mine, mask)
            for k in range(lanes):
                basis_all[:, aligned(e, pv), k * LANES : (k + 1) * LANES] = ref[
                    index, :, k * pv : (k + 1) * pv, :
                ]
            factor_all[:, aligned(e // lanes, tall), aligned(lax.rem(e, lanes), LANES)] = ref[
                index, :, lanes * pv :, :
            ]
    if first:
        n, each, width = start.shape
        pieces = start[...].reshape(n // cols, cols, each, width).sum(0)
        x = jnp.concatenate([pieces[c] for c in range(cols)], 1)
        x = jnp.concatenate([x] + [jnp.zeros_like(x)] * (8 // each - 1), 0)
    else:
        x = start[...]
    wide = x.shape[1]
    group_rows = basis_all.shape[1]
    before = jnp.int32(0)
    for slot, group in enumerate(groups):
        offset = offsets[group]
        x = pltpu.roll(x, lax.rem(before - offset + wide, wide), 1)
        before = offset
        block = x[:, :group_rows]
        weights = both(
            jnp.dot(two_terms(block), basis_all[slot], preferred_element_type=jnp.float32)
        )
        scaled = both(
            lax.dot_general(
                two_terms(weights), factor_all[slot], (((1,), (1,)), ((), ())),
                preferred_element_type=jnp.float32,
            )
        )
        change = both(
            lax.dot_general(
                two_terms(scaled), basis_all[slot], (((1,), (1,)), ((), ())),
                preferred_element_type=jnp.float32,
            )
        )
        x = jnp.concatenate([block - change, x[:, group_rows:]], 1)
    x = pltpu.roll(x, before, 1)
    if last:
        out[...] = x[: out.shape[0]].astype(out.dtype)
    else:
        out[...] = x


def local(rows, cols, sub_vectors, merge_factor, reflectors, wy_factors, owners, offsets):
    share = cols // rows

    def over_col(x, mask):
        return lax.ppermute(x, "col", [(c, c ^ mask) for c in range(cols)])

    def over_row(x, mask):
        return lax.ppermute(x, "row", [(r, r ^ mask) for r in range(rows)])

    basis, factor = reflectors[0], wy_factors[0]
    group_rows, reflect = basis.shape
    dtype = basis.dtype
    lanes = reflect // LANES
    tall = (group_rows + reflect) * lanes // SLICES

    packed = pl.pallas_call(
        pack_kernel,
        out_shape=jax.ShapeDtypeStruct((cols, tall, LANES), dtype),
        in_specs=[ANY, ANY],
        out_specs=VMEM,
        scratch_shapes=[
            pltpu.VMEM((group_rows // 2, reflect), dtype),
            pltpu.VMEM(factor.shape, dtype),
            pltpu.SemaphoreType.DMA((2,)),
        ],
        name="pack",
    )(basis, factor)
    row, top = lax.axis_index("row"), lax.axis_index("col") // share
    across = [merge_factor] + [over_col(merge_factor, m * share) for m in range(1, rows)]
    packed, across = lax.optimization_barrier((packed, across))

    def for_row(mask):
        index = top ^ row ^ mask
        block = across[0]
        for k in range(1, rows):
            block = jnp.where(index == k, across[k], block)
        return block

    m_held = [for_row(0)] + [over_row(for_row(m), m) for m in range(1, rows)]
    slices = lax.all_to_all(packed, "col", 0, 0)
    slices, m_held = lax.optimization_barrier((slices, m_held))
    m_held = jnp.stack(m_held)
    picked = pl.pallas_call(
        pick_kernel,
        out_shape=jax.ShapeDtypeStruct((COLOURS, GROUPS // COLOURS, tall, LANES), dtype),
        in_specs=[SMEM, VMEM],
        out_specs=VMEM,
        name="pick",
    )(owners, slices)

    z_two = over_col(picked, 2 * NEAR)
    bit = share // 2
    while bit >= NEAR:
        m_held = jnp.concatenate([m_held, over_col(m_held, bit)])
        bit //= 2
    z_two, m_held = lax.optimization_barrier((z_two, m_held))
    m_two = over_col(m_held, 2)
    m_held = [m_held, over_col(m_held, 1), m_two, over_col(m_two, 1)]

    links = [
        (NEAR * FAR, lambda v: over_row(v, 1)),
        (2, lambda v: over_col(v, 2)),
        (NEAR, lambda v: over_col(v, NEAR)),
    ]
    colours = [jnp.stack([picked[k], z_two[k]]) for k in range(COLOURS)]
    masks = [[0, 2 * NEAR] for _ in range(COLOURS)]
    for step in range(2):
        for k in range(COLOURS):
            mask, send = links[(k + step) % 3]
            colours[k] = jnp.concatenate([colours[k], send(colours[k])])
            masks[k] = masks[k] + [m ^ mask for m in masks[k]]
    held, held_masks = [], []
    for k in range(COLOURS):
        mask, send = links[(k + 2) % 3]
        held.append([colours[k], send(colours[k])])
        held_masks.append([masks[k], [m ^ mask for m in masks[k]]])
    for k in range(COLOURS):
        held[k] += [over_col(v, 1) for v in held[k]]
        held_masks[k] += [[m ^ 1 for m in ms] for ms in held_masks[k]]

    wanted, width = merge_factor.shape[0] * rows, sub_vectors.shape[1]
    each = wanted // (rows * cols)
    merged = pl.pallas_call(
        functools.partial(merge_kernel, rows, cols),
        out_shape=jax.ShapeDtypeStruct((wanted, width), jnp.float32),
        in_specs=[VMEM] + [VMEM] * NEAR,
        out_specs=VMEM,
        compiler_params=LIMIT,
        name="merge",
    )(sub_vectors, *m_held)
    state = lax.all_to_all(merged.reshape(rows * cols, each, width), ("row", "col"), 0, 0)

    wide = cols * width
    for k in range(COLOURS):
        first, last = k == 0, k == COLOURS - 1
        per = GROUPS // COLOURS
        groups = range(k * per, (k + 1) * per)
        state = pl.pallas_call(
            functools.partial(chain_kernel, cols, groups, held_masks[k], first, last),
            out_shape=jax.ShapeDtypeStruct(
                (each, wide) if last else (8, wide), jnp.bfloat16 if last else jnp.float32
            ),
            in_specs=[SMEM, VMEM] + [VMEM] * len(held[k]),
            out_specs=VMEM,
            scratch_shapes=[
                pltpu.VMEM((per, group_rows, reflect), dtype),
                pltpu.VMEM((per, reflect, reflect), dtype),
            ],
            compiler_params=LIMIT,
            name=f"chain{k}",
        )(offsets, state, *held[k])
    return state


def solution(mesh):
    rows, cols = mesh.shape["row"], mesh.shape["col"]
    in_specs = (
        P("row", "col"),
        P("row", "col"),
        P("col", None, None),
        P("col", None, None),
        P(),
        P(),
    )
    out_specs = P(("row", "col"), None)
    return jax.shard_map(
        functools.partial(local, rows, cols),
        mesh=mesh,
        in_specs=in_specs,
        out_specs=out_specs,
        check_vma=False,
    )
```

```python
import functools

import jax
import jax.numpy as jnp
from jax import lax
from jax.experimental import pallas as pl
from jax.experimental.pallas import tpu as pltpu
from jax.sharding import PartitionSpec as P

GROUPS = 6
COLOURS = 3
HALF = 8
SLICES = 2 * HALF
LANES = 128
VMEM = pl.BlockSpec(memory_space=pltpu.VMEM)
SMEM = pl.BlockSpec(memory_space=pltpu.SMEM)
ANY = pl.BlockSpec(memory_space=pl.ANY)


def limit(mib):
    return pltpu.CompilerParams(vmem_limit_bytes=mib * 1024 * 1024)


def slice_index():
    row, col = lax.axis_index("row"), lax.axis_index("col")
    return lax.rem(row, 2) * HALF + lax.rem(col, HALF)


def aligned(index, size):
    return pl.ds(pl.multiple_of(index * size, size), size)


def pack_kernel(basis_hbm, factor_hbm, out, basis, factor, sems):
    row_bit = lax.rem(lax.axis_index("row"), 2)
    first = pltpu.make_async_copy(
        basis_hbm.at[aligned(row_bit, basis.shape[0])], basis, sems.at[0]
    )
    second = pltpu.make_async_copy(
        factor_hbm.at[aligned(row_bit, factor.shape[0])], factor, sems.at[1]
    )
    first.start()
    second.start()
    first.wait()
    second.wait()
    pv, pt = basis.shape[0] // HALF, factor.shape[0] // HALF
    lanes = basis.shape[1] // LANES
    for c in range(HALF):
        for k in range(lanes):
            at = slice(k * LANES, (k + 1) * LANES)
            out[c, k * pv : (k + 1) * pv, :] = basis[c * pv : (c + 1) * pv, at]
            low = lanes * pv + k * pt
            out[c, low : low + pt, :] = factor[c * pt : (c + 1) * pt, at]


def places(owners, group):
    half = owners[group] // HALF
    rank = jnp.int32(0)
    for before in range(group):
        rank = rank + (owners[before] // HALF == half).astype(jnp.int32)
    return half, rank


def pick_kernel(owners, held, out):
    mine = lax.axis_index("col") // HALF
    for group in range(GROUPS):
        half, rank = places(owners, group)
        rank = jnp.minimum(rank, out.shape[0] - 1)

        @pl.when(half == mine)
        def _():
            out[rank] = held[lax.rem(owners[group], HALF)]


def order_kernel(owners, held, *refs):
    others, outs = refs[:-COLOURS], refs[-COLOURS:]
    mine = lax.axis_index("col") // HALF
    each = GROUPS // COLOURS
    for group in range(GROUPS):
        half, rank = places(owners, group)
        piece = held[lax.rem(owners[group], HALF)]
        for mask, ref in enumerate(others, 1):
            other = ref[jnp.minimum(rank, ref.shape[0] - 1)]
            piece = jnp.where(jnp.bitwise_xor(half, mine) == mask, other, piece)
        outs[group // each][0, group % each] = piece


def merge_kernel(rows, cols, sub, *refs):
    held, total = refs[:-1], refs[-1]
    row, col = lax.axis_index("row"), lax.axis_index("col")
    share = cols // rows
    deep, tall = held[0].shape[2], held[0].shape[1]
    total[...] = jnp.zeros_like(total)
    for near, ref in enumerate(held):
        for index in range(ref.shape[0]):
            far, row_mask = index // rows, index % rows
            j = jnp.bitwise_xor(lax.rem(col, share), far * len(held) + near)
            part = jnp.dot(ref[index], sub[aligned(j, deep), :], preferred_element_type=jnp.float32)
            at = aligned(jnp.bitwise_xor(row, row_mask), tall)
            total[at, :] = total[at, :] + part


def two_terms(x):
    high = x.astype(jnp.bfloat16)
    low = (x - high.astype(jnp.float32)).astype(jnp.bfloat16)
    return jnp.concatenate([high, low], 0)


def both(products):
    half = products.shape[0] // 2
    return products[:half] + products[half:]


def chain_kernel(cols, groups, masks, first, last, offsets, start, *refs):
    held, (out, basis_all, factor_all) = refs[: len(masks)], refs[len(masks) :]
    mine = slice_index()
    lanes = basis_all.shape[2] // LANES
    pv = basis_all.shape[1] // SLICES
    pt = factor_all.shape[1] // SLICES
    for own_masks, ref in zip(masks, held):
        for index, mask in enumerate(own_masks):
            e = jnp.bitwise_xor(mine, mask)
            for k in range(lanes):
                at = slice(k * LANES, (k + 1) * LANES)
                basis_all[:, aligned(e, pv), at] = ref[index, :, k * pv : (k + 1) * pv, :]
                low = lanes * pv + k * pt
                factor_all[:, aligned(e, pt), at] = ref[index, :, low : low + pt, :]
    if first:
        n, each, width = start.shape
        pieces = start[...].reshape(n // cols, cols, each, width).sum(0)
        x = jnp.concatenate([pieces[c] for c in range(cols)], 1)
        x = jnp.concatenate([x] + [jnp.zeros_like(x)] * (8 // each - 1), 0)
    else:
        x = start[...]
    wide = x.shape[1]
    group_rows = basis_all.shape[1]
    before = jnp.int32(0)
    for slot, group in enumerate(groups):
        offset = offsets[group]
        x = pltpu.roll(x, lax.rem(before - offset + wide, wide), 1)
        before = offset
        block = x[:, :group_rows]
        weights = both(
            jnp.dot(two_terms(block), basis_all[slot], preferred_element_type=jnp.float32)
        )
        scaled = both(
            lax.dot_general(
                two_terms(weights), factor_all[slot], (((1,), (1,)), ((), ())),
                preferred_element_type=jnp.float32,
            )
        )
        change = both(
            lax.dot_general(
                two_terms(scaled), basis_all[slot], (((1,), (1,)), ((), ())),
                preferred_element_type=jnp.float32,
            )
        )
        x = jnp.concatenate([block - change, x[:, group_rows:]], 1)
    x = pltpu.roll(x, before, 1)
    if last:
        out[...] = x[: out.shape[0]].astype(out.dtype)
    else:
        out[...] = x


def local(rows, cols, sub_vectors, merge_factor, reflectors, wy_factors, owners, offsets):
    share = cols // rows
    halves = cols // HALF

    def over_col(x, mask):
        return lax.ppermute(x, "col", [(c, c ^ mask) for c in range(cols)])

    def over_row(x, mask):
        return lax.ppermute(x, "row", [(r, r ^ mask) for r in range(rows)])

    basis, factor = reflectors[0], wy_factors[0]
    group_rows, reflect = basis.shape
    dtype = basis.dtype
    tall = (group_rows + reflect) * (reflect // LANES) // SLICES

    across = [merge_factor] + [over_col(merge_factor, m * share) for m in range(1, rows)]

    packed = pl.pallas_call(
        pack_kernel,
        out_shape=jax.ShapeDtypeStruct((HALF, tall, LANES), dtype),
        in_specs=[ANY, ANY],
        out_specs=VMEM,
        scratch_shapes=[
            pltpu.VMEM((group_rows // 2, reflect), dtype),
            pltpu.VMEM((factor.shape[0] // 2, reflect), dtype),
            pltpu.SemaphoreType.DMA((2,)),
        ],
        compiler_params=limit(4),
        name="pack",
    )(basis, factor)
    members = [[h * HALF + c for c in range(HALF)] for h in range(halves)]
    slices = lax.all_to_all(packed, "col", 0, 0, axis_index_groups=members)
    slices, across = lax.optimization_barrier((slices, across))

    picked = pl.pallas_call(
        pick_kernel,
        out_shape=jax.ShapeDtypeStruct((GROUPS - 1, tall, LANES), dtype),
        in_specs=[SMEM, VMEM],
        out_specs=VMEM,
        compiler_params=limit(4),
        name="pick",
    )(owners, slices)
    others = [over_col(picked, m * HALF) for m in range(1, halves)]

    row, top = lax.axis_index("row"), lax.axis_index("col") // share

    def for_row(mask):
        index = top ^ row ^ mask
        block = across[0]
        for k in range(1, rows):
            block = jnp.where(index == k, across[k], block)
        return block

    m_held = jnp.stack([for_row(0)] + [over_row(for_row(m), m) for m in range(1, rows)])
    bit = share // 2
    while bit >= 4:
        m_held = jnp.concatenate([m_held, over_col(m_held, bit)])
        bit //= 2
    others, m_held = lax.optimization_barrier((others, m_held))
    m_two = over_col(m_held, 2)

    per = GROUPS // COLOURS
    colours = pl.pallas_call(
        order_kernel,
        out_shape=[jax.ShapeDtypeStruct((1, per, tall, LANES), dtype)] * COLOURS,
        in_specs=[SMEM, VMEM] + [VMEM] * len(others),
        out_specs=[VMEM] * COLOURS,
        compiler_params=limit(4),
        name="order",
    )(owners, slices, *others)
    colours = list(colours)
    links = [
        (HALF, lambda v: over_row(v, 1)),
        (2, lambda v: over_col(v, 2)),
        (4, lambda v: over_col(v, 4)),
    ]
    masks = [[0] for _ in range(COLOURS)]
    for step in range(2):
        for k in range(COLOURS):
            mask, send = links[(k + step) % 3]
            colours[k] = jnp.concatenate([colours[k], send(colours[k])])
            masks[k] = masks[k] + [m ^ mask for m in masks[k]]
        if step == 0:
            colours, m_two = lax.optimization_barrier((list(colours), m_two))
    m_held = [m_held, over_col(m_held, 1), m_two, over_col(m_two, 1)]

    wanted, width = merge_factor.shape[0] * rows, sub_vectors.shape[1]
    each = wanted // (rows * cols)
    merged = pl.pallas_call(
        functools.partial(merge_kernel, rows, cols),
        out_shape=jax.ShapeDtypeStruct((wanted, width), jnp.float32),
        in_specs=[VMEM] + [VMEM] * len(m_held),
        out_specs=VMEM,
        compiler_params=limit(8),
        name="merge",
    )(sub_vectors, *m_held)
    state = lax.all_to_all(merged.reshape(rows * cols, each, width), ("row", "col"), 0, 0)

    last_round = []
    for k in range(COLOURS):
        mask, send = links[(k + 2) % 3]
        last_round.append(send(colours[k]))
        masks[k] = [masks[k], [m ^ mask for m in masks[k]]]
        masks[k] += [[m ^ 1 for m in ms] for ms in masks[k]]
    last_round, state = lax.optimization_barrier((last_round, state))
    held = []
    for k in range(COLOURS):
        held.append([colours[k], last_round[k], over_col(colours[k], 1), over_col(last_round[k], 1)])

    wide = cols * width
    for k in range(COLOURS):
        first, last = k == 0, k == COLOURS - 1
        groups = range(k * per, (k + 1) * per)
        state = pl.pallas_call(
            functools.partial(chain_kernel, cols, groups, masks[k], first, last),
            out_shape=jax.ShapeDtypeStruct(
                (each, wide) if last else (8, wide), jnp.bfloat16 if last else jnp.float32
            ),
            in_specs=[SMEM, VMEM] + [VMEM] * len(held[k]),
            out_specs=VMEM,
            scratch_shapes=[
                pltpu.VMEM((per, group_rows, reflect), dtype),
                pltpu.VMEM((per, reflect, reflect), dtype),
            ],
            compiler_params=limit(12),
            name=f"chain{k}",
        )(offsets, state, *held[k])
    return state


def solution(mesh):
    rows, cols = mesh.shape["row"], mesh.shape["col"]
    in_specs = (
        P("row", "col"),
        P("row", "col"),
        P("col", None, None),
        P("col", None, None),
        P(),
        P(),
    )
    out_specs = P(("row", "col"), None)
    return jax.shard_map(
        functools.partial(local, rows, cols),
        mesh=mesh,
        in_specs=in_specs,
        out_specs=out_specs,
        check_vma=False,
    )
```

```python
import functools

import jax
import jax.numpy as jnp
from jax import lax
from jax.experimental import pallas as pl
from jax.experimental.pallas import tpu as pltpu
from jax.sharding import PartitionSpec as P

GROUPS = 6
COLOURS = 3
HALF = 8
SLICES = 2 * HALF
VMEM = pl.BlockSpec(memory_space=pltpu.VMEM)
SMEM = pl.BlockSpec(memory_space=pltpu.SMEM)
HBM = pl.BlockSpec(memory_space=pltpu.HBM)


def limit(mib):
    return pltpu.CompilerParams(vmem_limit_bytes=mib * 1024 * 1024)


def slice_index():
    row, col = lax.axis_index("row"), lax.axis_index("col")
    return lax.rem(row, 2) * HALF + lax.rem(col, HALF)


def aligned(index, size):
    return pl.ds(pl.multiple_of(index * size, size), size)


def pack_kernel(basis, factor, out, sems):
    at = aligned(lax.rem(lax.axis_index("row"), 2), HALF)
    pv = basis.shape[1]
    copies = [
        pltpu.make_async_copy(basis.at[at], out.at[:, :pv, :], sems.at[0]),
        pltpu.make_async_copy(factor.at[at], out.at[:, pv:, :], sems.at[1]),
    ]
    for copy in copies:
        copy.start()
    for copy in copies:
        copy.wait()


def places(owners, group):
    half = owners[group] // HALF
    rank = jnp.int32(0)
    for before in range(group):
        rank = rank + (owners[before] // HALF == half).astype(jnp.int32)
    return half, rank


def pick_kernel(owners, held, out):
    mine = lax.axis_index("col") // HALF
    for group in range(GROUPS):
        half, rank = places(owners, group)
        rank = jnp.minimum(rank, out.shape[0] - 1)

        @pl.when(half == mine)
        def _():
            out[rank] = held[lax.rem(owners[group], HALF)]


def order_kernel(owners, held, *refs):
    others, outs = refs[:-COLOURS], refs[-COLOURS:]
    mine = lax.axis_index("col") // HALF
    each = GROUPS // COLOURS
    for group in range(GROUPS):
        half, rank = places(owners, group)
        piece = held[lax.rem(owners[group], HALF)]
        for mask, ref in enumerate(others, 1):
            other = ref[jnp.minimum(rank, ref.shape[0] - 1)]
            piece = jnp.where(jnp.bitwise_xor(half, mine) == mask, other, piece)
        outs[group // each][0, group % each] = piece


def merge_kernel(rows, cols, sub, *refs):
    held, total = refs[:-1], refs[-1]
    row, col = lax.axis_index("row"), lax.axis_index("col")
    share = cols // rows
    deep, tall = held[0].shape[2], held[0].shape[1]
    total[...] = jnp.zeros_like(total)
    for near, ref in enumerate(held):
        for index in range(ref.shape[0]):
            far, row_mask = index // rows, index % rows
            j = jnp.bitwise_xor(lax.rem(col, share), far * len(held) + near)
            part = jnp.dot(ref[index], sub[aligned(j, deep), :], preferred_element_type=jnp.float32)
            at = aligned(jnp.bitwise_xor(row, row_mask), tall)
            total[at, :] = total[at, :] + part


def two_terms(x):
    high = x.astype(jnp.bfloat16)
    low = (x - high.astype(jnp.float32)).astype(jnp.bfloat16)
    return jnp.concatenate([high, low], 0)


def both(products):
    half = products.shape[0] // 2
    return products[:half] + products[half:]


def chain_kernel(cols, groups, masks, first, last, offsets, start, *refs):
    held, (out, basis_all, factor_all) = refs[: len(masks)], refs[len(masks) :]
    mine = slice_index()
    pv, pt = basis_all.shape[1] // SLICES, factor_all.shape[1] // SLICES
    for own_masks, ref in zip(masks, held):
        for index, mask in enumerate(own_masks):
            e = jnp.bitwise_xor(mine, mask)
            basis_all[:, aligned(e, pv), :] = ref[index, :, :pv, :]
            factor_all[:, aligned(e, pt), :] = ref[index, :, pv:, :]
    if first:
        n, each, width = start.shape
        pieces = start[...].reshape(n // cols, cols, each, width).sum(0)
        x = jnp.concatenate([pieces[c] for c in range(cols)], 1)
        x = jnp.concatenate([x] + [jnp.zeros_like(x)] * (8 // each - 1), 0)
    else:
        x = start[...]
    wide = x.shape[1]
    group_rows = basis_all.shape[1]
    before = jnp.int32(0)
    for slot, group in enumerate(groups):
        offset = offsets[group]
        x = pltpu.roll(x, lax.rem(before - offset + wide, wide), 1)
        before = offset
        block = x[:, :group_rows]
        weights = both(
            jnp.dot(two_terms(block), basis_all[slot], preferred_element_type=jnp.float32)
        )
        scaled = both(
            lax.dot_general(
                two_terms(weights), factor_all[slot], (((1,), (1,)), ((), ())),
                preferred_element_type=jnp.float32,
            )
        )
        change = both(
            lax.dot_general(
                two_terms(scaled), basis_all[slot], (((1,), (1,)), ((), ())),
                preferred_element_type=jnp.float32,
            )
        )
        x = jnp.concatenate([block - change, x[:, group_rows:]], 1)
    x = pltpu.roll(x, before, 1)
    if last:
        out[...] = x[: out.shape[0]].astype(out.dtype)
    else:
        out[...] = x


def local(rows, cols, sub_vectors, merge_factor, reflectors, wy_factors, owners, offsets):
    share = cols // rows
    halves = cols // HALF

    def over_col(x, mask):
        return lax.ppermute(x, "col", [(c, c ^ mask) for c in range(cols)])

    def over_row(x, mask):
        return lax.ppermute(x, "row", [(r, r ^ mask) for r in range(rows)])

    basis, factor = reflectors[0], wy_factors[0]
    group_rows, reflect = basis.shape
    dtype = basis.dtype
    pv, pt = group_rows // SLICES, reflect // SLICES
    piece = (pv + pt, reflect)

    across = [merge_factor] + [over_col(merge_factor, m * share) for m in range(1, rows)]

    packed = pl.pallas_call(
        pack_kernel,
        out_shape=jax.ShapeDtypeStruct((HALF,) + piece, dtype),
        in_specs=[HBM, HBM],
        out_specs=VMEM,
        scratch_shapes=[pltpu.SemaphoreType.DMA((2,))],
        compiler_params=limit(2),
        name="pack",
    )(basis.reshape(SLICES, pv, reflect), factor.reshape(SLICES, pt, reflect))
    members = [[h * HALF + c for c in range(HALF)] for h in range(halves)]
    slices = lax.all_to_all(packed, "col", 0, 0, axis_index_groups=members)

    picked = pl.pallas_call(
        pick_kernel,
        out_shape=jax.ShapeDtypeStruct((GROUPS - 1,) + piece, dtype),
        in_specs=[SMEM, VMEM],
        out_specs=VMEM,
        compiler_params=limit(4),
        name="pick",
    )(owners, slices)
    picked, across = lax.optimization_barrier((picked, across))
    others = [over_col(picked, m * HALF) for m in range(1, halves)]

    row, top = lax.axis_index("row"), lax.axis_index("col") // share

    def for_row(mask):
        index = top ^ row ^ mask
        block = across[0]
        for k in range(1, rows):
            block = jnp.where(index == k, across[k], block)
        return block

    m_held = jnp.stack([for_row(0)] + [over_row(for_row(m), m) for m in range(1, rows)])
    bit = share // 2
    while bit >= 4:
        m_held = jnp.concatenate([m_held, over_col(m_held, bit)])
        bit //= 2
    others, m_held = lax.optimization_barrier((others, m_held))
    m_two = over_col(m_held, 2)

    per = GROUPS // COLOURS
    colours = pl.pallas_call(
        order_kernel,
        out_shape=[jax.ShapeDtypeStruct((1, per) + piece, dtype)] * COLOURS,
        in_specs=[SMEM, VMEM] + [VMEM] * len(others),
        out_specs=[VMEM] * COLOURS,
        compiler_params=limit(4),
        name="order",
    )(owners, slices, *others)
    colours = list(colours)
    links = [
        (HALF, lambda v: over_row(v, 1)),
        (2, lambda v: over_col(v, 2)),
        (4, lambda v: over_col(v, 4)),
    ]
    masks = [[0] for _ in range(COLOURS)]
    for step in range(2):
        for k in range(COLOURS):
            mask, send = links[(k + step) % 3]
            colours[k] = jnp.concatenate([colours[k], send(colours[k])])
            masks[k] = masks[k] + [m ^ mask for m in masks[k]]
    m_held = [m_held, over_col(m_held, 1), m_two, over_col(m_two, 1)]

    wanted, width = merge_factor.shape[0] * rows, sub_vectors.shape[1]
    each = wanted // (rows * cols)
    merged = pl.pallas_call(
        functools.partial(merge_kernel, rows, cols),
        out_shape=jax.ShapeDtypeStruct((wanted, width), jnp.float32),
        in_specs=[VMEM] + [VMEM] * len(m_held),
        out_specs=VMEM,
        compiler_params=limit(8),
        name="merge",
    )(sub_vectors, *m_held)
    state = lax.all_to_all(merged.reshape(rows * cols, each, width), ("row", "col"), 0, 0)

    last_round = []
    for k in range(COLOURS):
        mask, send = links[(k + 2) % 3]
        last_round.append(send(colours[k]))
        masks[k] = [masks[k], [m ^ mask for m in masks[k]]]
        masks[k] += [[m ^ 1 for m in ms] for ms in masks[k]]
    last_round, state = lax.optimization_barrier((last_round, state))
    held = []
    for k in range(COLOURS):
        held.append([colours[k], last_round[k], over_col(colours[k], 1), over_col(last_round[k], 1)])

    wide = cols * width
    for k in range(COLOURS):
        first, last = k == 0, k == COLOURS - 1
        groups = range(k * per, (k + 1) * per)
        state = pl.pallas_call(
            functools.partial(chain_kernel, cols, groups, masks[k], first, last),
            out_shape=jax.ShapeDtypeStruct(
                (each, wide) if last else (8, wide), jnp.bfloat16 if last else jnp.float32
            ),
            in_specs=[SMEM, VMEM] + [VMEM] * len(held[k]),
            out_specs=VMEM,
            scratch_shapes=[
                pltpu.VMEM((per, group_rows, reflect), dtype),
                pltpu.VMEM((per, reflect, reflect), dtype),
            ],
            compiler_params=limit(12),
            name=f"chain{k}",
        )(offsets, state, *held[k])
    return state


def solution(mesh):
    rows, cols = mesh.shape["row"], mesh.shape["col"]
    in_specs = (
        P("row", "col"),
        P("row", "col"),
        P("col", None, None),
        P("col", None, None),
        P(),
        P(),
    )
    out_specs = P(("row", "col"), None)
    return jax.shard_map(
        functools.partial(local, rows, cols),
        mesh=mesh,
        in_specs=in_specs,
        out_specs=out_specs,
        check_vma=False,
    )
```

```python
import functools

import jax
import jax.numpy as jnp
from jax import lax
from jax.experimental import pallas as pl
from jax.experimental.pallas import tpu as pltpu
from jax.sharding import PartitionSpec as P

GROUPS = 6
COLOURS = 3
HALF = 8
SLICES = 2 * HALF
VMEM = pl.BlockSpec(memory_space=pltpu.VMEM)
SMEM = pl.BlockSpec(memory_space=pltpu.SMEM)
HBM = pl.BlockSpec(memory_space=pltpu.HBM)


def limit(mib):
    return pltpu.CompilerParams(vmem_limit_bytes=mib * 1024 * 1024)


def slice_index():
    row, col = lax.axis_index("row"), lax.axis_index("col")
    return lax.rem(row, 2) * HALF + lax.rem(col, HALF)


def aligned(index, size):
    return pl.ds(pl.multiple_of(index * size, size), size)


def pack_kernel(basis, factor, out, sems):
    at = aligned(lax.rem(lax.axis_index("row"), 2), HALF)
    pv = basis.shape[1]
    copies = [
        pltpu.make_async_copy(basis.at[at], out.at[:, :pv, :], sems.at[0]),
        pltpu.make_async_copy(factor.at[at], out.at[:, pv:, :], sems.at[1]),
    ]
    for copy in copies:
        copy.start()
    for copy in copies:
        copy.wait()


def places(owners, group):
    half = owners[group] // HALF
    rank = jnp.int32(0)
    for before in range(group):
        rank = rank + (owners[before] // HALF == half).astype(jnp.int32)
    return half, rank


def pick_kernel(owners, held, out):
    mine = lax.axis_index("col") // HALF
    for group in range(GROUPS):
        half, rank = places(owners, group)
        rank = jnp.minimum(rank, out.shape[0] - 1)

        @pl.when(half == mine)
        def _():
            out[rank] = held[lax.rem(owners[group], HALF)]


def order_kernel(owners, held, *refs):
    others, outs = refs[:-COLOURS], refs[-COLOURS:]
    mine = lax.axis_index("col") // HALF
    each = GROUPS // COLOURS
    for group in range(GROUPS):
        half, rank = places(owners, group)
        piece = held[lax.rem(owners[group], HALF)]
        for mask, ref in enumerate(others, 1):
            other = ref[jnp.minimum(rank, ref.shape[0] - 1)]
            piece = jnp.where(jnp.bitwise_xor(half, mine) == mask, other, piece)
        outs[group // each][0, group % each] = piece


def merge_kernel(rows, cols, sub, *refs):
    held, total = refs[:-1], refs[-1]
    row, col = lax.axis_index("row"), lax.axis_index("col")
    share = cols // rows
    deep, tall = held[0].shape[2], held[0].shape[1]
    total[...] = jnp.zeros_like(total)
    for near, ref in enumerate(held):
        for index in range(ref.shape[0]):
            far, row_mask = index // rows, index % rows
            j = jnp.bitwise_xor(lax.rem(col, share), far * len(held) + near)
            part = jnp.dot(ref[index], sub[aligned(j, deep), :], preferred_element_type=jnp.float32)
            at = aligned(jnp.bitwise_xor(row, row_mask), tall)
            total[at, :] = total[at, :] + part


def two_terms(x):
    high = x.astype(jnp.bfloat16)
    low = (x - high.astype(jnp.float32)).astype(jnp.bfloat16)
    return jnp.concatenate([high, low], 0)


def both(products):
    half = products.shape[0] // 2
    return products[:half] + products[half:]


def chain_kernel(cols, groups, masks, first, last, offsets, start, *refs):
    held, (out, basis_all, factor_all) = refs[: len(masks)], refs[len(masks) :]
    mine = slice_index()
    pv, pt = basis_all.shape[1] // SLICES, factor_all.shape[1] // SLICES
    for own_masks, ref in zip(masks, held):
        for index, mask in enumerate(own_masks):
            e = jnp.bitwise_xor(mine, mask)
            basis_all[:, aligned(e, pv), :] = ref[index, :, :pv, :]
            factor_all[:, aligned(e, pt), :] = ref[index, :, pv:, :]
    if first:
        n, each, width = start.shape
        pieces = start[...].reshape(n // cols, cols, each, width).sum(0)
        x = jnp.concatenate([pieces[c] for c in range(cols)], 1)
        x = jnp.concatenate([x] + [jnp.zeros_like(x)] * (8 // each - 1), 0)
    else:
        x = start[...]
    wide = x.shape[1]
    group_rows = basis_all.shape[1]
    before = jnp.int32(0)
    for slot, group in enumerate(groups):
        offset = offsets[group]
        x = pltpu.roll(x, lax.rem(before - offset + wide, wide), 1)
        before = offset
        block = x[:, :group_rows]
        weights = both(
            jnp.dot(two_terms(block), basis_all[slot], preferred_element_type=jnp.float32)
        )
        scaled = both(
            lax.dot_general(
                two_terms(weights), factor_all[slot], (((1,), (1,)), ((), ())),
                preferred_element_type=jnp.float32,
            )
        )
        change = both(
            lax.dot_general(
                two_terms(scaled), basis_all[slot], (((1,), (1,)), ((), ())),
                preferred_element_type=jnp.float32,
            )
        )
        x = jnp.concatenate([block - change, x[:, group_rows:]], 1)
    x = pltpu.roll(x, before, 1)
    if last:
        out[...] = x[: out.shape[0]].astype(out.dtype)
    else:
        out[...] = x


def local(rows, cols, sub_vectors, merge_factor, reflectors, wy_factors, owners, offsets):
    share = cols // rows
    halves = cols // HALF

    def over_col(x, mask):
        return lax.ppermute(x, "col", [(c, c ^ mask) for c in range(cols)])

    def over_row(x, mask):
        return lax.ppermute(x, "row", [(r, r ^ mask) for r in range(rows)])

    basis, factor = reflectors[0], wy_factors[0]
    group_rows, reflect = basis.shape
    dtype = basis.dtype
    pv, pt = group_rows // SLICES, reflect // SLICES
    piece = (pv + pt, reflect)

    across = [merge_factor] + [over_col(merge_factor, m * share) for m in range(1, rows)]

    packed = pl.pallas_call(
        pack_kernel,
        out_shape=jax.ShapeDtypeStruct((HALF,) + piece, dtype),
        in_specs=[HBM, HBM],
        out_specs=VMEM,
        scratch_shapes=[pltpu.SemaphoreType.DMA((2,))],
        compiler_params=limit(2),
        name="pack",
    )(basis.reshape(SLICES, pv, reflect), factor.reshape(SLICES, pt, reflect))
    packed, across = lax.optimization_barrier((packed, across))
    members = [[h * HALF + c for c in range(HALF)] for h in range(halves)]
    slices = lax.all_to_all(packed, "col", 0, 0, axis_index_groups=members)

    picked = pl.pallas_call(
        pick_kernel,
        out_shape=jax.ShapeDtypeStruct((GROUPS - 1,) + piece, dtype),
        in_specs=[SMEM, VMEM],
        out_specs=VMEM,
        compiler_params=limit(4),
        name="pick",
    )(owners, slices)

    row, top = lax.axis_index("row"), lax.axis_index("col") // share

    def for_row(mask):
        index = top ^ row ^ mask
        block = across[0]
        for k in range(1, rows):
            block = jnp.where(index == k, across[k], block)
        return block

    m_held = jnp.stack([for_row(0)] + [over_row(for_row(m), m) for m in range(1, rows)])
    bit = share // 2
    while bit >= 4:
        m_held = jnp.concatenate([m_held, over_col(m_held, bit)])
        bit //= 2
    picked, m_held = lax.optimization_barrier((picked, m_held))
    others = [over_col(picked, m * HALF) for m in range(1, halves)]
    m_two = over_col(m_held, 2)

    per = GROUPS // COLOURS
    colours = pl.pallas_call(
        order_kernel,
        out_shape=[jax.ShapeDtypeStruct((1, per) + piece, dtype)] * COLOURS,
        in_specs=[SMEM, VMEM] + [VMEM] * len(others),
        out_specs=[VMEM] * COLOURS,
        compiler_params=limit(4),
        name="order",
    )(owners, slices, *others)
    colours = list(colours)
    links = [
        (HALF, lambda v: over_row(v, 1)),
        (2, lambda v: over_col(v, 2)),
        (4, lambda v: over_col(v, 4)),
    ]
    masks = [[0] for _ in range(COLOURS)]
    for step in range(2):
        for k in range(COLOURS):
            mask, send = links[(k + step) % 3]
            colours[k] = jnp.concatenate([colours[k], send(colours[k])])
            masks[k] = masks[k] + [m ^ mask for m in masks[k]]
    m_held = [m_held, over_col(m_held, 1), m_two, over_col(m_two, 1)]

    wanted, width = merge_factor.shape[0] * rows, sub_vectors.shape[1]
    each = wanted // (rows * cols)
    merged = pl.pallas_call(
        functools.partial(merge_kernel, rows, cols),
        out_shape=jax.ShapeDtypeStruct((wanted, width), jnp.float32),
        in_specs=[VMEM] + [VMEM] * len(m_held),
        out_specs=VMEM,
        compiler_params=limit(8),
        name="merge",
    )(sub_vectors, *m_held)
    state = lax.all_to_all(merged.reshape(rows * cols, each, width), ("row", "col"), 0, 0)

    last_round = []
    for k in range(COLOURS):
        mask, send = links[(k + 2) % 3]
        last_round.append(send(colours[k]))
        masks[k] = [masks[k], [m ^ mask for m in masks[k]]]
        masks[k] += [[m ^ 1 for m in ms] for ms in masks[k]]
    last_round, state = lax.optimization_barrier((last_round, state))
    held = []
    for k in range(COLOURS):
        held.append([colours[k], last_round[k], over_col(colours[k], 1), over_col(last_round[k], 1)])

    wide = cols * width
    for k in range(COLOURS):
        first, last = k == 0, k == COLOURS - 1
        groups = range(k * per, (k + 1) * per)
        state = pl.pallas_call(
            functools.partial(chain_kernel, cols, groups, masks[k], first, last),
            out_shape=jax.ShapeDtypeStruct(
                (each, wide) if last else (8, wide), jnp.bfloat16 if last else jnp.float32
            ),
            in_specs=[SMEM, VMEM] + [VMEM] * len(held[k]),
            out_specs=VMEM,
            scratch_shapes=[
                pltpu.VMEM((per, group_rows, reflect), dtype),
                pltpu.VMEM((per, reflect, reflect), dtype),
            ],
            compiler_params=limit(12),
            name=f"chain{k}",
        )(offsets, state, *held[k])
    return state


def solution(mesh):
    rows, cols = mesh.shape["row"], mesh.shape["col"]
    in_specs = (
        P("row", "col"),
        P("row", "col"),
        P("col", None, None),
        P("col", None, None),
        P(),
        P(),
    )
    out_specs = P(("row", "col"), None)
    return jax.shard_map(
        functools.partial(local, rows, cols),
        mesh=mesh,
        in_specs=in_specs,
        out_specs=out_specs,
        check_vma=False,
    )
```

```python
import functools

import jax
import jax.numpy as jnp
from jax import lax
from jax.experimental import pallas as pl
from jax.experimental.pallas import tpu as pltpu
from jax.sharding import PartitionSpec as P

GROUPS = 6
COLOURS = 3
HALF = 8
SLICES = 2 * HALF
VMEM = pl.BlockSpec(memory_space=pltpu.VMEM)
SMEM = pl.BlockSpec(memory_space=pltpu.SMEM)
HBM = pl.BlockSpec(memory_space=pltpu.HBM)


def limit(mib):
    return pltpu.CompilerParams(vmem_limit_bytes=mib * 1024 * 1024)


def slice_index():
    row, col = lax.axis_index("row"), lax.axis_index("col")
    return lax.rem(row, 2) * HALF + lax.rem(col, HALF)


def aligned(index, size):
    return pl.ds(pl.multiple_of(index * size, size), size)


def pack_kernel(basis, factor, out, sems):
    at = aligned(lax.rem(lax.axis_index("row"), 2), HALF)
    pv = basis.shape[1]
    copies = [
        pltpu.make_async_copy(basis.at[at], out.at[:, :pv, :], sems.at[0]),
        pltpu.make_async_copy(factor.at[at], out.at[:, pv:, :], sems.at[1]),
    ]
    for copy in copies:
        copy.start()
    for copy in copies:
        copy.wait()


def places(owners, group):
    half = owners[group] // HALF
    rank = jnp.int32(0)
    for before in range(group):
        rank = rank + (owners[before] // HALF == half).astype(jnp.int32)
    return half, rank


def pick_kernel(owners, held, out):
    mine = lax.axis_index("col") // HALF
    for group in range(GROUPS):
        half, rank = places(owners, group)
        rank = jnp.minimum(rank, out.shape[0] - 1)

        @pl.when(half == mine)
        def _():
            out[rank] = held[lax.rem(owners[group], HALF)]


def order_kernel(owners, held, *refs):
    others, outs = refs[:-COLOURS], refs[-COLOURS:]
    mine = lax.axis_index("col") // HALF
    each = GROUPS // COLOURS
    for group in range(GROUPS):
        half, rank = places(owners, group)
        piece = held[lax.rem(owners[group], HALF)]
        for mask, ref in enumerate(others, 1):
            other = ref[jnp.minimum(rank, ref.shape[0] - 1)]
            piece = jnp.where(jnp.bitwise_xor(half, mine) == mask, other, piece)
        outs[group // each][0, group % each] = piece


def merge_kernel(rows, cols, tags, sub, *refs):
    held, total = refs[:-1], refs[-1]
    row, col = lax.axis_index("row"), lax.axis_index("col")
    deep, tall = held[0].shape[2], held[0].shape[1]
    total[...] = jnp.zeros_like(total)
    for own_tags, ref in zip(tags, held):
        for index, (row_mask, col_mask) in enumerate(own_tags):
            j = jnp.bitwise_xor(lax.rem(col, cols // rows), col_mask)
            part = jnp.dot(ref[index], sub[aligned(j, deep), :], preferred_element_type=jnp.float32)
            at = aligned(jnp.bitwise_xor(row, row_mask), tall)
            total[at, :] = total[at, :] + part


def two_terms(x):
    high = x.astype(jnp.bfloat16)
    low = (x - high.astype(jnp.float32)).astype(jnp.bfloat16)
    return jnp.concatenate([high, low], 0)


def both(products):
    half = products.shape[0] // 2
    return products[:half] + products[half:]


def chain_kernel(cols, groups, masks, first, last, offsets, start, *refs):
    held, (out, basis_all, factor_all) = refs[: len(masks)], refs[len(masks) :]
    mine = slice_index()
    pv, pt = basis_all.shape[1] // SLICES, factor_all.shape[1] // SLICES
    for own_masks, ref in zip(masks, held):
        for index, mask in enumerate(own_masks):
            e = jnp.bitwise_xor(mine, mask)
            basis_all[:, aligned(e, pv), :] = ref[index, :, :pv, :]
            factor_all[:, aligned(e, pt), :] = ref[index, :, pv:, :]
    if first:
        n, each, width = start.shape
        pieces = start[...].reshape(n // cols, cols, each, width).sum(0)
        x = jnp.concatenate([pieces[c] for c in range(cols)], 1)
        x = jnp.concatenate([x] + [jnp.zeros_like(x)] * (8 // each - 1), 0)
    else:
        x = start[...]
    wide = x.shape[1]
    group_rows = basis_all.shape[1]
    before = jnp.int32(0)
    for slot, group in enumerate(groups):
        offset = offsets[group]
        x = pltpu.roll(x, lax.rem(before - offset + wide, wide), 1)
        before = offset
        block = x[:, :group_rows]
        weights = both(
            jnp.dot(two_terms(block), basis_all[slot], preferred_element_type=jnp.float32)
        )
        scaled = both(
            lax.dot_general(
                two_terms(weights), factor_all[slot], (((1,), (1,)), ((), ())),
                preferred_element_type=jnp.float32,
            )
        )
        change = both(
            lax.dot_general(
                two_terms(scaled), basis_all[slot], (((1,), (1,)), ((), ())),
                preferred_element_type=jnp.float32,
            )
        )
        x = jnp.concatenate([block - change, x[:, group_rows:]], 1)
    x = pltpu.roll(x, before, 1)
    if last:
        out[...] = x[: out.shape[0]].astype(out.dtype)
    else:
        out[...] = x


def local(rows, cols, sub_vectors, merge_factor, reflectors, wy_factors, owners, offsets):
    share = cols // rows
    halves = cols // HALF

    def over_col(x, mask):
        return lax.ppermute(x, "col", [(c, c ^ mask) for c in range(cols)])

    def over_row(x, mask):
        return lax.ppermute(x, "row", [(r, r ^ mask) for r in range(rows)])

    basis, factor = reflectors[0], wy_factors[0]
    group_rows, reflect = basis.shape
    dtype = basis.dtype
    pv, pt = group_rows // SLICES, reflect // SLICES
    piece = (pv + pt, reflect)

    across = [merge_factor] + [over_col(merge_factor, m * share) for m in range(1, rows)]

    packed = pl.pallas_call(
        pack_kernel,
        out_shape=jax.ShapeDtypeStruct((HALF,) + piece, dtype),
        in_specs=[HBM, HBM],
        out_specs=VMEM,
        scratch_shapes=[pltpu.SemaphoreType.DMA((2,))],
        compiler_params=limit(2),
        name="pack",
    )(basis.reshape(SLICES, pv, reflect), factor.reshape(SLICES, pt, reflect))
    packed, across = lax.optimization_barrier((packed, across))
    members = [[h * HALF + c for c in range(HALF)] for h in range(halves)]
    slices = lax.all_to_all(packed, "col", 0, 0, axis_index_groups=members)

    picked = pl.pallas_call(
        pick_kernel,
        out_shape=jax.ShapeDtypeStruct((GROUPS - 1,) + piece, dtype),
        in_specs=[SMEM, VMEM],
        out_specs=VMEM,
        compiler_params=limit(4),
        name="pick",
    )(owners, slices)

    row, top = lax.axis_index("row"), lax.axis_index("col") // share

    def for_row(mask):
        index = top ^ row ^ mask
        block = across[0]
        for k in range(1, rows):
            block = jnp.where(index == k, across[k], block)
        return block

    blocks = [for_row(0)] + [over_row(for_row(m), m) for m in range(1, rows)]
    groups = [range(rows // 2), range(rows // 2, rows)]
    sides = [jnp.stack([blocks[m] for m in group]) for group in groups]
    tags = [[(m, 0) for m in group] for group in groups]

    def double(side, bit):
        sides[side] = jnp.concatenate([sides[side], over_col(sides[side], bit)])
        tags[side] = tags[side] + [(m, c ^ bit) for m, c in tags[side]]

    bit = share // 2
    while bit > 4:
        double(0, bit)
        double(1, bit)
        bit //= 2
    double(0, 2)
    double(1, 4)
    picked, sides = lax.optimization_barrier((picked, sides))
    others = [over_col(picked, m * HALF) for m in range(1, halves)]
    late = jnp.concatenate([over_col(sides[0], 4), over_col(sides[1], 2)])
    late_tags = [(m, c ^ 4) for m, c in tags[0]] + [(m, c ^ 2) for m, c in tags[1]]
    m_held = [jnp.concatenate(sides), late]
    tags = [tags[0] + tags[1], late_tags]
    m_held += [over_col(x, 1) for x in m_held]
    tags += [[(m, c ^ 1) for m, c in ts] for ts in tags]
    wanted, width = merge_factor.shape[0] * rows, sub_vectors.shape[1]
    each = wanted // (rows * cols)
    merged = pl.pallas_call(
        functools.partial(merge_kernel, rows, cols, tags),
        out_shape=jax.ShapeDtypeStruct((wanted, width), jnp.float32),
        in_specs=[VMEM] + [VMEM] * len(m_held),
        out_specs=VMEM,
        compiler_params=limit(8),
        name="merge",
    )(sub_vectors, *m_held)
    others, merged = lax.optimization_barrier((others, merged))
    state = lax.all_to_all(merged.reshape(rows * cols, each, width), ("row", "col"), 0, 0)

    per = GROUPS // COLOURS
    colours = pl.pallas_call(
        order_kernel,
        out_shape=[jax.ShapeDtypeStruct((1, per) + piece, dtype)] * COLOURS,
        in_specs=[SMEM, VMEM] + [VMEM] * len(others),
        out_specs=[VMEM] * COLOURS,
        compiler_params=limit(4),
        name="order",
    )(owners, slices, *others)
    colours = list(colours)
    links = [
        (HALF, lambda v: over_row(v, 1)),
        (2, lambda v: over_col(v, 2)),
        (4, lambda v: over_col(v, 4)),
    ]
    masks = [[0] for _ in range(COLOURS)]
    for step in range(2):
        for k in range(COLOURS):
            mask, send = links[(k + step) % 3]
            colours[k] = jnp.concatenate([colours[k], send(colours[k])])
            masks[k] = masks[k] + [m ^ mask for m in masks[k]]
        if step == 0:
            colours, state = lax.optimization_barrier((colours, state))
    last_round = []
    for k in range(COLOURS):
        mask, send = links[(k + 2) % 3]
        last_round.append(send(colours[k]))
        masks[k] = [masks[k], [m ^ mask for m in masks[k]]]
        masks[k] += [[m ^ 1 for m in ms] for ms in masks[k]]
    held = []
    for k in range(COLOURS):
        held.append([colours[k], last_round[k], over_col(colours[k], 1), over_col(last_round[k], 1)])

    wide = cols * width
    for k in range(COLOURS):
        first, last = k == 0, k == COLOURS - 1
        groups = range(k * per, (k + 1) * per)
        state = pl.pallas_call(
            functools.partial(chain_kernel, cols, groups, masks[k], first, last),
            out_shape=jax.ShapeDtypeStruct(
                (each, wide) if last else (8, wide), jnp.bfloat16 if last else jnp.float32
            ),
            in_specs=[SMEM, VMEM] + [VMEM] * len(held[k]),
            out_specs=VMEM,
            scratch_shapes=[
                pltpu.VMEM((per, group_rows, reflect), dtype),
                pltpu.VMEM((per, reflect, reflect), dtype),
            ],
            compiler_params=limit(12),
            name=f"chain{k}",
        )(offsets, state, *held[k])
    return state


def solution(mesh):
    rows, cols = mesh.shape["row"], mesh.shape["col"]
    in_specs = (
        P("row", "col"),
        P("row", "col"),
        P("col", None, None),
        P("col", None, None),
        P(),
        P(),
    )
    out_specs = P(("row", "col"), None)
    return jax.shard_map(
        functools.partial(local, rows, cols),
        mesh=mesh,
        in_specs=in_specs,
        out_specs=out_specs,
        check_vma=False,
    )
```

```python
import functools

import jax
import jax.numpy as jnp
from jax import lax
from jax.experimental import pallas as pl
from jax.experimental.pallas import tpu as pltpu
from jax.sharding import PartitionSpec as P

GROUPS = 6
COLOURS = 3
HALF = 8
SLICES = 2 * HALF
VMEM = pl.BlockSpec(memory_space=pltpu.VMEM)
SMEM = pl.BlockSpec(memory_space=pltpu.SMEM)
HBM = pl.BlockSpec(memory_space=pltpu.HBM)


def limit(mib):
    return pltpu.CompilerParams(vmem_limit_bytes=mib * 1024 * 1024)


def slice_index():
    row, col = lax.axis_index("row"), lax.axis_index("col")
    return lax.rem(row, 2) * HALF + lax.rem(col, HALF)


def aligned(index, size):
    return pl.ds(pl.multiple_of(index * size, size), size)


def pack_kernel(basis, factor, out, sems):
    at = aligned(lax.rem(lax.axis_index("row"), 2), HALF)
    pv = basis.shape[1]
    copies = [
        pltpu.make_async_copy(basis.at[at], out.at[:, :pv, :], sems.at[0]),
        pltpu.make_async_copy(factor.at[at], out.at[:, pv:, :], sems.at[1]),
    ]
    for copy in copies:
        copy.start()
    for copy in copies:
        copy.wait()


def places(owners, group):
    half = owners[group] // HALF
    rank = jnp.int32(0)
    for before in range(group):
        rank = rank + (owners[before] // HALF == half).astype(jnp.int32)
    return half, rank


def pick_kernel(owners, held, out):
    mine = lax.axis_index("col") // HALF
    for group in range(GROUPS):
        half, rank = places(owners, group)
        rank = jnp.minimum(rank, out.shape[0] - 1)

        @pl.when(half == mine)
        def _():
            out[rank] = held[lax.rem(owners[group], HALF)]


def order_kernel(owners, held, *refs):
    others, outs = refs[:-COLOURS], refs[-COLOURS:]
    mine = lax.axis_index("col") // HALF
    each = GROUPS // COLOURS
    for group in range(GROUPS):
        half, rank = places(owners, group)
        piece = held[lax.rem(owners[group], HALF)]
        for mask in range(1, len(others) // 2 + 1):
            head, tail = others[2 * mask - 2 : 2 * mask]
            other = tail[jnp.clip(rank - 1, 0, tail.shape[0] - 1)]
            other = jnp.where(rank == 0, head[0], other)
            piece = jnp.where(jnp.bitwise_xor(half, mine) == mask, other, piece)
        outs[group // each][0, group % each] = piece


def merge_kernel(rows, cols, tags, sub, *refs):
    held, total = refs[:-1], refs[-1]
    row, col = lax.axis_index("row"), lax.axis_index("col")
    deep, tall = held[0].shape[2], held[0].shape[1]
    total[...] = jnp.zeros_like(total)
    for own_tags, ref in zip(tags, held):
        for index, (row_mask, col_mask) in enumerate(own_tags):
            j = jnp.bitwise_xor(lax.rem(col, cols // rows), col_mask)
            part = jnp.dot(ref[index], sub[aligned(j, deep), :], preferred_element_type=jnp.float32)
            at = aligned(jnp.bitwise_xor(row, row_mask), tall)
            total[at, :] = total[at, :] + part


def two_terms(x):
    high = x.astype(jnp.bfloat16)
    low = (x - high.astype(jnp.float32)).astype(jnp.bfloat16)
    return jnp.concatenate([high, low], 0)


def both(products):
    half = products.shape[0] // 2
    return products[:half] + products[half:]


def chain_kernel(cols, groups, masks, first, last, offsets, start, *refs):
    held, (out, basis_all, factor_all) = refs[: len(masks)], refs[len(masks) :]
    mine = slice_index()
    pv, pt = basis_all.shape[1] // SLICES, factor_all.shape[1] // SLICES
    for own_masks, ref in zip(masks, held):
        for index, mask in enumerate(own_masks):
            e = jnp.bitwise_xor(mine, mask)
            basis_all[:, aligned(e, pv), :] = ref[index, :, :pv, :]
            factor_all[:, aligned(e, pt), :] = ref[index, :, pv:, :]
    if first:
        n, each, width = start.shape
        pieces = start[...].reshape(n // cols, cols, each, width).sum(0)
        x = jnp.concatenate([pieces[c] for c in range(cols)], 1)
        x = jnp.concatenate([x] + [jnp.zeros_like(x)] * (8 // each - 1), 0)
    else:
        x = start[...]
    wide = x.shape[1]
    group_rows = basis_all.shape[1]
    before = jnp.int32(0)
    for slot, group in enumerate(groups):
        offset = offsets[group]
        x = pltpu.roll(x, lax.rem(before - offset + wide, wide), 1)
        before = offset
        block = x[:, :group_rows]
        weights = both(
            jnp.dot(two_terms(block), basis_all[slot], preferred_element_type=jnp.float32)
        )
        scaled = both(
            lax.dot_general(
                two_terms(weights), factor_all[slot], (((1,), (1,)), ((), ())),
                preferred_element_type=jnp.float32,
            )
        )
        change = both(
            lax.dot_general(
                two_terms(scaled), basis_all[slot], (((1,), (1,)), ((), ())),
                preferred_element_type=jnp.float32,
            )
        )
        x = jnp.concatenate([block - change, x[:, group_rows:]], 1)
    x = pltpu.roll(x, before, 1)
    if last:
        out[...] = x[: out.shape[0]].astype(out.dtype)
    else:
        out[...] = x


def local(rows, cols, sub_vectors, merge_factor, reflectors, wy_factors, owners, offsets):
    share = cols // rows
    halves = cols // HALF

    def over_col(x, mask):
        return lax.ppermute(x, "col", [(c, c ^ mask) for c in range(cols)])

    def over_row(x, mask):
        return lax.ppermute(x, "row", [(r, r ^ mask) for r in range(rows)])

    basis, factor = reflectors[0], wy_factors[0]
    group_rows, reflect = basis.shape
    dtype = basis.dtype
    pv, pt = group_rows // SLICES, reflect // SLICES
    piece = (pv + pt, reflect)

    across = [merge_factor] + [over_col(merge_factor, m * share) for m in range(1, rows)]

    packed = pl.pallas_call(
        pack_kernel,
        out_shape=jax.ShapeDtypeStruct((HALF,) + piece, dtype),
        in_specs=[HBM, HBM],
        out_specs=VMEM,
        scratch_shapes=[pltpu.SemaphoreType.DMA((2,))],
        compiler_params=limit(2),
        name="pack",
    )(basis.reshape(SLICES, pv, reflect), factor.reshape(SLICES, pt, reflect))
    packed, across = lax.optimization_barrier((packed, across))
    members = [[h * HALF + c for c in range(HALF)] for h in range(halves)]
    slices = lax.all_to_all(packed, "col", 0, 0, axis_index_groups=members)

    picked = pl.pallas_call(
        pick_kernel,
        out_shape=jax.ShapeDtypeStruct((GROUPS - 1,) + piece, dtype),
        in_specs=[SMEM, VMEM],
        out_specs=VMEM,
        compiler_params=limit(4),
        name="pick",
    )(owners, slices)

    row, top = lax.axis_index("row"), lax.axis_index("col") // share

    def for_row(mask):
        index = top ^ row ^ mask
        block = across[0]
        for k in range(1, rows):
            block = jnp.where(index == k, across[k], block)
        return block

    blocks = [for_row(0)] + [over_row(for_row(m), m) for m in range(1, rows)]
    groups = [range(rows // 2), range(rows // 2, rows)]
    sides = [jnp.stack([blocks[m] for m in group]) for group in groups]
    tags = [[(m, 0) for m in group] for group in groups]

    def double(side, bit):
        sides[side] = jnp.concatenate([sides[side], over_col(sides[side], bit)])
        tags[side] = tags[side] + [(m, c ^ bit) for m, c in tags[side]]

    bit = share // 2
    while bit > 4:
        double(0, bit)
        double(1, bit)
        bit //= 2
    double(0, 2)
    double(1, 4)
    picked, sides = lax.optimization_barrier((picked, sides))
    heads = [over_col(picked[:1], m * HALF) for m in range(1, halves)]
    tails = [over_col(picked[1:], m * HALF) for m in range(1, halves)]
    heads, sides = lax.optimization_barrier((heads, sides))
    others = [x for pair in zip(heads, tails) for x in pair]
    late = jnp.concatenate([over_col(sides[0], 4), over_col(sides[1], 2)])
    late_tags = [(m, c ^ 4) for m, c in tags[0]] + [(m, c ^ 2) for m, c in tags[1]]
    m_held = [jnp.concatenate(sides), late]
    tags = [tags[0] + tags[1], late_tags]
    m_held += [over_col(x, 1) for x in m_held]
    tags += [[(m, c ^ 1) for m, c in ts] for ts in tags]
    wanted, width = merge_factor.shape[0] * rows, sub_vectors.shape[1]
    each = wanted // (rows * cols)
    merged = pl.pallas_call(
        functools.partial(merge_kernel, rows, cols, tags),
        out_shape=jax.ShapeDtypeStruct((wanted, width), jnp.float32),
        in_specs=[VMEM] + [VMEM] * len(m_held),
        out_specs=VMEM,
        compiler_params=limit(8),
        name="merge",
    )(sub_vectors, *m_held)
    others, merged = lax.optimization_barrier((others, merged))
    state = lax.all_to_all(merged.reshape(rows * cols, each, width), ("row", "col"), 0, 0)

    per = GROUPS // COLOURS
    colours = pl.pallas_call(
        order_kernel,
        out_shape=[jax.ShapeDtypeStruct((1, per) + piece, dtype)] * COLOURS,
        in_specs=[SMEM, VMEM] + [VMEM] * len(others),
        out_specs=[VMEM] * COLOURS,
        compiler_params=limit(4),
        name="order",
    )(owners, slices, *others)
    colours = list(colours)
    links = [
        (HALF, lambda v: over_row(v, 1)),
        (2, lambda v: over_col(v, 2)),
        (4, lambda v: over_col(v, 4)),
    ]
    masks = [[0] for _ in range(COLOURS)]
    for step in range(2):
        for k in range(COLOURS):
            mask, send = links[(k + step) % 3]
            colours[k] = jnp.concatenate([colours[k], send(colours[k])])
            masks[k] = masks[k] + [m ^ mask for m in masks[k]]
    colours, state = lax.optimization_barrier((colours, state))
    last_round = []
    for k in range(COLOURS):
        mask, send = links[(k + 2) % 3]
        last_round.append(send(colours[k]))
        masks[k] = [masks[k], [m ^ mask for m in masks[k]]]
        masks[k] += [[m ^ 1 for m in ms] for ms in masks[k]]
    held = []
    for k in range(COLOURS):
        held.append([colours[k], last_round[k], over_col(colours[k], 1), over_col(last_round[k], 1)])

    wide = cols * width
    for k in range(COLOURS):
        first, last = k == 0, k == COLOURS - 1
        groups = range(k * per, (k + 1) * per)
        state = pl.pallas_call(
            functools.partial(chain_kernel, cols, groups, masks[k], first, last),
            out_shape=jax.ShapeDtypeStruct(
                (each, wide) if last else (8, wide), jnp.bfloat16 if last else jnp.float32
            ),
            in_specs=[SMEM, VMEM] + [VMEM] * len(held[k]),
            out_specs=VMEM,
            scratch_shapes=[
                pltpu.VMEM((per, group_rows, reflect), dtype),
                pltpu.VMEM((per, reflect, reflect), dtype),
            ],
            compiler_params=limit(12),
            name=f"chain{k}",
        )(offsets, state, *held[k])
    return state


def solution(mesh):
    rows, cols = mesh.shape["row"], mesh.shape["col"]
    in_specs = (
        P("row", "col"),
        P("row", "col"),
        P("col", None, None),
        P("col", None, None),
        P(),
        P(),
    )
    out_specs = P(("row", "col"), None)
    return jax.shard_map(
        functools.partial(local, rows, cols),
        mesh=mesh,
        in_specs=in_specs,
        out_specs=out_specs,
        check_vma=False,
    )
```

```python
import functools

import jax
import jax.numpy as jnp
from jax import lax
from jax.experimental import pallas as pl
from jax.experimental.pallas import tpu as pltpu
from jax.sharding import PartitionSpec as P

GROUPS = 6
COLOURS = 3
HALF = 8
SLICES = 2 * HALF
VMEM = pl.BlockSpec(memory_space=pltpu.VMEM)
SMEM = pl.BlockSpec(memory_space=pltpu.SMEM)
HBM = pl.BlockSpec(memory_space=pltpu.HBM)


def limit(mib):
    return pltpu.CompilerParams(vmem_limit_bytes=mib * 1024 * 1024)


def cost(arrays, flops=0):
    size = sum(a.size * a.dtype.itemsize for a in arrays)
    return pl.CostEstimate(flops=flops, bytes_accessed=size, transcendentals=0)


def slice_index():
    row, col = lax.axis_index("row"), lax.axis_index("col")
    return lax.rem(row, 2) * HALF + lax.rem(col, HALF)


def aligned(index, size):
    return pl.ds(pl.multiple_of(index * size, size), size)


def pack_kernel(basis, factor, out, sems):
    at = aligned(lax.rem(lax.axis_index("row"), 2), HALF)
    pv = basis.shape[1]
    copies = [
        pltpu.make_async_copy(basis.at[at], out.at[:, :pv, :], sems.at[0]),
        pltpu.make_async_copy(factor.at[at], out.at[:, pv:, :], sems.at[1]),
    ]
    for copy in copies:
        copy.start()
    for copy in copies:
        copy.wait()


def places(owners, group):
    half = owners[group] // HALF
    rank = jnp.int32(0)
    for before in range(group):
        rank = rank + (owners[before] // HALF == half).astype(jnp.int32)
    return half, rank


def pick_kernel(owners, held, out):
    mine = lax.axis_index("col") // HALF
    for group in range(GROUPS):
        half, rank = places(owners, group)
        rank = jnp.minimum(rank, out.shape[0] - 1)

        @pl.when(half == mine)
        def _():
            out[rank] = held[lax.rem(owners[group], HALF)]


def order_kernel(owners, held, *refs):
    others, outs = refs[:-COLOURS], refs[-COLOURS:]
    mine = lax.axis_index("col") // HALF
    each = GROUPS // COLOURS
    for group in range(GROUPS):
        half, rank = places(owners, group)
        piece = held[lax.rem(owners[group], HALF)]
        for mask, ref in enumerate(others, 1):
            other = ref[jnp.minimum(rank, ref.shape[0] - 1)]
            piece = jnp.where(jnp.bitwise_xor(half, mine) == mask, other, piece)
        outs[group // each][0, group % each] = piece


def merge_kernel(rows, cols, tags, sub, *refs):
    held, total = refs[:-1], refs[-1]
    row, col = lax.axis_index("row"), lax.axis_index("col")
    deep, tall = held[0].shape[2], held[0].shape[1]
    total[...] = jnp.zeros_like(total)
    for own_tags, ref in zip(tags, held):
        for index, (row_mask, col_mask) in enumerate(own_tags):
            j = jnp.bitwise_xor(lax.rem(col, cols // rows), col_mask)
            part = jnp.dot(ref[index], sub[aligned(j, deep), :], preferred_element_type=jnp.float32)
            at = aligned(jnp.bitwise_xor(row, row_mask), tall)
            total[at, :] = total[at, :] + part


def two_terms(x):
    high = x.astype(jnp.bfloat16)
    low = (x - high.astype(jnp.float32)).astype(jnp.bfloat16)
    return jnp.concatenate([high, low], 0)


def both(products):
    half = products.shape[0] // 2
    return products[:half] + products[half:]


def chain_kernel(cols, groups, masks, first, last, offsets, start, *refs):
    held, (out, basis_all, factor_all) = refs[: len(masks)], refs[len(masks) :]
    mine = slice_index()
    pv, pt = basis_all.shape[1] // SLICES, factor_all.shape[1] // SLICES
    for own_masks, ref in zip(masks, held):
        for index, mask in enumerate(own_masks):
            e = jnp.bitwise_xor(mine, mask)
            basis_all[:, aligned(e, pv), :] = ref[index, :, :pv, :]
            factor_all[:, aligned(e, pt), :] = ref[index, :, pv:, :]
    if first:
        n, each, width = start.shape
        pieces = start[...].reshape(n // cols, cols, each, width).sum(0)
        x = jnp.concatenate([pieces[c] for c in range(cols)], 1)
        x = jnp.concatenate([x] + [jnp.zeros_like(x)] * (8 // each - 1), 0)
    else:
        x = start[...]
    wide = x.shape[1]
    group_rows = basis_all.shape[1]
    before = jnp.int32(0)
    for slot, group in enumerate(groups):
        offset = offsets[group]
        x = pltpu.roll(x, lax.rem(before - offset + wide, wide), 1)
        before = offset
        block = x[:, :group_rows]
        weights = both(
            jnp.dot(two_terms(block), basis_all[slot], preferred_element_type=jnp.float32)
        )
        scaled = both(
            lax.dot_general(
                two_terms(weights), factor_all[slot], (((1,), (1,)), ((), ())),
                preferred_element_type=jnp.float32,
            )
        )
        change = both(
            lax.dot_general(
                two_terms(scaled), basis_all[slot], (((1,), (1,)), ((), ())),
                preferred_element_type=jnp.float32,
            )
        )
        x = jnp.concatenate([block - change, x[:, group_rows:]], 1)
    x = pltpu.roll(x, before, 1)
    if last:
        out[...] = x[: out.shape[0]].astype(out.dtype)
    else:
        out[...] = x


def local(rows, cols, sub_vectors, merge_factor, reflectors, wy_factors, owners, offsets):
    share = cols // rows
    halves = cols // HALF

    def over_col(x, mask):
        return lax.ppermute(x, "col", [(c, c ^ mask) for c in range(cols)])

    def over_row(x, mask):
        return lax.ppermute(x, "row", [(r, r ^ mask) for r in range(rows)])

    basis, factor = reflectors[0], wy_factors[0]
    group_rows, reflect = basis.shape
    dtype = basis.dtype
    pv, pt = group_rows // SLICES, reflect // SLICES
    piece = (pv + pt, reflect)

    across = [merge_factor] + [over_col(merge_factor, m * share) for m in range(1, rows)]

    packed = pl.pallas_call(
        pack_kernel,
        out_shape=jax.ShapeDtypeStruct((HALF,) + piece, dtype),
        in_specs=[HBM, HBM],
        out_specs=VMEM,
        scratch_shapes=[pltpu.SemaphoreType.DMA((2,))],
        compiler_params=limit(2),
        cost_estimate=cost([basis, factor]),
        name="pack",
    )(basis.reshape(SLICES, pv, reflect), factor.reshape(SLICES, pt, reflect))
    members = [[h * HALF + c for c in range(HALF)] for h in range(halves)]
    slices = lax.all_to_all(packed, "col", 0, 0, axis_index_groups=members)

    row, top = lax.axis_index("row"), lax.axis_index("col") // share

    def for_row(mask):
        index = top ^ row ^ mask
        block = across[0]
        for k in range(1, rows):
            block = jnp.where(index == k, across[k], block)
        return block

    blocks = [for_row(0)] + [over_row(for_row(m), m) for m in range(1, rows)]
    groups = [range(rows // 2), range(rows // 2, rows)]
    sides = [jnp.stack([blocks[m] for m in group]) for group in groups]
    tags = [[(m, 0) for m in group] for group in groups]

    def double(side, bit):
        sides[side] = jnp.concatenate([sides[side], over_col(sides[side], bit)])
        tags[side] = tags[side] + [(m, c ^ bit) for m, c in tags[side]]

    bit = share // 2
    while bit > 4:
        double(0, bit)
        double(1, bit)
        bit //= 2
    double(0, 2)
    double(1, 4)
    slices, sides = lax.optimization_barrier((slices, sides))

    picked = pl.pallas_call(
        pick_kernel,
        out_shape=jax.ShapeDtypeStruct((GROUPS - 1,) + piece, dtype),
        in_specs=[SMEM, VMEM],
        out_specs=VMEM,
        compiler_params=limit(4),
        cost_estimate=cost([slices]),
        name="pick",
    )(owners, slices)
    others = [over_col(picked, m * HALF) for m in range(1, halves)]
    late = jnp.concatenate([over_col(sides[0], 4), over_col(sides[1], 2)])
    late_tags = [(m, c ^ 4) for m, c in tags[0]] + [(m, c ^ 2) for m, c in tags[1]]
    m_held = [jnp.concatenate(sides), late]
    tags = [tags[0] + tags[1], late_tags]
    m_held += [over_col(x, 1) for x in m_held]
    tags += [[(m, c ^ 1) for m, c in ts] for ts in tags]
    wanted, width = merge_factor.shape[0] * rows, sub_vectors.shape[1]
    each = wanted // (rows * cols)
    merged = pl.pallas_call(
        functools.partial(merge_kernel, rows, cols, tags),
        out_shape=jax.ShapeDtypeStruct((wanted, width), jnp.float32),
        in_specs=[VMEM] + [VMEM] * len(m_held),
        out_specs=VMEM,
        compiler_params=limit(8),
        cost_estimate=cost([sub_vectors], 2 * wanted * sub_vectors.size),
        name="merge",
    )(sub_vectors, *m_held)
    per = GROUPS // COLOURS
    colours = pl.pallas_call(
        order_kernel,
        out_shape=[jax.ShapeDtypeStruct((1, per) + piece, dtype)] * COLOURS,
        in_specs=[SMEM, VMEM] + [VMEM] * len(others),
        out_specs=[VMEM] * COLOURS,
        compiler_params=limit(4),
        cost_estimate=cost([slices]),
        name="order",
    )(owners, slices, *others)
    colours = list(colours)
    links = [
        (HALF, lambda v: over_row(v, 1)),
        (2, lambda v: over_col(v, 2)),
        (4, lambda v: over_col(v, 4)),
    ]
    masks = [[0] for _ in range(COLOURS)]
    for step in range(2):
        for k in range(COLOURS):
            mask, send = links[(k + step) % 3]
            colours[k] = jnp.concatenate([colours[k], send(colours[k])])
            masks[k] = masks[k] + [m ^ mask for m in masks[k]]
        if step == 0:
            colours, merged = lax.optimization_barrier((colours, merged))
    state = lax.all_to_all(merged.reshape(rows * cols, each, width), ("row", "col"), 0, 0)
    last_round = []
    for k in range(COLOURS):
        mask, send = links[(k + 2) % 3]
        last_round.append(send(colours[k]))
        masks[k] = [masks[k], [m ^ mask for m in masks[k]]]
        masks[k] += [[m ^ 1 for m in ms] for ms in masks[k]]
    last_round, state = lax.optimization_barrier((last_round, state))
    held = []
    for k in range(COLOURS):
        held.append([colours[k], last_round[k], over_col(colours[k], 1), over_col(last_round[k], 1)])

    wide = cols * width
    for k in range(COLOURS):
        first, last = k == 0, k == COLOURS - 1
        groups = range(k * per, (k + 1) * per)
        state = pl.pallas_call(
            functools.partial(chain_kernel, cols, groups, masks[k], first, last),
            out_shape=jax.ShapeDtypeStruct(
                (each, wide) if last else (8, wide), jnp.bfloat16 if last else jnp.float32
            ),
            in_specs=[SMEM, VMEM] + [VMEM] * len(held[k]),
            out_specs=VMEM,
            scratch_shapes=[
                pltpu.VMEM((per, group_rows, reflect), dtype),
                pltpu.VMEM((per, reflect, reflect), dtype),
            ],
            compiler_params=limit(12),
            cost_estimate=cost(held[k], 2 * per * 64 * group_rows * reflect),
            name=f"chain{k}",
        )(offsets, state, *held[k])
    return state


def solution(mesh):
    rows, cols = mesh.shape["row"], mesh.shape["col"]
    in_specs = (
        P("row", "col"),
        P("row", "col"),
        P("col", None, None),
        P("col", None, None),
        P(),
        P(),
    )
    out_specs = P(("row", "col"), None)
    return jax.shard_map(
        functools.partial(local, rows, cols),
        mesh=mesh,
        in_specs=in_specs,
        out_specs=out_specs,
        check_vma=False,
    )
```

```python
import functools

import jax
import jax.numpy as jnp
from jax import lax
from jax.experimental import pallas as pl
from jax.experimental.pallas import tpu as pltpu
from jax.sharding import PartitionSpec as P

GROUPS = 6
COLOURS = 3
HALF = 8
SLICES = 2 * HALF
VMEM = pl.BlockSpec(memory_space=pltpu.VMEM)
SMEM = pl.BlockSpec(memory_space=pltpu.SMEM)
HBM = pl.BlockSpec(memory_space=pltpu.HBM)


def limit(mib):
    return pltpu.CompilerParams(vmem_limit_bytes=mib * 1024 * 1024)


def cost(arrays, flops=0):
    size = sum(a.size * a.dtype.itemsize for a in arrays)
    return pl.CostEstimate(flops=flops, bytes_accessed=size, transcendentals=0)


def slice_index():
    row, col = lax.axis_index("row"), lax.axis_index("col")
    return lax.rem(row, 2) * HALF + lax.rem(col, HALF)


def aligned(index, size):
    return pl.ds(pl.multiple_of(index * size, size), size)


def pack_kernel(basis, factor, out, sems):
    at = aligned(lax.rem(lax.axis_index("row"), 2), HALF)
    pv = basis.shape[1]
    copies = [
        pltpu.make_async_copy(basis.at[at], out.at[:, :pv, :], sems.at[0]),
        pltpu.make_async_copy(factor.at[at], out.at[:, pv:, :], sems.at[1]),
    ]
    for copy in copies:
        copy.start()
    for copy in copies:
        copy.wait()


def places(owners, group):
    half = owners[group] // HALF
    rank = jnp.int32(0)
    for before in range(group):
        rank = rank + (owners[before] // HALF == half).astype(jnp.int32)
    return half, rank


def pick_kernel(owners, held, out):
    mine = lax.axis_index("col") // HALF
    for group in range(GROUPS):
        half, rank = places(owners, group)
        rank = jnp.minimum(rank, out.shape[0] - 1)

        @pl.when(half == mine)
        def _():
            out[rank] = held[lax.rem(owners[group], HALF)]


def order_kernel(owners, held, *refs):
    others, outs = refs[:-COLOURS], refs[-COLOURS:]
    mine = lax.axis_index("col") // HALF
    each = GROUPS // COLOURS
    for group in range(GROUPS):
        half, rank = places(owners, group)
        piece = held[lax.rem(owners[group], HALF)]
        for mask in range(1, len(others) // 2 + 1):
            head, tail = others[2 * mask - 2 : 2 * mask]
            other = tail[jnp.clip(rank - 1, 0, tail.shape[0] - 1)]
            other = jnp.where(rank == 0, head[0], other)
            piece = jnp.where(jnp.bitwise_xor(half, mine) == mask, other, piece)
        outs[group // each][0, group % each] = piece


def merge_kernel(rows, cols, tags, sub, *refs):
    held, total = refs[:-1], refs[-1]
    row, col = lax.axis_index("row"), lax.axis_index("col")
    deep, tall = held[0].shape[2], held[0].shape[1]
    total[...] = jnp.zeros_like(total)
    for own_tags, ref in zip(tags, held):
        for index, (row_mask, col_mask) in enumerate(own_tags):
            j = jnp.bitwise_xor(lax.rem(col, cols // rows), col_mask)
            part = jnp.dot(ref[index], sub[aligned(j, deep), :], preferred_element_type=jnp.float32)
            at = aligned(jnp.bitwise_xor(row, row_mask), tall)
            total[at, :] = total[at, :] + part


def two_terms(x):
    high = x.astype(jnp.bfloat16)
    low = (x - high.astype(jnp.float32)).astype(jnp.bfloat16)
    return jnp.concatenate([high, low], 0)


def both(products):
    half = products.shape[0] // 2
    return products[:half] + products[half:]


def chain_kernel(cols, groups, masks, first, last, offsets, start, *refs):
    held, (out, basis_all, factor_all) = refs[: len(masks)], refs[len(masks) :]
    mine = slice_index()
    pv, pt = basis_all.shape[1] // SLICES, factor_all.shape[1] // SLICES
    for own_masks, ref in zip(masks, held):
        for index, mask in enumerate(own_masks):
            e = jnp.bitwise_xor(mine, mask)
            basis_all[:, aligned(e, pv), :] = ref[index, :, :pv, :]
            factor_all[:, aligned(e, pt), :] = ref[index, :, pv:, :]
    if first:
        n, each, width = start.shape
        pieces = start[...].reshape(n // cols, cols, each, width).sum(0)
        x = jnp.concatenate([pieces[c] for c in range(cols)], 1)
        x = jnp.concatenate([x] + [jnp.zeros_like(x)] * (8 // each - 1), 0)
    else:
        x = start[...]
    wide = x.shape[1]
    group_rows = basis_all.shape[1]
    before = jnp.int32(0)
    for slot, group in enumerate(groups):
        offset = offsets[group]
        x = pltpu.roll(x, lax.rem(before - offset + wide, wide), 1)
        before = offset
        block = x[:, :group_rows]
        weights = both(
            jnp.dot(two_terms(block), basis_all[slot], preferred_element_type=jnp.float32)
        )
        scaled = both(
            lax.dot_general(
                two_terms(weights), factor_all[slot], (((1,), (1,)), ((), ())),
                preferred_element_type=jnp.float32,
            )
        )
        change = both(
            lax.dot_general(
                two_terms(scaled), basis_all[slot], (((1,), (1,)), ((), ())),
                preferred_element_type=jnp.float32,
            )
        )
        x = jnp.concatenate([block - change, x[:, group_rows:]], 1)
    x = pltpu.roll(x, before, 1)
    if last:
        out[...] = x[: out.shape[0]].astype(out.dtype)
    else:
        out[...] = x


def local(rows, cols, sub_vectors, merge_factor, reflectors, wy_factors, owners, offsets):
    share = cols // rows
    halves = cols // HALF

    def over_col(x, mask):
        return lax.ppermute(x, "col", [(c, c ^ mask) for c in range(cols)])

    def over_row(x, mask):
        return lax.ppermute(x, "row", [(r, r ^ mask) for r in range(rows)])

    basis, factor = reflectors[0], wy_factors[0]
    group_rows, reflect = basis.shape
    dtype = basis.dtype
    pv, pt = group_rows // SLICES, reflect // SLICES
    piece = (pv + pt, reflect)

    across = [merge_factor] + [over_col(merge_factor, m * share) for m in range(1, rows)]

    packed = pl.pallas_call(
        pack_kernel,
        out_shape=jax.ShapeDtypeStruct((HALF,) + piece, dtype),
        in_specs=[HBM, HBM],
        out_specs=VMEM,
        scratch_shapes=[pltpu.SemaphoreType.DMA((2,))],
        compiler_params=limit(56),
        cost_estimate=cost([basis, factor]),
        name="pack",
    )(basis.reshape(SLICES, pv, reflect), factor.reshape(SLICES, pt, reflect))
    members = [[h * HALF + c for c in range(HALF)] for h in range(halves)]
    slices = lax.all_to_all(packed, "col", 0, 0, axis_index_groups=members)

    row, top = lax.axis_index("row"), lax.axis_index("col") // share

    def for_row(mask):
        index = top ^ row ^ mask
        block = across[0]
        for k in range(1, rows):
            block = jnp.where(index == k, across[k], block)
        return block

    blocks = [for_row(0)] + [over_row(for_row(m), m) for m in range(1, rows)]
    groups = [range(rows // 2), range(rows // 2, rows)]
    sides = [jnp.stack([blocks[m] for m in group]) for group in groups]
    tags = [[(m, 0) for m in group] for group in groups]

    def double(side, bit):
        sides[side] = jnp.concatenate([sides[side], over_col(sides[side], bit)])
        tags[side] = tags[side] + [(m, c ^ bit) for m, c in tags[side]]

    bit = share // 2
    while bit > 4:
        double(0, bit)
        double(1, bit)
        bit //= 2
    double(0, 2)
    double(1, 4)
    slices, sides = lax.optimization_barrier((slices, sides))

    picked = pl.pallas_call(
        pick_kernel,
        out_shape=jax.ShapeDtypeStruct((GROUPS - 1,) + piece, dtype),
        in_specs=[SMEM, VMEM],
        out_specs=VMEM,
        compiler_params=limit(4),
        cost_estimate=cost([slices]),
        name="pick",
    )(owners, slices)
    heads = [over_col(picked[:1], m * HALF) for m in range(1, halves)]
    tails = [over_col(picked[1:], m * HALF) for m in range(1, halves)]
    heads, sides = lax.optimization_barrier((heads, sides))
    others = [x for pair in zip(heads, tails) for x in pair]
    late = jnp.concatenate([over_col(sides[0], 4), over_col(sides[1], 2)])
    late_tags = [(m, c ^ 4) for m, c in tags[0]] + [(m, c ^ 2) for m, c in tags[1]]
    m_held = [jnp.concatenate(sides), late]
    tags = [tags[0] + tags[1], late_tags]
    m_held += [over_col(x, 1) for x in m_held]
    tags += [[(m, c ^ 1) for m, c in ts] for ts in tags]
    wanted, width = merge_factor.shape[0] * rows, sub_vectors.shape[1]
    each = wanted // (rows * cols)
    merged = pl.pallas_call(
        functools.partial(merge_kernel, rows, cols, tags),
        out_shape=jax.ShapeDtypeStruct((wanted, width), jnp.float32),
        in_specs=[VMEM] + [VMEM] * len(m_held),
        out_specs=VMEM,
        compiler_params=limit(8),
        cost_estimate=cost([sub_vectors], 2 * wanted * sub_vectors.size),
        name="merge",
    )(sub_vectors, *m_held)
    per = GROUPS // COLOURS
    colours = pl.pallas_call(
        order_kernel,
        out_shape=[jax.ShapeDtypeStruct((1, per) + piece, dtype)] * COLOURS,
        in_specs=[SMEM, VMEM] + [VMEM] * len(others),
        out_specs=[VMEM] * COLOURS,
        compiler_params=limit(4),
        cost_estimate=cost([slices]),
        name="order",
    )(owners, slices, *others)
    colours = list(colours)
    links = [
        (HALF, lambda v: over_row(v, 1)),
        (2, lambda v: over_col(v, 2)),
        (4, lambda v: over_col(v, 4)),
    ]
    masks = [[0] for _ in range(COLOURS)]
    for step in range(2):
        for k in range(COLOURS):
            mask, send = links[(k + step) % 3]
            colours[k] = jnp.concatenate([colours[k], send(colours[k])])
            masks[k] = masks[k] + [m ^ mask for m in masks[k]]
        if step == 0:
            colours, merged = lax.optimization_barrier((colours, merged))
    state = lax.all_to_all(merged.reshape(rows * cols, each, width), ("row", "col"), 0, 0)
    last_round = []
    for k in range(COLOURS):
        mask, send = links[(k + 2) % 3]
        last_round.append(send(colours[k]))
        masks[k] = [masks[k], [m ^ mask for m in masks[k]]]
        masks[k] += [[m ^ 1 for m in ms] for ms in masks[k]]
    last_round, state = lax.optimization_barrier((last_round, state))
    held = []
    for k in range(COLOURS):
        held.append([colours[k], last_round[k], over_col(colours[k], 1), over_col(last_round[k], 1)])

    wide = cols * width
    for k in range(COLOURS):
        first, last = k == 0, k == COLOURS - 1
        groups = range(k * per, (k + 1) * per)
        state = pl.pallas_call(
            functools.partial(chain_kernel, cols, groups, masks[k], first, last),
            out_shape=jax.ShapeDtypeStruct(
                (each, wide) if last else (8, wide), jnp.bfloat16 if last else jnp.float32
            ),
            in_specs=[SMEM, VMEM] + [VMEM] * len(held[k]),
            out_specs=VMEM,
            scratch_shapes=[
                pltpu.VMEM((per, group_rows, reflect), dtype),
                pltpu.VMEM((per, reflect, reflect), dtype),
            ],
            compiler_params=limit(12),
            cost_estimate=cost(held[k], 2 * per * 64 * group_rows * reflect),
            name=f"chain{k}",
        )(offsets, state, *held[k])
    return state


def solution(mesh):
    rows, cols = mesh.shape["row"], mesh.shape["col"]
    in_specs = (
        P("row", "col"),
        P("row", "col"),
        P("col", None, None),
        P("col", None, None),
        P(),
        P(),
    )
    out_specs = P(("row", "col"), None)
    return jax.shard_map(
        functools.partial(local, rows, cols),
        mesh=mesh,
        in_specs=in_specs,
        out_specs=out_specs,
        check_vma=False,
    )
```

```python
import functools

import jax
import jax.numpy as jnp
from jax import lax
from jax.experimental import pallas as pl
from jax.experimental.pallas import tpu as pltpu
from jax.sharding import PartitionSpec as P

GROUPS = 6
SETS = ((0, 1, 2, 3), (4, 5))
HALF = 8
SLICES = 2 * HALF
VMEM = pl.BlockSpec(memory_space=pltpu.VMEM)
SMEM = pl.BlockSpec(memory_space=pltpu.SMEM)
HBM = pl.BlockSpec(memory_space=pltpu.HBM)


def limit(mib):
    return pltpu.CompilerParams(vmem_limit_bytes=mib * 1024 * 1024)


def cost(arrays, flops=0):
    size = sum(a.size * a.dtype.itemsize for a in arrays)
    return pl.CostEstimate(flops=flops, bytes_accessed=size, transcendentals=0)


def slice_index():
    row, col = lax.axis_index("row"), lax.axis_index("col")
    return lax.rem(row, 2) * HALF + lax.rem(col, HALF)


def aligned(index, size):
    return pl.ds(pl.multiple_of(index * size, size), size)


def pack_kernel(basis, factor, out, sems):
    at = aligned(lax.rem(lax.axis_index("row"), 2), HALF)
    pv = basis.shape[1]
    copies = [
        pltpu.make_async_copy(basis.at[at], out.at[:, :pv, :], sems.at[0]),
        pltpu.make_async_copy(factor.at[at], out.at[:, pv:, :], sems.at[1]),
    ]
    for copy in copies:
        copy.start()
    for copy in copies:
        copy.wait()


def places(owners, group):
    half = owners[group] // HALF
    rank = jnp.int32(0)
    for before in range(group):
        rank = rank + (owners[before] // HALF == half).astype(jnp.int32)
    return half, rank


def pick_kernel(owners, held, out):
    mine = lax.axis_index("col") // HALF
    for group in range(GROUPS):
        half, rank = places(owners, group)
        rank = jnp.minimum(rank, out.shape[0] - 1)

        @pl.when(half == mine)
        def _():
            out[rank] = held[lax.rem(owners[group], HALF)]


def order_kernel(owners, held, *refs):
    others, outs = refs[: -len(SETS)], refs[-len(SETS) :]
    mine = lax.axis_index("col") // HALF
    for groups, out in zip(SETS, outs):
        for slot, group in enumerate(groups):
            half, rank = places(owners, group)
            piece = held[lax.rem(owners[group], HALF)]
            for mask, ref in enumerate(others, 1):
                other = ref[jnp.minimum(rank, ref.shape[0] - 1)]
                piece = jnp.where(jnp.bitwise_xor(half, mine) == mask, other, piece)
            out[0, slot] = piece


def by_core(pair):
    if pair[0] == pair[1]:
        return pair[0]
    return jnp.where(lax.rem(lax.axis_index("col"), 2) == 0, pair[0], pair[1])


def swap(pair):
    return (pair[1] ^ 1, pair[0] ^ 1)


def merge_kernel(rows, cols, tags, ready, sub, *refs):
    held, total = refs[:-1], refs[-1]
    row, col = lax.axis_index("row"), lax.axis_index("col")
    deep, tall = held[0].shape[2], held[0].shape[1]
    total[...] = jnp.zeros_like(total)
    for own_tags, ref in zip(tags, held):
        for index, (row_mask, col_mask) in enumerate(own_tags):
            j = jnp.bitwise_xor(lax.rem(col, cols // rows), by_core(col_mask))
            part = jnp.dot(ref[index], sub[aligned(j, deep), :], preferred_element_type=jnp.float32)
            at = aligned(jnp.bitwise_xor(row, row_mask), tall)
            total[at, :] = total[at, :] + part


def two_terms(x):
    high = x.astype(jnp.bfloat16)
    low = (x - high.astype(jnp.float32)).astype(jnp.bfloat16)
    return jnp.concatenate([high, low], 0)


def both(products):
    half = products.shape[0] // 2
    return products[:half] + products[half:]


def chain_kernel(cols, groups, masks, first, last, offsets, start, *refs):
    held, (out, basis_all, factor_all) = refs[: len(masks)], refs[len(masks) :]
    mine = slice_index()
    pv, pt = basis_all.shape[1] // SLICES, factor_all.shape[1] // SLICES
    for own_masks, ref in zip(masks, held):
        for index, mask in enumerate(own_masks):
            e = jnp.bitwise_xor(mine, by_core(mask))
            basis_all[:, aligned(e, pv), :] = ref[index, :, :pv, :]
            factor_all[:, aligned(e, pt), :] = ref[index, :, pv:, :]
    if first:
        n, each, width = start.shape
        pieces = start[...].reshape(n // cols, cols, each, width).sum(0)
        x = jnp.concatenate([pieces[c] for c in range(cols)], 1)
        x = jnp.concatenate([x] + [jnp.zeros_like(x)] * (8 // each - 1), 0)
    else:
        x = start[...]
    wide = x.shape[1]
    group_rows = basis_all.shape[1]
    before = jnp.int32(0)
    for slot, group in enumerate(groups):
        offset = offsets[group]
        x = pltpu.roll(x, lax.rem(before - offset + wide, wide), 1)
        before = offset
        block = x[:, :group_rows]
        weights = both(
            jnp.dot(two_terms(block), basis_all[slot], preferred_element_type=jnp.float32)
        )
        scaled = both(
            lax.dot_general(
                two_terms(weights), factor_all[slot], (((1,), (1,)), ((), ())),
                preferred_element_type=jnp.float32,
            )
        )
        change = both(
            lax.dot_general(
                two_terms(scaled), basis_all[slot], (((1,), (1,)), ((), ())),
                preferred_element_type=jnp.float32,
            )
        )
        x = jnp.concatenate([block - change, x[:, group_rows:]], 1)
    x = pltpu.roll(x, before, 1)
    if last:
        out[...] = x[: out.shape[0]].astype(out.dtype)
    else:
        out[...] = x


def local(rows, cols, sub_vectors, merge_factor, reflectors, wy_factors, owners, offsets):
    share = cols // rows
    halves = cols // HALF

    def over_col(x, mask):
        return lax.ppermute(x, "col", [(c, c ^ mask) for c in range(cols)])

    def over_row(x, mask):
        return lax.ppermute(x, "row", [(r, r ^ mask) for r in range(rows)])

    def over_links(x, *bits):
        pairs = []
        for r in range(rows):
            for c in range(cols):
                bit = bits[c % 2]
                to = (r ^ 1) * cols + c if bit == HALF else r * cols + (c ^ bit)
                pairs.append((r * cols + c, to))
        return lax.ppermute(x, ("row", "col"), pairs)

    basis, factor = reflectors[0], wy_factors[0]
    group_rows, reflect = basis.shape
    dtype = basis.dtype
    pv, pt = group_rows // SLICES, reflect // SLICES
    piece = (pv + pt, reflect)

    across = [merge_factor] + [over_col(merge_factor, m * share) for m in range(1, rows)]

    packed = pl.pallas_call(
        pack_kernel,
        out_shape=jax.ShapeDtypeStruct((HALF,) + piece, dtype),
        in_specs=[HBM, HBM],
        out_specs=VMEM,
        scratch_shapes=[pltpu.SemaphoreType.DMA((2,))],
        compiler_params=limit(56),
        cost_estimate=cost([basis, factor]),
        name="pack",
    )(basis.reshape(SLICES, pv, reflect), factor.reshape(SLICES, pt, reflect))
    members = [[h * HALF + c for c in range(HALF)] for h in range(halves)]
    slices = lax.all_to_all(packed, "col", 0, 0, axis_index_groups=members)

    row, top = lax.axis_index("row"), lax.axis_index("col") // share

    def for_row(mask):
        index = top ^ row ^ mask
        block = across[0]
        for k in range(1, rows):
            block = jnp.where(index == k, across[k], block)
        return block

    m_held = jnp.stack([for_row(0)] + [over_row(for_row(m), m) for m in range(1, rows)])
    tags = [(m, (0, 0)) for m in range(rows)]

    def double(held, tags, *bits):
        held = jnp.concatenate([held, over_links(held, *bits)])
        return held, tags + [(m, (c[0] ^ bits[0], c[1] ^ bits[1])) for m, c in tags]

    bit = share // 2
    while bit > 4:
        m_held, tags = double(m_held, tags, bit, bit)
        bit //= 2
    m_held, tags = double(m_held, tags, 2, 4)
    slices, m_held = lax.optimization_barrier((slices, m_held))

    picked = pl.pallas_call(
        pick_kernel,
        out_shape=jax.ShapeDtypeStruct((GROUPS - 1,) + piece, dtype),
        in_specs=[SMEM, VMEM],
        out_specs=VMEM,
        compiler_params=limit(4),
        cost_estimate=cost([slices]),
        name="pick",
    )(owners, slices)
    others = [over_col(picked, m * HALF) for m in range(1, halves)]
    ready = over_col(picked[0, :16], 1)
    ready, m_held = lax.optimization_barrier((ready, m_held))
    late = over_links(m_held, 4, 2)
    late_tags = [(m, (c[0] ^ 4, c[1] ^ 2)) for m, c in tags]
    m_held, tags = [m_held, late], [tags, late_tags]
    m_held += [over_col(x, 1) for x in m_held]
    tags += [[(m, swap(c)) for m, c in ts] for ts in tags]
    wanted, width = merge_factor.shape[0] * rows, sub_vectors.shape[1]
    each = wanted // (rows * cols)
    merged = pl.pallas_call(
        functools.partial(merge_kernel, rows, cols, tags),
        out_shape=jax.ShapeDtypeStruct((wanted, width), jnp.float32),
        in_specs=[HBM, VMEM] + [VMEM] * len(m_held),
        out_specs=VMEM,
        compiler_params=limit(8),
        cost_estimate=cost([sub_vectors], 2 * wanted * sub_vectors.size),
        name="merge",
    )(ready, sub_vectors, *m_held)
    parts = pl.pallas_call(
        order_kernel,
        out_shape=[jax.ShapeDtypeStruct((1, len(groups)) + piece, dtype) for groups in SETS],
        in_specs=[SMEM, VMEM] + [VMEM] * len(others),
        out_specs=[VMEM] * len(SETS),
        compiler_params=limit(4),
        cost_estimate=cost([slices]),
        name="order",
    )(owners, slices, *others)
    parts = list(parts)
    x, y, z = HALF, 2, 4
    links = [[(x, y), (y, z), (z, x)], [(z, z), (x, x), (y, y)]]
    masks = [[(0, 0)] for _ in SETS]

    def other_masks(k, step):
        bits = links[k][step]
        return [(m[0] ^ bits[0], m[1] ^ bits[1]) for m in masks[k]]

    for step in range(2):
        for k in range(len(SETS)):
            parts[k] = jnp.concatenate([parts[k], over_links(parts[k], *links[k][step])])
            masks[k] = masks[k] + other_masks(k, step)
        if step == 0:
            parts, merged = lax.optimization_barrier((parts, merged))

    state = lax.all_to_all(merged.reshape(rows * cols, each, width), ("row", "col"), 0, 0)
    last_round = []
    for k in range(len(SETS)):
        last_round.append(over_links(parts[k], *links[k][2]))
        masks[k] = [masks[k], other_masks(k, 2)]
        masks[k] += [[swap(m) for m in ms] for ms in masks[k]]
    last_round, state = lax.optimization_barrier((last_round, state))
    held = []
    for k in range(len(SETS)):
        held.append([parts[k], last_round[k], over_col(parts[k], 1), over_col(last_round[k], 1)])

    wide = cols * width
    for k, groups in enumerate(SETS):
        first, last = k == 0, k == len(SETS) - 1
        state = pl.pallas_call(
            functools.partial(chain_kernel, cols, groups, masks[k], first, last),
            out_shape=jax.ShapeDtypeStruct(
                (each, wide) if last else (8, wide), jnp.bfloat16 if last else jnp.float32
            ),
            in_specs=[SMEM, VMEM] + [VMEM] * len(held[k]),
            out_specs=VMEM,
            scratch_shapes=[
                pltpu.VMEM((len(groups), group_rows, reflect), dtype),
                pltpu.VMEM((len(groups), reflect, reflect), dtype),
            ],
            compiler_params=limit(12),
            cost_estimate=cost(held[k], 2 * len(groups) * 64 * group_rows * reflect),
            name=f"chain{k}",
        )(offsets, state, *held[k])
    return state


def solution(mesh):
    rows, cols = mesh.shape["row"], mesh.shape["col"]
    in_specs = (
        P("row", "col"),
        P("row", "col"),
        P("col", None, None),
        P("col", None, None),
        P(),
        P(),
    )
    out_specs = P(("row", "col"), None)
    return jax.shard_map(
        functools.partial(local, rows, cols),
        mesh=mesh,
        in_specs=in_specs,
        out_specs=out_specs,
        check_vma=False,
    )
```

```python
import functools

import jax
import jax.numpy as jnp
from jax import lax
from jax.experimental import pallas as pl
from jax.experimental.pallas import tpu as pltpu
from jax.sharding import PartitionSpec as P

GROUPS = 6
COLOURS = 3
CHAINS = ((0,), (1, 2))
HALF = 8
SLICES = 2 * HALF
VMEM = pl.BlockSpec(memory_space=pltpu.VMEM)
SMEM = pl.BlockSpec(memory_space=pltpu.SMEM)
HBM = pl.BlockSpec(memory_space=pltpu.HBM)


def limit(mib):
    return pltpu.CompilerParams(vmem_limit_bytes=mib * 1024 * 1024)


def cost(arrays, flops=0):
    size = sum(a.size * a.dtype.itemsize for a in arrays)
    return pl.CostEstimate(flops=flops, bytes_accessed=size, transcendentals=0)


def slice_index():
    row, col = lax.axis_index("row"), lax.axis_index("col")
    return lax.rem(row, 2) * HALF + lax.rem(col, HALF)


def aligned(index, size):
    return pl.ds(pl.multiple_of(index * size, size), size)


def pack_kernel(basis, factor, out, sems):
    at = aligned(lax.rem(lax.axis_index("row"), 2), HALF)
    pv = basis.shape[1]
    copies = [
        pltpu.make_async_copy(basis.at[at], out.at[:, :pv, :], sems.at[0]),
        pltpu.make_async_copy(factor.at[at], out.at[:, pv:, :], sems.at[1]),
    ]
    for copy in copies:
        copy.start()
    for copy in copies:
        copy.wait()


def places(owners, group):
    half = owners[group] // HALF
    rank = jnp.int32(0)
    for before in range(group):
        rank = rank + (owners[before] // HALF == half).astype(jnp.int32)
    return half, rank


def pick_kernel(owners, held, out):
    mine = lax.axis_index("col") // HALF
    for group in range(GROUPS):
        half, rank = places(owners, group)
        rank = jnp.minimum(rank, out.shape[0] - 1)

        @pl.when(half == mine)
        def _():
            out[rank] = held[lax.rem(owners[group], HALF)]


def order_kernel(owners, held, *refs):
    others, outs = refs[:-COLOURS], refs[-COLOURS:]
    mine = lax.axis_index("col") // HALF
    each = GROUPS // COLOURS
    for group in range(GROUPS):
        half, rank = places(owners, group)
        piece = held[lax.rem(owners[group], HALF)]
        for mask, ref in enumerate(others, 1):
            other = ref[jnp.minimum(rank, ref.shape[0] - 1)]
            piece = jnp.where(jnp.bitwise_xor(half, mine) == mask, other, piece)
        outs[group // each][0, group % each] = piece


def merge_kernel(rows, cols, tags, ready, sub, *refs):
    held, total = refs[:-1], refs[-1]
    row, col = lax.axis_index("row"), lax.axis_index("col")
    deep, tall = held[0].shape[2], held[0].shape[1]
    total[...] = jnp.zeros_like(total)
    for own_tags, ref in zip(tags, held):
        for index, (row_mask, col_mask) in enumerate(own_tags):
            j = jnp.bitwise_xor(lax.rem(col, cols // rows), col_mask)
            part = jnp.dot(ref[index], sub[aligned(j, deep), :], preferred_element_type=jnp.float32)
            at = aligned(jnp.bitwise_xor(row, row_mask), tall)
            total[at, :] = total[at, :] + part


def two_terms(x):
    high = x.astype(jnp.bfloat16)
    low = (x - high.astype(jnp.float32)).astype(jnp.bfloat16)
    return jnp.concatenate([high, low], 0)


def both(products):
    half = products.shape[0] // 2
    return products[:half] + products[half:]


def chain_kernel(cols, groups, slots, masks, first, last, offsets, start, *refs):
    held, (out, basis_all, factor_all) = refs[: len(masks)], refs[len(masks) :]
    mine = slice_index()
    pv, pt = basis_all.shape[1] // SLICES, factor_all.shape[1] // SLICES
    for slot, own_masks, ref in zip(slots, masks, held):
        to = slice(slot, slot + ref.shape[1])
        for index, mask in enumerate(own_masks):
            e = jnp.bitwise_xor(mine, mask)
            basis_all[to, aligned(e, pv), :] = ref[index, :, :pv, :]
            factor_all[to, aligned(e, pt), :] = ref[index, :, pv:, :]
    if first:
        n, each, width = start.shape
        pieces = start[...].reshape(n // cols, cols, each, width).sum(0)
        x = jnp.concatenate([pieces[c] for c in range(cols)], 1)
        x = jnp.concatenate([x] + [jnp.zeros_like(x)] * (8 // each - 1), 0)
    else:
        x = start[...]
    wide = x.shape[1]
    group_rows = basis_all.shape[1]
    before = jnp.int32(0)
    for slot, group in enumerate(groups):
        offset = offsets[group]
        x = pltpu.roll(x, lax.rem(before - offset + wide, wide), 1)
        before = offset
        block = x[:, :group_rows]
        weights = both(
            jnp.dot(two_terms(block), basis_all[slot], preferred_element_type=jnp.float32)
        )
        scaled = both(
            lax.dot_general(
                two_terms(weights), factor_all[slot], (((1,), (1,)), ((), ())),
                preferred_element_type=jnp.float32,
            )
        )
        change = both(
            lax.dot_general(
                two_terms(scaled), basis_all[slot], (((1,), (1,)), ((), ())),
                preferred_element_type=jnp.float32,
            )
        )
        x = jnp.concatenate([block - change, x[:, group_rows:]], 1)
    x = pltpu.roll(x, before, 1)
    if last:
        out[...] = x[: out.shape[0]].astype(out.dtype)
    else:
        out[...] = x


def local(rows, cols, sub_vectors, merge_factor, reflectors, wy_factors, owners, offsets):
    share = cols // rows
    halves = cols // HALF

    def over_col(x, mask):
        return lax.ppermute(x, "col", [(c, c ^ mask) for c in range(cols)])

    def over_row(x, mask):
        return lax.ppermute(x, "row", [(r, r ^ mask) for r in range(rows)])

    basis, factor = reflectors[0], wy_factors[0]
    group_rows, reflect = basis.shape
    dtype = basis.dtype
    pv, pt = group_rows // SLICES, reflect // SLICES
    piece = (pv + pt, reflect)

    packed = pl.pallas_call(
        pack_kernel,
        out_shape=jax.ShapeDtypeStruct((HALF,) + piece, dtype),
        in_specs=[HBM, HBM],
        out_specs=VMEM,
        scratch_shapes=[pltpu.SemaphoreType.DMA((2,))],
        compiler_params=limit(56),
        cost_estimate=cost([basis, factor]),
        name="pack",
    )(basis.reshape(SLICES, pv, reflect), factor.reshape(SLICES, pt, reflect))
    packed, merge_factor = lax.optimization_barrier((packed, merge_factor))
    members = [[h * HALF + c for c in range(HALF)] for h in range(halves)]
    slices = lax.all_to_all(packed, "col", 0, 0, axis_index_groups=members)

    picked = pl.pallas_call(
        pick_kernel,
        out_shape=jax.ShapeDtypeStruct((GROUPS - 1,) + piece, dtype),
        in_specs=[SMEM, VMEM],
        out_specs=VMEM,
        compiler_params=limit(4),
        cost_estimate=cost([slices]),
        name="pick",
    )(owners, slices)
    ready = over_col(picked[0, :16], HALF)
    others = [over_col(picked, m * HALF) for m in range(1, halves)]

    across = [merge_factor] + [over_col(merge_factor, m * share) for m in range(1, rows)]

    row, top = lax.axis_index("row"), lax.axis_index("col") // share

    def for_row(mask):
        index = top ^ row ^ mask
        block = across[0]
        for k in range(1, rows):
            block = jnp.where(index == k, across[k], block)
        return block

    m_held = jnp.stack([for_row(0)] + [over_row(for_row(m), m) for m in range(1, rows)])
    ready, m_held = lax.optimization_barrier((ready, m_held))
    tags = [(m, 0) for m in range(rows)]
    bit = share // 2
    while bit > 4:
        m_held = jnp.concatenate([m_held, over_col(m_held, bit)])
        tags = tags + [(m, c ^ bit) for m, c in tags]
        bit //= 2
    late = jnp.concatenate([over_col(m_held, mask) for mask in (2, 4, 6)])
    late_tags = [(m, c ^ mask) for mask in (2, 4, 6) for m, c in tags]
    m_held, tags = [m_held, late], [tags, late_tags]
    m_held += [over_col(x, 1) for x in m_held]
    tags += [[(m, c ^ 1) for m, c in ts] for ts in tags]
    wanted, width = merge_factor.shape[0] * rows, sub_vectors.shape[1]
    each = wanted // (rows * cols)
    merged = pl.pallas_call(
        functools.partial(merge_kernel, rows, cols, tags),
        out_shape=jax.ShapeDtypeStruct((wanted, width), jnp.float32),
        in_specs=[HBM, VMEM] + [VMEM] * len(m_held),
        out_specs=VMEM,
        compiler_params=limit(8),
        cost_estimate=cost([sub_vectors], 2 * wanted * sub_vectors.size),
        name="merge",
    )(ready, sub_vectors, *m_held)
    per = GROUPS // COLOURS
    colours = pl.pallas_call(
        order_kernel,
        out_shape=[jax.ShapeDtypeStruct((1, per) + piece, dtype)] * COLOURS,
        in_specs=[SMEM, VMEM] + [VMEM] * len(others),
        out_specs=[VMEM] * COLOURS,
        compiler_params=limit(4),
        cost_estimate=cost([slices]),
        name="order",
    )(owners, slices, *others)
    colours = list(colours)
    links = [
        (HALF, lambda v: over_row(v, 1)),
        (2, lambda v: over_col(v, 2)),
        (4, lambda v: over_col(v, 4)),
    ]
    masks = [[0] for _ in range(COLOURS)]
    for step in range(2):
        for k in range(COLOURS):
            mask, send = links[(k + step) % 3]
            colours[k] = jnp.concatenate([colours[k], send(colours[k])])
            masks[k] = masks[k] + [m ^ mask for m in masks[k]]
        if step == 0:
            colours, merged = lax.optimization_barrier((colours, merged))
    state = lax.all_to_all(merged.reshape(rows * cols, each, width), ("row", "col"), 0, 0)
    last_round = []
    for k in range(COLOURS):
        mask, send = links[(k + 2) % 3]
        last_round.append(send(colours[k]))
        masks[k] = [masks[k], [m ^ mask for m in masks[k]]]
        masks[k] += [[m ^ 1 for m in ms] for ms in masks[k]]
    last_round, state = lax.optimization_barrier((last_round, state))
    held = []
    for k in range(COLOURS):
        held.append([colours[k], last_round[k], over_col(colours[k], 1), over_col(last_round[k], 1)])

    wide = cols * width
    for members in CHAINS:
        first, last = members[0] == 0, members[-1] == COLOURS - 1
        groups = range(members[0] * per, (members[-1] + 1) * per)
        arrays = [x for k in members for x in held[k]]
        slots = [per * i for i, k in enumerate(members) for _ in held[k]]
        state = pl.pallas_call(
            functools.partial(
                chain_kernel, cols, groups, slots, sum((masks[k] for k in members), []), first, last
            ),
            out_shape=jax.ShapeDtypeStruct(
                (each, wide) if last else (8, wide), jnp.bfloat16 if last else jnp.float32
            ),
            in_specs=[SMEM, VMEM] + [VMEM] * len(arrays),
            out_specs=VMEM,
            scratch_shapes=[
                pltpu.VMEM((len(groups), group_rows, reflect), dtype),
                pltpu.VMEM((len(groups), reflect, reflect), dtype),
            ],
            compiler_params=limit(12),
            cost_estimate=cost(arrays, 2 * len(groups) * 64 * group_rows * reflect),
            name=f"chain{members[0]}",
        )(offsets, state, *arrays)
    return state


def solution(mesh):
    rows, cols = mesh.shape["row"], mesh.shape["col"]
    in_specs = (
        P("row", "col"),
        P("row", "col"),
        P("col", None, None),
        P("col", None, None),
        P(),
        P(),
    )
    out_specs = P(("row", "col"), None)
    return jax.shard_map(
        functools.partial(local, rows, cols),
        mesh=mesh,
        in_specs=in_specs,
        out_specs=out_specs,
        check_vma=False,
    )
```

```python
import functools

import jax
import jax.numpy as jnp
from jax import lax
from jax.experimental import pallas as pl
from jax.experimental.pallas import tpu as pltpu
from jax.sharding import PartitionSpec as P

GROUPS = 6
COLOURS = 3
CHAINS = ((0,), (1, 2))
HALF = 8
SLICES = 2 * HALF
VMEM = pl.BlockSpec(memory_space=pltpu.VMEM)
SMEM = pl.BlockSpec(memory_space=pltpu.SMEM)
HBM = pl.BlockSpec(memory_space=pltpu.HBM)


def limit(mib):
    return pltpu.CompilerParams(vmem_limit_bytes=mib * 1024 * 1024)


def cost(arrays, flops=0):
    size = sum(a.size * a.dtype.itemsize for a in arrays)
    return pl.CostEstimate(flops=flops, bytes_accessed=size, transcendentals=0)


def slice_index():
    row, col = lax.axis_index("row"), lax.axis_index("col")
    return lax.rem(row, 2) * HALF + lax.rem(col, HALF)


def aligned(index, size):
    return pl.ds(pl.multiple_of(index * size, size), size)


def pack_kernel(basis, factor, out, sems):
    at = aligned(lax.rem(lax.axis_index("row"), 2), HALF)
    pv = basis.shape[1]
    copies = [
        pltpu.make_async_copy(basis.at[at], out.at[:, :pv, :], sems.at[0]),
        pltpu.make_async_copy(factor.at[at], out.at[:, pv:, :], sems.at[1]),
    ]
    for copy in copies:
        copy.start()
    for copy in copies:
        copy.wait()


def places(owners, group):
    half = owners[group] // HALF
    rank = jnp.int32(0)
    for before in range(group):
        rank = rank + (owners[before] // HALF == half).astype(jnp.int32)
    return half, rank


def pick_kernel(owners, held, out):
    mine = lax.axis_index("col") // HALF
    for group in range(GROUPS):
        half, rank = places(owners, group)
        rank = jnp.minimum(rank, out.shape[0] - 1)

        @pl.when(half == mine)
        def _():
            out[rank] = held[lax.rem(owners[group], HALF)]


def order_kernel(owners, held, *refs):
    others, outs = refs[:-COLOURS], refs[-COLOURS:]
    mine = lax.axis_index("col") // HALF
    each = GROUPS // COLOURS
    for group in range(GROUPS):
        half, rank = places(owners, group)
        piece = held[lax.rem(owners[group], HALF)]
        for mask, ref in enumerate(others, 1):
            other = ref[jnp.minimum(rank, ref.shape[0] - 1)]
            piece = jnp.where(jnp.bitwise_xor(half, mine) == mask, other, piece)
        outs[group // each][0, group % each] = piece


def merge_kernel(rows, cols, tags, sub, *refs):
    held, total = refs[:-1], refs[-1]
    row, col = lax.axis_index("row"), lax.axis_index("col")
    deep, tall = held[0].shape[2], held[0].shape[1]
    total[...] = jnp.zeros_like(total)
    for own_tags, ref in zip(tags, held):
        for index, (row_mask, col_mask) in enumerate(own_tags):
            j = jnp.bitwise_xor(lax.rem(col, cols // rows), col_mask)
            part = jnp.dot(ref[index], sub[aligned(j, deep), :], preferred_element_type=jnp.float32)
            at = aligned(jnp.bitwise_xor(row, row_mask), tall)
            total[at, :] = total[at, :] + part


def two_terms(x):
    high = x.astype(jnp.bfloat16)
    low = (x - high.astype(jnp.float32)).astype(jnp.bfloat16)
    return jnp.concatenate([high, low], 0)


def both(products):
    half = products.shape[0] // 2
    return products[:half] + products[half:]


def chain_kernel(cols, groups, slots, masks, first, last, offsets, start, *refs):
    held, (out, basis_all, factor_all) = refs[: len(masks)], refs[len(masks) :]
    mine = slice_index()
    pv, pt = basis_all.shape[1] // SLICES, factor_all.shape[1] // SLICES
    for slot, own_masks, ref in zip(slots, masks, held):
        to = slice(slot, slot + ref.shape[1])
        for index, mask in enumerate(own_masks):
            e = jnp.bitwise_xor(mine, mask)
            basis_all[to, aligned(e, pv), :] = ref[index, :, :pv, :]
            factor_all[to, aligned(e, pt), :] = ref[index, :, pv:, :]
    if first:
        n, each, width = start.shape
        pieces = start[...].reshape(n // cols, cols, each, width).sum(0)
        x = jnp.concatenate([pieces[c] for c in range(cols)], 1)
        x = jnp.concatenate([x] + [jnp.zeros_like(x)] * (8 // each - 1), 0)
    else:
        x = start[...]
    wide = x.shape[1]
    group_rows = basis_all.shape[1]
    before = jnp.int32(0)
    for slot, group in enumerate(groups):
        offset = offsets[group]
        x = pltpu.roll(x, lax.rem(before - offset + wide, wide), 1)
        before = offset
        block = x[:, :group_rows]
        weights = both(
            jnp.dot(two_terms(block), basis_all[slot], preferred_element_type=jnp.float32)
        )
        scaled = both(
            lax.dot_general(
                two_terms(weights), factor_all[slot], (((1,), (1,)), ((), ())),
                preferred_element_type=jnp.float32,
            )
        )
        change = both(
            lax.dot_general(
                two_terms(scaled), basis_all[slot], (((1,), (1,)), ((), ())),
                preferred_element_type=jnp.float32,
            )
        )
        x = jnp.concatenate([block - change, x[:, group_rows:]], 1)
    x = pltpu.roll(x, before, 1)
    if last:
        out[...] = x[: out.shape[0]].astype(out.dtype)
    else:
        out[...] = x


def local(rows, cols, sub_vectors, merge_factor, reflectors, wy_factors, owners, offsets):
    share = cols // rows
    halves = cols // HALF

    def over_col(x, mask):
        return lax.ppermute(x, "col", [(c, c ^ mask) for c in range(cols)])

    def over_row(x, mask):
        return lax.ppermute(x, "row", [(r, r ^ mask) for r in range(rows)])

    basis, factor = reflectors[0], wy_factors[0]
    group_rows, reflect = basis.shape
    dtype = basis.dtype
    pv, pt = group_rows // SLICES, reflect // SLICES
    piece = (pv + pt, reflect)

    across = [merge_factor] + [over_col(merge_factor, m * share) for m in range(1, rows)]

    packed = pl.pallas_call(
        pack_kernel,
        out_shape=jax.ShapeDtypeStruct((HALF,) + piece, dtype),
        in_specs=[HBM, HBM],
        out_specs=VMEM,
        scratch_shapes=[pltpu.SemaphoreType.DMA((2,))],
        compiler_params=limit(56),
        cost_estimate=cost([basis, factor]),
        name="pack",
    )(basis.reshape(SLICES, pv, reflect), factor.reshape(SLICES, pt, reflect))
    members = [[h * HALF + c for c in range(HALF)] for h in range(halves)]
    slices = lax.all_to_all(packed, "col", 0, 0, axis_index_groups=members)

    row, top = lax.axis_index("row"), lax.axis_index("col") // share

    def for_row(mask):
        index = top ^ row ^ mask
        block = across[0]
        for k in range(1, rows):
            block = jnp.where(index == k, across[k], block)
        return block

    m_held = jnp.stack([for_row(0)] + [over_row(for_row(m), m) for m in range(1, rows)])
    slices, m_held = lax.optimization_barrier((slices, m_held))

    picked = pl.pallas_call(
        pick_kernel,
        out_shape=jax.ShapeDtypeStruct((GROUPS - 1,) + piece, dtype),
        in_specs=[SMEM, VMEM],
        out_specs=VMEM,
        compiler_params=limit(4),
        cost_estimate=cost([slices]),
        name="pick",
    )(owners, slices)
    others = [over_col(picked, m * HALF) for m in range(1, halves)]

    tags = [(m, 0) for m in range(rows)]
    bit = share // 2
    while bit > 4:
        m_held = jnp.concatenate([m_held, over_col(m_held, bit)])
        tags = tags + [(m, c ^ bit) for m, c in tags]
        bit //= 2
    late = jnp.concatenate([over_col(m_held, mask) for mask in (2, 4, 6)])
    late_tags = [(m, c ^ mask) for mask in (2, 4, 6) for m, c in tags]
    m_held, tags = [m_held, late], [tags, late_tags]
    m_held += [over_col(x, 1) for x in m_held]
    tags += [[(m, c ^ 1) for m, c in ts] for ts in tags]
    wanted, width = merge_factor.shape[0] * rows, sub_vectors.shape[1]
    each = wanted // (rows * cols)
    merged = pl.pallas_call(
        functools.partial(merge_kernel, rows, cols, tags),
        out_shape=jax.ShapeDtypeStruct((wanted, width), jnp.float32),
        in_specs=[VMEM] + [VMEM] * len(m_held),
        out_specs=VMEM,
        compiler_params=limit(8),
        cost_estimate=cost([sub_vectors], 2 * wanted * sub_vectors.size),
        name="merge",
    )(sub_vectors, *m_held)
    per = GROUPS // COLOURS
    colours = pl.pallas_call(
        order_kernel,
        out_shape=[jax.ShapeDtypeStruct((1, per) + piece, dtype)] * COLOURS,
        in_specs=[SMEM, VMEM] + [VMEM] * len(others),
        out_specs=[VMEM] * COLOURS,
        compiler_params=limit(4),
        cost_estimate=cost([slices]),
        name="order",
    )(owners, slices, *others)
    colours = list(colours)
    links = [
        (HALF, lambda v: over_row(v, 1)),
        (2, lambda v: over_col(v, 2)),
        (4, lambda v: over_col(v, 4)),
    ]
    masks = [[0] for _ in range(COLOURS)]
    for step in range(2):
        for k in range(COLOURS):
            mask, send = links[(k + step) % 3]
            colours[k] = jnp.concatenate([colours[k], send(colours[k])])
            masks[k] = masks[k] + [m ^ mask for m in masks[k]]
        if step == 0:
            colours, merged = lax.optimization_barrier((colours, merged))
    state = lax.all_to_all(merged.reshape(rows * cols, each, width), ("row", "col"), 0, 0)
    last_round = []
    for k in range(COLOURS):
        mask, send = links[(k + 2) % 3]
        last_round.append(send(colours[k]))
        masks[k] = [masks[k], [m ^ mask for m in masks[k]]]
        masks[k] += [[m ^ 1 for m in ms] for ms in masks[k]]
    last_round, state = lax.optimization_barrier((last_round, state))
    held = []
    for k in range(COLOURS):
        held.append([colours[k], last_round[k], over_col(colours[k], 1), over_col(last_round[k], 1)])

    wide = cols * width
    for members in CHAINS:
        first, last = members[0] == 0, members[-1] == COLOURS - 1
        groups = range(members[0] * per, (members[-1] + 1) * per)
        arrays = [x for k in members for x in held[k]]
        slots = [per * i for i, k in enumerate(members) for _ in held[k]]
        state = pl.pallas_call(
            functools.partial(
                chain_kernel, cols, groups, slots, sum((masks[k] for k in members), []), first, last
            ),
            out_shape=jax.ShapeDtypeStruct(
                (each, wide) if last else (8, wide), jnp.bfloat16 if last else jnp.float32
            ),
            in_specs=[SMEM, VMEM] + [VMEM] * len(arrays),
            out_specs=VMEM,
            scratch_shapes=[
                pltpu.VMEM((len(groups), group_rows, reflect), dtype),
                pltpu.VMEM((len(groups), reflect, reflect), dtype),
            ],
            compiler_params=limit(12),
            cost_estimate=cost(arrays, 2 * len(groups) * 64 * group_rows * reflect),
            name=f"chain{members[0]}",
        )(offsets, state, *arrays)
    return state


def solution(mesh):
    rows, cols = mesh.shape["row"], mesh.shape["col"]
    in_specs = (
        P("row", "col"),
        P("row", "col"),
        P("col", None, None),
        P("col", None, None),
        P(),
        P(),
    )
    out_specs = P(("row", "col"), None)
    return jax.shard_map(
        functools.partial(local, rows, cols),
        mesh=mesh,
        in_specs=in_specs,
        out_specs=out_specs,
        check_vma=False,
    )
```

```python
import functools

import jax
import jax.numpy as jnp
from jax import lax
from jax.experimental import pallas as pl
from jax.experimental.pallas import tpu as pltpu
from jax.sharding import PartitionSpec as P

GROUPS = 6
COLOURS = 3
CHAINS = ((0,), (1, 2))
HALF = 8
SLICES = 2 * HALF
VMEM = pl.BlockSpec(memory_space=pltpu.VMEM)
SMEM = pl.BlockSpec(memory_space=pltpu.SMEM)
HBM = pl.BlockSpec(memory_space=pltpu.HBM)


def limit(mib):
    return pltpu.CompilerParams(vmem_limit_bytes=mib * 1024 * 1024)


def cost(arrays, flops=0):
    size = sum(a.size * a.dtype.itemsize for a in arrays)
    return pl.CostEstimate(flops=flops, bytes_accessed=size, transcendentals=0)


def slice_index():
    row, col = lax.axis_index("row"), lax.axis_index("col")
    return lax.rem(row, 2) * HALF + lax.rem(col, HALF)


def aligned(index, size):
    return pl.ds(pl.multiple_of(index * size, size), size)


def pack_kernel(basis, factor, out, sems):
    at = aligned(lax.rem(lax.axis_index("row"), 2), HALF)
    pv = basis.shape[1]
    copies = [
        pltpu.make_async_copy(basis.at[at], out.at[:, :pv, :], sems.at[0]),
        pltpu.make_async_copy(factor.at[at], out.at[:, pv:, :], sems.at[1]),
    ]
    for copy in copies:
        copy.start()
    for copy in copies:
        copy.wait()


def places(owners, group):
    half = owners[group] // HALF
    rank = jnp.int32(0)
    for before in range(group):
        rank = rank + (owners[before] // HALF == half).astype(jnp.int32)
    return half, rank


def pick_kernel(owners, held, out):
    mine = lax.axis_index("col") // HALF
    for group in range(GROUPS):
        half, rank = places(owners, group)
        rank = jnp.minimum(rank, out.shape[0] - 1)

        @pl.when(half == mine)
        def _():
            out[rank] = held[lax.rem(owners[group], HALF)]


def order_kernel(owners, held, *refs):
    others, outs = refs[:-COLOURS], refs[-COLOURS:]
    mine = lax.axis_index("col") // HALF
    each = GROUPS // COLOURS
    for group in range(GROUPS):
        half, rank = places(owners, group)
        piece = held[lax.rem(owners[group], HALF)]
        for mask, ref in enumerate(others, 1):
            other = ref[jnp.minimum(rank, ref.shape[0] - 1)]
            piece = jnp.where(jnp.bitwise_xor(half, mine) == mask, other, piece)
        outs[group // each][0, group % each] = piece


def merge_kernel(rows, cols, tags, sub, *refs):
    held, total = refs[:-1], refs[-1]
    row, col = lax.axis_index("row"), lax.axis_index("col")
    deep, tall = held[0].shape[2], held[0].shape[1]
    total[...] = jnp.zeros_like(total)
    for own_tags, ref in zip(tags, held):
        for index, (row_mask, col_mask) in enumerate(own_tags):
            j = jnp.bitwise_xor(lax.rem(col, cols // rows), col_mask)
            part = jnp.dot(ref[index], sub[aligned(j, deep), :], preferred_element_type=jnp.float32)
            at = aligned(jnp.bitwise_xor(row, row_mask), tall)
            total[at, :] = total[at, :] + part


def two_terms(x):
    high = x.astype(jnp.bfloat16)
    low = (x - high.astype(jnp.float32)).astype(jnp.bfloat16)
    return jnp.concatenate([high, low], 0)


def both(products):
    half = products.shape[0] // 2
    return products[:half] + products[half:]


def chain_kernel(cols, groups, slots, masks, first, last, offsets, start, *refs):
    held, (out, basis_all, factor_all) = refs[: len(masks)], refs[len(masks) :]
    mine = slice_index()
    pv, pt = basis_all.shape[1] // SLICES, factor_all.shape[1] // SLICES
    for slot, own_masks, ref in zip(slots, masks, held):
        to = slice(slot, slot + ref.shape[1])
        for index, mask in enumerate(own_masks):
            e = jnp.bitwise_xor(mine, mask)
            basis_all[to, aligned(e, pv), :] = ref[index, :, :pv, :]
            factor_all[to, aligned(e, pt), :] = ref[index, :, pv:, :]
    if first:
        n, each, width = start.shape
        pieces = start[...].reshape(n // cols, cols, each, width).sum(0)
        x = jnp.concatenate([pieces[c] for c in range(cols)], 1)
        x = jnp.concatenate([x] + [jnp.zeros_like(x)] * (8 // each - 1), 0)
    else:
        x = start[...]
    wide = x.shape[1]
    group_rows = basis_all.shape[1]
    before = jnp.int32(0)
    for slot, group in enumerate(groups):
        offset = offsets[group]
        x = pltpu.roll(x, lax.rem(before - offset + wide, wide), 1)
        before = offset
        block = x[:, :group_rows]
        weights = both(
            jnp.dot(two_terms(block), basis_all[slot], preferred_element_type=jnp.float32)
        )
        scaled = both(
            lax.dot_general(
                two_terms(weights), factor_all[slot], (((1,), (1,)), ((), ())),
                preferred_element_type=jnp.float32,
            )
        )
        change = both(
            lax.dot_general(
                two_terms(scaled), basis_all[slot], (((1,), (1,)), ((), ())),
                preferred_element_type=jnp.float32,
            )
        )
        x = jnp.concatenate([block - change, x[:, group_rows:]], 1)
    x = pltpu.roll(x, before, 1)
    if last:
        out[...] = x[: out.shape[0]].astype(out.dtype)
    else:
        out[...] = x


def local(rows, cols, sub_vectors, merge_factor, reflectors, wy_factors, owners, offsets):
    share = cols // rows
    halves = cols // HALF

    def over_col(x, mask):
        return lax.ppermute(x, "col", [(c, c ^ mask) for c in range(cols)])

    def over_row(x, mask):
        return lax.ppermute(x, "row", [(r, r ^ mask) for r in range(rows)])

    basis, factor = reflectors[0], wy_factors[0]
    group_rows, reflect = basis.shape
    dtype = basis.dtype
    pv, pt = group_rows // SLICES, reflect // SLICES
    piece = (pv + pt, reflect)

    packed = pl.pallas_call(
        pack_kernel,
        out_shape=jax.ShapeDtypeStruct((HALF,) + piece, dtype),
        in_specs=[HBM, HBM],
        out_specs=VMEM,
        scratch_shapes=[pltpu.SemaphoreType.DMA((2,))],
        compiler_params=limit(56),
        cost_estimate=cost([basis, factor]),
        name="pack",
    )(basis.reshape(SLICES, pv, reflect), factor.reshape(SLICES, pt, reflect))
    packed, merge_factor = lax.optimization_barrier((packed, merge_factor))
    members = [[h * HALF + c for c in range(HALF)] for h in range(halves)]
    slices = lax.all_to_all(packed, "col", 0, 0, axis_index_groups=members)

    picked = pl.pallas_call(
        pick_kernel,
        out_shape=jax.ShapeDtypeStruct((GROUPS - 1,) + piece, dtype),
        in_specs=[SMEM, VMEM],
        out_specs=VMEM,
        compiler_params=limit(4),
        cost_estimate=cost([slices]),
        name="pick",
    )(owners, slices)
    others = [over_col(picked, m * HALF) for m in range(1, halves)]

    across = [merge_factor] + [over_col(merge_factor, m * share) for m in range(1, rows)]

    row, top = lax.axis_index("row"), lax.axis_index("col") // share

    def for_row(mask):
        index = top ^ row ^ mask
        block = across[0]
        for k in range(1, rows):
            block = jnp.where(index == k, across[k], block)
        return block

    blocks = [for_row(0)] + [over_row(for_row(m), m) for m in range(1, rows)]
    others, blocks = lax.optimization_barrier((others, blocks))
    groups = [range(rows // 2), range(rows // 2, rows)]
    sides = [jnp.stack([blocks[m] for m in group]) for group in groups]
    tags = [[(m, 0) for m in group] for group in groups]

    def double(side, bit):
        sides[side] = jnp.concatenate([sides[side], over_col(sides[side], bit)])
        tags[side] = tags[side] + [(m, c ^ bit) for m, c in tags[side]]

    bit = share // 2
    while bit > 4:
        double(0, bit)
        double(1, bit)
        bit //= 2
    double(0, 2)
    double(1, 4)
    late = jnp.concatenate([over_col(sides[0], 4), over_col(sides[1], 2)])
    late_tags = [(m, c ^ 4) for m, c in tags[0]] + [(m, c ^ 2) for m, c in tags[1]]
    m_held = [jnp.concatenate(sides), late]
    tags = [tags[0] + tags[1], late_tags]
    m_held += [over_col(x, 1) for x in m_held]
    tags += [[(m, c ^ 1) for m, c in ts] for ts in tags]
    wanted, width = merge_factor.shape[0] * rows, sub_vectors.shape[1]
    each = wanted // (rows * cols)
    merged = pl.pallas_call(
        functools.partial(merge_kernel, rows, cols, tags),
        out_shape=jax.ShapeDtypeStruct((wanted, width), jnp.float32),
        in_specs=[VMEM] + [VMEM] * len(m_held),
        out_specs=VMEM,
        compiler_params=limit(8),
        cost_estimate=cost([sub_vectors], 2 * wanted * sub_vectors.size),
        name="merge",
    )(sub_vectors, *m_held)
    per = GROUPS // COLOURS
    colours = pl.pallas_call(
        order_kernel,
        out_shape=[jax.ShapeDtypeStruct((1, per) + piece, dtype)] * COLOURS,
        in_specs=[SMEM, VMEM] + [VMEM] * len(others),
        out_specs=[VMEM] * COLOURS,
        compiler_params=limit(4),
        cost_estimate=cost([slices]),
        name="order",
    )(owners, slices, *others)
    colours = list(colours)
    links = [
        (HALF, lambda v: over_row(v, 1)),
        (2, lambda v: over_col(v, 2)),
        (4, lambda v: over_col(v, 4)),
    ]
    masks = [[0] for _ in range(COLOURS)]
    for step in range(2):
        for k in range(COLOURS):
            mask, send = links[(k + step) % 3]
            colours[k] = jnp.concatenate([colours[k], send(colours[k])])
            masks[k] = masks[k] + [m ^ mask for m in masks[k]]
    state = lax.all_to_all(merged.reshape(rows * cols, each, width), ("row", "col"), 0, 0)
    last_round = []
    for k in range(COLOURS):
        mask, send = links[(k + 2) % 3]
        last_round.append(send(colours[k]))
        masks[k] = [masks[k], [m ^ mask for m in masks[k]]]
        masks[k] += [[m ^ 1 for m in ms] for ms in masks[k]]
    last_round, state = lax.optimization_barrier((last_round, state))
    held = []
    for k in range(COLOURS):
        held.append([colours[k], last_round[k], over_col(colours[k], 1), over_col(last_round[k], 1)])

    wide = cols * width
    for members in CHAINS:
        first, last = members[0] == 0, members[-1] == COLOURS - 1
        groups = range(members[0] * per, (members[-1] + 1) * per)
        arrays = [x for k in members for x in held[k]]
        slots = [per * i for i, k in enumerate(members) for _ in held[k]]
        state = pl.pallas_call(
            functools.partial(
                chain_kernel, cols, groups, slots, sum((masks[k] for k in members), []), first, last
            ),
            out_shape=jax.ShapeDtypeStruct(
                (each, wide) if last else (8, wide), jnp.bfloat16 if last else jnp.float32
            ),
            in_specs=[SMEM, VMEM] + [VMEM] * len(arrays),
            out_specs=VMEM,
            scratch_shapes=[
                pltpu.VMEM((len(groups), group_rows, reflect), dtype),
                pltpu.VMEM((len(groups), reflect, reflect), dtype),
            ],
            compiler_params=limit(12),
            cost_estimate=cost(arrays, 2 * len(groups) * 64 * group_rows * reflect),
            name=f"chain{members[0]}",
        )(offsets, state, *arrays)
    return state


def solution(mesh):
    rows, cols = mesh.shape["row"], mesh.shape["col"]
    in_specs = (
        P("row", "col"),
        P("row", "col"),
        P("col", None, None),
        P("col", None, None),
        P(),
        P(),
    )
    out_specs = P(("row", "col"), None)
    return jax.shard_map(
        functools.partial(local, rows, cols),
        mesh=mesh,
        in_specs=in_specs,
        out_specs=out_specs,
        check_vma=False,
    )
```

```python
import functools

import jax
import jax.numpy as jnp
from jax import lax
from jax.experimental import pallas as pl
from jax.experimental.pallas import tpu as pltpu
from jax.sharding import PartitionSpec as P

GROUPS = 6
COLOURS = 3
CHAINS = ((0,), (1, 2))
HALF = 8
SLICES = 2 * HALF
VMEM = pl.BlockSpec(memory_space=pltpu.VMEM)
SMEM = pl.BlockSpec(memory_space=pltpu.SMEM)
HBM = pl.BlockSpec(memory_space=pltpu.HBM)


def limit(mib):
    return pltpu.CompilerParams(vmem_limit_bytes=mib * 1024 * 1024)


def cost(arrays, flops=0):
    size = sum(a.size * a.dtype.itemsize for a in arrays)
    return pl.CostEstimate(flops=flops, bytes_accessed=size, transcendentals=0)


def slice_index():
    row, col = lax.axis_index("row"), lax.axis_index("col")
    return lax.rem(row, 2) * HALF + lax.rem(col, HALF)


def aligned(index, size):
    return pl.ds(pl.multiple_of(index * size, size), size)


def pack_kernel(basis, factor, out, sems):
    at = aligned(lax.rem(lax.axis_index("row"), 2), HALF)
    pv = basis.shape[1]
    copies = [
        pltpu.make_async_copy(basis.at[at], out.at[:, :pv, :], sems.at[0]),
        pltpu.make_async_copy(factor.at[at], out.at[:, pv:, :], sems.at[1]),
    ]
    for copy in copies:
        copy.start()
    for copy in copies:
        copy.wait()


def places(owners, group):
    half = owners[group] // HALF
    rank = jnp.int32(0)
    for before in range(group):
        rank = rank + (owners[before] // HALF == half).astype(jnp.int32)
    return half, rank


def pick_kernel(owners, held, out):
    mine = lax.axis_index("col") // HALF
    for group in range(GROUPS):
        half, rank = places(owners, group)
        rank = jnp.minimum(rank, out.shape[0] - 1)

        @pl.when(half == mine)
        def _():
            out[rank] = held[lax.rem(owners[group], HALF)]


def order_kernel(owners, held, *refs):
    others, outs = refs[:-COLOURS], refs[-COLOURS:]
    mine = lax.axis_index("col") // HALF
    each = GROUPS // COLOURS
    for group in range(GROUPS):
        half, rank = places(owners, group)
        piece = held[lax.rem(owners[group], HALF)]
        for mask, ref in enumerate(others, 1):
            other = ref[jnp.minimum(rank, ref.shape[0] - 1)]
            piece = jnp.where(jnp.bitwise_xor(half, mine) == mask, other, piece)
        outs[group // each][0, group % each] = piece


def merge_kernel(rows, cols, tags, sub, *refs):
    held, outs, total = refs[: -rows - 1], refs[-rows - 1 : -1], refs[-1]
    row, col = lax.axis_index("row"), lax.axis_index("col")
    deep, tall = held[0].shape[2], held[0].shape[1]
    total[...] = jnp.zeros_like(total)
    for own_tags, ref in zip(tags, held):
        for index, (row_mask, col_mask) in enumerate(own_tags):
            j = jnp.bitwise_xor(lax.rem(col, cols // rows), col_mask)
            part = jnp.dot(ref[index], sub[aligned(j, deep), :], preferred_element_type=jnp.float32)
            at = aligned(jnp.bitwise_xor(row, row_mask), tall)
            total[at, :] = total[at, :] + part
    for row_mask, out in enumerate(outs):
        out[...] = total[aligned(jnp.bitwise_xor(row, row_mask), tall), :]


def two_terms(x):
    high = x.astype(jnp.bfloat16)
    low = (x - high.astype(jnp.float32)).astype(jnp.bfloat16)
    return jnp.concatenate([high, low], 0)


def both(products):
    half = products.shape[0] // 2
    return products[:half] + products[half:]


def chain_kernel(cols, groups, slots, masks, first, last, offsets, start, *refs):
    held, (out, basis_all, factor_all) = refs[: len(masks)], refs[len(masks) :]
    mine = slice_index()
    pv, pt = basis_all.shape[1] // SLICES, factor_all.shape[1] // SLICES
    for slot, own_masks, ref in zip(slots, masks, held):
        to = slice(slot, slot + ref.shape[1])
        for index, mask in enumerate(own_masks):
            e = jnp.bitwise_xor(mine, mask)
            basis_all[to, aligned(e, pv), :] = ref[index, :, :pv, :]
            factor_all[to, aligned(e, pt), :] = ref[index, :, pv:, :]
    if first:
        pieces = start[...]
        each = pieces.shape[1]
        x = jnp.concatenate([pieces[c] for c in range(cols)], 1)
        x = jnp.concatenate([x] + [jnp.zeros_like(x)] * (8 // each - 1), 0)
    else:
        x = start[...]
    wide = x.shape[1]
    group_rows = basis_all.shape[1]
    before = jnp.int32(0)
    for slot, group in enumerate(groups):
        offset = offsets[group]
        x = pltpu.roll(x, lax.rem(before - offset + wide, wide), 1)
        before = offset
        block = x[:, :group_rows]
        weights = both(
            jnp.dot(two_terms(block), basis_all[slot], preferred_element_type=jnp.float32)
        )
        scaled = both(
            lax.dot_general(
                two_terms(weights), factor_all[slot], (((1,), (1,)), ((), ())),
                preferred_element_type=jnp.float32,
            )
        )
        change = both(
            lax.dot_general(
                two_terms(scaled), basis_all[slot], (((1,), (1,)), ((), ())),
                preferred_element_type=jnp.float32,
            )
        )
        x = jnp.concatenate([block - change, x[:, group_rows:]], 1)
    x = pltpu.roll(x, before, 1)
    if last:
        out[...] = x[: out.shape[0]].astype(out.dtype)
    else:
        out[...] = x


def local(rows, cols, sub_vectors, merge_factor, reflectors, wy_factors, owners, offsets):
    share = cols // rows
    halves = cols // HALF

    def over_col(x, mask):
        return lax.ppermute(x, "col", [(c, c ^ mask) for c in range(cols)])

    def over_row(x, mask):
        return lax.ppermute(x, "row", [(r, r ^ mask) for r in range(rows)])

    basis, factor = reflectors[0], wy_factors[0]
    group_rows, reflect = basis.shape
    dtype = basis.dtype
    pv, pt = group_rows // SLICES, reflect // SLICES
    piece = (pv + pt, reflect)

    packed = pl.pallas_call(
        pack_kernel,
        out_shape=jax.ShapeDtypeStruct((HALF,) + piece, dtype),
        in_specs=[HBM, HBM],
        out_specs=VMEM,
        scratch_shapes=[pltpu.SemaphoreType.DMA((2,))],
        compiler_params=limit(56),
        cost_estimate=cost([basis, factor]),
        name="pack",
    )(basis.reshape(SLICES, pv, reflect), factor.reshape(SLICES, pt, reflect))
    packed, merge_factor = lax.optimization_barrier((packed, merge_factor))
    members = [[h * HALF + c for c in range(HALF)] for h in range(halves)]
    slices = lax.all_to_all(packed, "col", 0, 0, axis_index_groups=members)

    picked = pl.pallas_call(
        pick_kernel,
        out_shape=jax.ShapeDtypeStruct((GROUPS - 1,) + piece, dtype),
        in_specs=[SMEM, VMEM],
        out_specs=VMEM,
        compiler_params=limit(4),
        cost_estimate=cost([slices]),
        name="pick",
    )(owners, slices)
    others = [over_col(picked, m * HALF) for m in range(1, halves)]

    across = [merge_factor] + [over_col(merge_factor, m * share) for m in range(1, rows)]

    row, top = lax.axis_index("row"), lax.axis_index("col") // share

    def for_row(mask):
        index = top ^ row ^ mask
        block = across[0]
        for k in range(1, rows):
            block = jnp.where(index == k, across[k], block)
        return block

    blocks = [for_row(0)] + [over_row(for_row(m), m) for m in range(1, rows)]
    others, blocks = lax.optimization_barrier((others, blocks))
    groups = [range(rows // 2), range(rows // 2, rows)]
    sides = [jnp.stack([blocks[m] for m in group]) for group in groups]
    tags = [[(m, 0) for m in group] for group in groups]

    def double(side, bit):
        sides[side] = jnp.concatenate([sides[side], over_col(sides[side], bit)])
        tags[side] = tags[side] + [(m, c ^ bit) for m, c in tags[side]]

    bit = share // 2
    while bit > 4:
        double(0, bit)
        double(1, bit)
        bit //= 2
    double(0, 2)
    double(1, 4)
    late = jnp.concatenate([over_col(sides[0], 4), over_col(sides[1], 2)])
    late_tags = [(m, c ^ 4) for m, c in tags[0]] + [(m, c ^ 2) for m, c in tags[1]]
    m_held = [jnp.concatenate(sides), late]
    tags = [tags[0] + tags[1], late_tags]
    m_held += [over_col(x, 1) for x in m_held]
    tags += [[(m, c ^ 1) for m, c in ts] for ts in tags]
    wanted, width = merge_factor.shape[0] * rows, sub_vectors.shape[1]
    each = wanted // (rows * cols)
    merged = pl.pallas_call(
        functools.partial(merge_kernel, rows, cols, tags),
        out_shape=[jax.ShapeDtypeStruct((wanted // rows, width), jnp.float32)] * rows,
        in_specs=[VMEM] + [VMEM] * len(m_held),
        out_specs=[VMEM] * rows,
        scratch_shapes=[pltpu.VMEM((wanted, width), jnp.float32)],
        compiler_params=limit(8),
        cost_estimate=cost([sub_vectors], 2 * wanted * sub_vectors.size),
        name="merge",
    )(sub_vectors, *m_held)
    per = GROUPS // COLOURS
    colours = pl.pallas_call(
        order_kernel,
        out_shape=[jax.ShapeDtypeStruct((1, per) + piece, dtype)] * COLOURS,
        in_specs=[SMEM, VMEM] + [VMEM] * len(others),
        out_specs=[VMEM] * COLOURS,
        compiler_params=limit(4),
        cost_estimate=cost([slices]),
        name="order",
    )(owners, slices, *others)
    colours = list(colours)
    links = [
        (HALF, lambda v: over_row(v, 1)),
        (2, lambda v: over_col(v, 2)),
        (4, lambda v: over_col(v, 4)),
    ]
    masks = [[0] for _ in range(COLOURS)]
    for step in range(2):
        for k in range(COLOURS):
            mask, send = links[(k + step) % 3]
            colours[k] = jnp.concatenate([colours[k], send(colours[k])])
            masks[k] = masks[k] + [m ^ mask for m in masks[k]]
    colours[-1], merged = lax.optimization_barrier((colours[-1], list(merged)))
    merged = merged[0] + sum(over_row(merged[m], m) for m in range(1, rows))
    state = lax.all_to_all(merged.reshape(cols, each, width), "col", 0, 0)
    last_round = []
    for k in range(COLOURS):
        mask, send = links[(k + 2) % 3]
        last_round.append(send(colours[k]))
        masks[k] = [masks[k], [m ^ mask for m in masks[k]]]
        masks[k] += [[m ^ 1 for m in ms] for ms in masks[k]]
    last_round, state = lax.optimization_barrier((last_round, state))
    held = []
    for k in range(COLOURS):
        held.append([colours[k], last_round[k], over_col(colours[k], 1), over_col(last_round[k], 1)])

    wide = cols * width
    for members in CHAINS:
        first, last = members[0] == 0, members[-1] == COLOURS - 1
        groups = range(members[0] * per, (members[-1] + 1) * per)
        arrays = [x for k in members for x in held[k]]
        slots = [per * i for i, k in enumerate(members) for _ in held[k]]
        state = pl.pallas_call(
            functools.partial(
                chain_kernel, cols, groups, slots, sum((masks[k] for k in members), []), first, last
            ),
            out_shape=jax.ShapeDtypeStruct(
                (each, wide) if last else (8, wide), jnp.bfloat16 if last else jnp.float32
            ),
            in_specs=[SMEM, VMEM] + [VMEM] * len(arrays),
            out_specs=VMEM,
            scratch_shapes=[
                pltpu.VMEM((len(groups), group_rows, reflect), dtype),
                pltpu.VMEM((len(groups), reflect, reflect), dtype),
            ],
            compiler_params=limit(12),
            cost_estimate=cost(arrays, 2 * len(groups) * 64 * group_rows * reflect),
            name=f"chain{members[0]}",
        )(offsets, state, *arrays)
    return state


def solution(mesh):
    rows, cols = mesh.shape["row"], mesh.shape["col"]
    in_specs = (
        P("row", "col"),
        P("row", "col"),
        P("col", None, None),
        P("col", None, None),
        P(),
        P(),
    )
    out_specs = P(("row", "col"), None)
    return jax.shard_map(
        functools.partial(local, rows, cols),
        mesh=mesh,
        in_specs=in_specs,
        out_specs=out_specs,
        check_vma=False,
    )
```

```python
import functools

import jax
import jax.numpy as jnp
from jax import lax
from jax.experimental import pallas as pl
from jax.experimental.pallas import tpu as pltpu
from jax.sharding import PartitionSpec as P

GROUPS = 6
COLOURS = 3
CHAINS = ((0,), (1, 2))
HALF = 8
SLICES = 2 * HALF
VMEM = pl.BlockSpec(memory_space=pltpu.VMEM)
SMEM = pl.BlockSpec(memory_space=pltpu.SMEM)
HBM = pl.BlockSpec(memory_space=pltpu.HBM)


def limit(mib):
    return pltpu.CompilerParams(vmem_limit_bytes=mib * 1024 * 1024)


def cost(arrays, flops=0):
    size = sum(a.size * a.dtype.itemsize for a in arrays)
    return pl.CostEstimate(flops=flops, bytes_accessed=size, transcendentals=0)


def slice_index():
    row, col = lax.axis_index("row"), lax.axis_index("col")
    return lax.rem(row, 2) * HALF + lax.rem(col, HALF)


def aligned(index, size):
    return pl.ds(pl.multiple_of(index * size, size), size)


def pack_kernel(basis, factor, out, sems):
    at = aligned(lax.rem(lax.axis_index("row"), 2), HALF)
    pv = basis.shape[1]
    copies = [
        pltpu.make_async_copy(basis.at[at], out.at[:, :pv, :], sems.at[0]),
        pltpu.make_async_copy(factor.at[at], out.at[:, pv:, :], sems.at[1]),
    ]
    for copy in copies:
        copy.start()
    for copy in copies:
        copy.wait()


def places(owners, group):
    half = owners[group] // HALF
    rank = jnp.int32(0)
    for before in range(group):
        rank = rank + (owners[before] // HALF == half).astype(jnp.int32)
    return half, rank


def pick_kernel(owners, held, out):
    mine = lax.axis_index("col") // HALF
    for group in range(GROUPS):
        half, rank = places(owners, group)
        rank = jnp.minimum(rank, out.shape[1] - 1)

        @pl.when(half == mine)
        def _():
            piece = held[lax.rem(owners[group], HALF)]
            for to in range(out.shape[0]):
                out[to, rank] = piece


def order_kernel(owners, held, *outs):
    each = GROUPS // COLOURS
    for group in range(GROUPS):
        half, rank = places(owners, group)
        rank = jnp.minimum(rank, held.shape[1] - 1)
        outs[group // each][0, group % each] = held[half, rank]


def merge_kernel(rows, cols, tags, sub, *refs):
    held, total = refs[:-1], refs[-1]
    row, col = lax.axis_index("row"), lax.axis_index("col")
    deep, tall = held[0].shape[2], held[0].shape[1]
    total[...] = jnp.zeros_like(total)
    for own_tags, ref in zip(tags, held):
        for index, (row_mask, col_mask) in enumerate(own_tags):
            j = jnp.bitwise_xor(lax.rem(col, cols // rows), col_mask)
            part = jnp.dot(ref[index], sub[aligned(j, deep), :], preferred_element_type=jnp.float32)
            at = aligned(jnp.bitwise_xor(row, row_mask), tall)
            total[at, :] = total[at, :] + part


def two_terms(x):
    high = x.astype(jnp.bfloat16)
    low = (x - high.astype(jnp.float32)).astype(jnp.bfloat16)
    return jnp.concatenate([high, low], 0)


def both(products):
    half = products.shape[0] // 2
    return products[:half] + products[half:]


def chain_kernel(cols, groups, slots, masks, first, last, offsets, start, *refs):
    held, (out, basis_all, factor_all) = refs[: len(masks)], refs[len(masks) :]
    mine = slice_index()
    pv, pt = basis_all.shape[1] // SLICES, factor_all.shape[1] // SLICES
    for slot, own_masks, ref in zip(slots, masks, held):
        to = slice(slot, slot + ref.shape[1])
        for index, mask in enumerate(own_masks):
            e = jnp.bitwise_xor(mine, mask)
            basis_all[to, aligned(e, pv), :] = ref[index, :, :pv, :]
            factor_all[to, aligned(e, pt), :] = ref[index, :, pv:, :]
    if first:
        n, each, width = start.shape
        pieces = start[...].reshape(n // cols, cols, each, width).sum(0)
        x = jnp.concatenate([pieces[c] for c in range(cols)], 1)
        x = jnp.concatenate([x] + [jnp.zeros_like(x)] * (8 // each - 1), 0)
    else:
        x = start[...]
    wide = x.shape[1]
    group_rows = basis_all.shape[1]
    before = jnp.int32(0)
    for slot, group in enumerate(groups):
        offset = offsets[group]
        x = pltpu.roll(x, lax.rem(before - offset + wide, wide), 1)
        before = offset
        block = x[:, :group_rows]
        weights = both(
            jnp.dot(two_terms(block), basis_all[slot], preferred_element_type=jnp.float32)
        )
        scaled = both(
            lax.dot_general(
                two_terms(weights), factor_all[slot], (((1,), (1,)), ((), ())),
                preferred_element_type=jnp.float32,
            )
        )
        change = both(
            lax.dot_general(
                two_terms(scaled), basis_all[slot], (((1,), (1,)), ((), ())),
                preferred_element_type=jnp.float32,
            )
        )
        x = jnp.concatenate([block - change, x[:, group_rows:]], 1)
    x = pltpu.roll(x, before, 1)
    if last:
        out[...] = x[: out.shape[0]].astype(out.dtype)
    else:
        out[...] = x


def local(rows, cols, sub_vectors, merge_factor, reflectors, wy_factors, owners, offsets):
    share = cols // rows
    halves = cols // HALF

    def over_col(x, mask):
        return lax.ppermute(x, "col", [(c, c ^ mask) for c in range(cols)])

    def over_row(x, mask):
        return lax.ppermute(x, "row", [(r, r ^ mask) for r in range(rows)])

    basis, factor = reflectors[0], wy_factors[0]
    group_rows, reflect = basis.shape
    dtype = basis.dtype
    pv, pt = group_rows // SLICES, reflect // SLICES
    piece = (pv + pt, reflect)

    packed = pl.pallas_call(
        pack_kernel,
        out_shape=jax.ShapeDtypeStruct((HALF,) + piece, dtype),
        in_specs=[HBM, HBM],
        out_specs=VMEM,
        scratch_shapes=[pltpu.SemaphoreType.DMA((2,))],
        compiler_params=limit(56),
        cost_estimate=cost([basis, factor]),
        name="pack",
    )(basis.reshape(SLICES, pv, reflect), factor.reshape(SLICES, pt, reflect))
    packed, merge_factor = lax.optimization_barrier((packed, merge_factor))
    members = [[h * HALF + c for c in range(HALF)] for h in range(halves)]
    slices = lax.all_to_all(packed, "col", 0, 0, axis_index_groups=members)

    picked = pl.pallas_call(
        pick_kernel,
        out_shape=jax.ShapeDtypeStruct((halves, GROUPS - 1) + piece, dtype),
        in_specs=[SMEM, VMEM],
        out_specs=VMEM,
        compiler_params=limit(4),
        cost_estimate=cost([slices]),
        name="pick",
    )(owners, slices)
    members = [[h * HALF + c for h in range(halves)] for c in range(HALF)]
    gathered = lax.all_to_all(picked, "col", 0, 0, axis_index_groups=members)

    across = [merge_factor] + [over_col(merge_factor, m * share) for m in range(1, rows)]

    row, top = lax.axis_index("row"), lax.axis_index("col") // share

    def for_row(mask):
        index = top ^ row ^ mask
        block = across[0]
        for k in range(1, rows):
            block = jnp.where(index == k, across[k], block)
        return block

    blocks = [for_row(0)] + [over_row(for_row(m), m) for m in range(1, rows)]
    groups = [range(rows // 2), range(rows // 2, rows)]
    sides = [jnp.stack([blocks[m] for m in group]) for group in groups]
    tags = [[(m, 0) for m in group] for group in groups]

    def double(side, bit):
        sides[side] = jnp.concatenate([sides[side], over_col(sides[side], bit)])
        tags[side] = tags[side] + [(m, c ^ bit) for m, c in tags[side]]

    bit = share // 2
    while bit > 4:
        double(0, bit)
        double(1, bit)
        bit //= 2
    double(0, 2)
    double(1, 4)
    late = jnp.concatenate([over_col(sides[0], 4), over_col(sides[1], 2)])
    late_tags = [(m, c ^ 4) for m, c in tags[0]] + [(m, c ^ 2) for m, c in tags[1]]
    m_held = [jnp.concatenate(sides), late]
    tags = [tags[0] + tags[1], late_tags]
    m_held += [over_col(x, 1) for x in m_held]
    tags += [[(m, c ^ 1) for m, c in ts] for ts in tags]
    wanted, width = merge_factor.shape[0] * rows, sub_vectors.shape[1]
    each = wanted // (rows * cols)
    merged = pl.pallas_call(
        functools.partial(merge_kernel, rows, cols, tags),
        out_shape=jax.ShapeDtypeStruct((wanted, width), jnp.float32),
        in_specs=[VMEM] + [VMEM] * len(m_held),
        out_specs=VMEM,
        compiler_params=limit(8),
        cost_estimate=cost([sub_vectors], 2 * wanted * sub_vectors.size),
        name="merge",
    )(sub_vectors, *m_held)
    per = GROUPS // COLOURS
    colours = pl.pallas_call(
        order_kernel,
        out_shape=[jax.ShapeDtypeStruct((1, per) + piece, dtype)] * COLOURS,
        in_specs=[SMEM, VMEM],
        out_specs=[VMEM] * COLOURS,
        compiler_params=limit(4),
        cost_estimate=cost([slices]),
        name="order",
    )(owners, gathered)
    colours = list(colours)
    links = [
        (HALF, lambda v: over_row(v, 1)),
        (2, lambda v: over_col(v, 2)),
        (4, lambda v: over_col(v, 4)),
    ]
    masks = [[0] for _ in range(COLOURS)]
    for step in range(2):
        for k in range(COLOURS):
            mask, send = links[(k + step) % 3]
            colours[k] = jnp.concatenate([colours[k], send(colours[k])])
            masks[k] = masks[k] + [m ^ mask for m in masks[k]]
    state = lax.all_to_all(merged.reshape(rows * cols, each, width), ("row", "col"), 0, 0)
    colours, state = lax.optimization_barrier((colours, state))
    last_round = []
    for k in range(COLOURS):
        mask, send = links[(k + 2) % 3]
        last_round.append(send(colours[k]))
        masks[k] = [masks[k], [m ^ mask for m in masks[k]]]
        masks[k] += [[m ^ 1 for m in ms] for ms in masks[k]]
    held = []
    for k in range(COLOURS):
        held.append([colours[k], last_round[k], over_col(colours[k], 1), over_col(last_round[k], 1)])

    wide = cols * width
    for members in CHAINS:
        first, last = members[0] == 0, members[-1] == COLOURS - 1
        groups = range(members[0] * per, (members[-1] + 1) * per)
        arrays = [x for k in members for x in held[k]]
        slots = [per * i for i, k in enumerate(members) for _ in held[k]]
        state = pl.pallas_call(
            functools.partial(
                chain_kernel, cols, groups, slots, sum((masks[k] for k in members), []), first, last
            ),
            out_shape=jax.ShapeDtypeStruct(
                (each, wide) if last else (8, wide), jnp.bfloat16 if last else jnp.float32
            ),
            in_specs=[SMEM, VMEM] + [VMEM] * len(arrays),
            out_specs=VMEM,
            scratch_shapes=[
                pltpu.VMEM((len(groups), group_rows, reflect), dtype),
                pltpu.VMEM((len(groups), reflect, reflect), dtype),
            ],
            compiler_params=limit(12),
            cost_estimate=cost(arrays, 2 * len(groups) * 64 * group_rows * reflect),
            name=f"chain{members[0]}",
        )(offsets, state, *arrays)
    return state


def solution(mesh):
    rows, cols = mesh.shape["row"], mesh.shape["col"]
    in_specs = (
        P("row", "col"),
        P("row", "col"),
        P("col", None, None),
        P("col", None, None),
        P(),
        P(),
    )
    out_specs = P(("row", "col"), None)
    return jax.shard_map(
        functools.partial(local, rows, cols),
        mesh=mesh,
        in_specs=in_specs,
        out_specs=out_specs,
        check_vma=False,
    )
```

```python
import functools

import jax
import jax.numpy as jnp
from jax import lax
from jax.experimental import pallas as pl
from jax.experimental.pallas import tpu as pltpu
from jax.sharding import PartitionSpec as P

GROUPS = 6
COLOURS = 3
HALF = 8
SLICES = 2 * HALF
VMEM = pl.BlockSpec(memory_space=pltpu.VMEM)
SMEM = pl.BlockSpec(memory_space=pltpu.SMEM)
HBM = pl.BlockSpec(memory_space=pltpu.HBM)


def limit(mib):
    return pltpu.CompilerParams(vmem_limit_bytes=mib * 1024 * 1024)


def cost(arrays, flops=0):
    size = sum(a.size * a.dtype.itemsize for a in arrays)
    return pl.CostEstimate(flops=flops, bytes_accessed=size, transcendentals=0)


def slice_index():
    row, col = lax.axis_index("row"), lax.axis_index("col")
    return lax.rem(row, 2) * HALF + lax.rem(col, HALF)


def aligned(index, size):
    return pl.ds(pl.multiple_of(index * size, size), size)


def pack_kernel(basis, factor, out, sems):
    at = aligned(lax.rem(lax.axis_index("row"), 2), HALF)
    pv = basis.shape[1]
    copies = [
        pltpu.make_async_copy(basis.at[at], out.at[:, :pv, :], sems.at[0]),
        pltpu.make_async_copy(factor.at[at], out.at[:, pv:, :], sems.at[1]),
    ]
    for copy in copies:
        copy.start()
    for copy in copies:
        copy.wait()


def places(owners, group):
    half = owners[group] // HALF
    rank = jnp.int32(0)
    for before in range(group):
        rank = rank + (owners[before] // HALF == half).astype(jnp.int32)
    return half, rank


def pick_kernel(owners, held, out):
    mine = lax.axis_index("col") // HALF
    for group in range(GROUPS):
        half, rank = places(owners, group)
        rank = jnp.minimum(rank, out.shape[0] - 1)

        @pl.when(half == mine)
        def _():
            out[rank] = held[lax.rem(owners[group], HALF)]


def order_kernel(owners, held, *refs):
    others, outs = refs[:-COLOURS], refs[-COLOURS:]
    mine = lax.axis_index("col") // HALF
    each = GROUPS // COLOURS
    for group in range(GROUPS):
        half, rank = places(owners, group)
        piece = held[lax.rem(owners[group], HALF)]
        for mask, ref in enumerate(others, 1):
            other = ref[jnp.minimum(rank, ref.shape[0] - 1)]
            piece = jnp.where(jnp.bitwise_xor(half, mine) == mask, other, piece)
        outs[group // each][0, group % each] = piece


def merge_kernel(rows, cols, tags, sub, *refs):
    held, total = refs[:-1], refs[-1]
    row, col = lax.axis_index("row"), lax.axis_index("col")
    deep, tall = held[0].shape[2], held[0].shape[1]
    total[...] = jnp.zeros_like(total)
    for own_tags, ref in zip(tags, held):
        for index, (row_mask, col_mask) in enumerate(own_tags):
            j = jnp.bitwise_xor(lax.rem(col, cols // rows), col_mask)
            part = jnp.dot(ref[index], sub[aligned(j, deep), :], preferred_element_type=jnp.float32)
            at = aligned(jnp.bitwise_xor(row, row_mask), tall)
            total[at, :] = total[at, :] + part


def two_terms(x):
    high = x.astype(jnp.bfloat16)
    low = (x - high.astype(jnp.float32)).astype(jnp.bfloat16)
    return jnp.concatenate([high, low], 0)


def both(products):
    half = products.shape[0] // 2
    return products[:half] + products[half:]


def assemble_kernel(masks, *refs):
    held, (basis, factor) = refs[:-2], refs[-2:]
    mine = slice_index()
    pv, pt = basis.shape[1] // SLICES, factor.shape[1] // SLICES
    for own_masks, ref in zip(masks, held):
        for index, mask in enumerate(own_masks):
            at = jnp.bitwise_xor(mine, mask)
            basis[:, aligned(at, pv), :] = ref[index, :, :pv, :]
            factor[:, aligned(at, pt), :] = ref[index, :, pv:, :]


def chain_kernel(cols, offsets, start, *refs):
    bases, factors, out = refs[:COLOURS], refs[COLOURS:-1], refs[-1]
    n, each, width = start.shape
    pieces = start[...].reshape(n // cols, cols, each, width).sum(0)
    x = jnp.concatenate([pieces[c] for c in range(cols)], 1)
    x = jnp.concatenate([x] + [jnp.zeros_like(x)] * (8 // each - 1), 0)
    wide = x.shape[1]
    group_rows = bases[0].shape[1]
    before = jnp.int32(0)
    per = GROUPS // COLOURS
    for group in range(GROUPS):
        basis, factor = bases[group // per][group % per], factors[group // per][group % per]
        offset = offsets[group]
        x = pltpu.roll(x, lax.rem(before - offset + wide, wide), 1)
        before = offset
        block = x[:, :group_rows]
        weights = both(
            jnp.dot(two_terms(block), basis, preferred_element_type=jnp.float32)
        )
        scaled = both(
            lax.dot_general(
                two_terms(weights), factor, (((1,), (1,)), ((), ())),
                preferred_element_type=jnp.float32,
            )
        )
        change = both(
            lax.dot_general(
                two_terms(scaled), basis, (((1,), (1,)), ((), ())),
                preferred_element_type=jnp.float32,
            )
        )
        x = jnp.concatenate([block - change, x[:, group_rows:]], 1)
    x = pltpu.roll(x, before, 1)
    out[...] = x[: out.shape[0]].astype(out.dtype)


def local(rows, cols, sub_vectors, merge_factor, reflectors, wy_factors, owners, offsets):
    share = cols // rows
    halves = cols // HALF

    def over_col(x, mask):
        return lax.ppermute(x, "col", [(c, c ^ mask) for c in range(cols)])

    def over_row(x, mask):
        return lax.ppermute(x, "row", [(r, r ^ mask) for r in range(rows)])

    basis, factor = reflectors[0], wy_factors[0]
    group_rows, reflect = basis.shape
    dtype = basis.dtype
    pv, pt = group_rows // SLICES, reflect // SLICES
    piece = (pv + pt, reflect)

    packed = pl.pallas_call(
        pack_kernel,
        out_shape=jax.ShapeDtypeStruct((HALF,) + piece, dtype),
        in_specs=[HBM, HBM],
        out_specs=VMEM,
        scratch_shapes=[pltpu.SemaphoreType.DMA((2,))],
        compiler_params=limit(56),
        cost_estimate=cost([basis, factor]),
        name="pack",
    )(basis.reshape(SLICES, pv, reflect), factor.reshape(SLICES, pt, reflect))
    packed, merge_factor = lax.optimization_barrier((packed, merge_factor))
    members = [[h * HALF + c for c in range(HALF)] for h in range(halves)]
    slices = lax.all_to_all(packed, "col", 0, 0, axis_index_groups=members)

    picked = pl.pallas_call(
        pick_kernel,
        out_shape=jax.ShapeDtypeStruct((GROUPS - 1,) + piece, dtype),
        in_specs=[SMEM, VMEM],
        out_specs=VMEM,
        compiler_params=limit(4),
        cost_estimate=cost([slices]),
        name="pick",
    )(owners, slices)
    others = [over_col(picked, m * HALF) for m in range(1, halves)]

    across = [merge_factor] + [over_col(merge_factor, m * share) for m in range(1, rows)]

    row, top = lax.axis_index("row"), lax.axis_index("col") // share

    def for_row(mask):
        index = top ^ row ^ mask
        block = across[0]
        for k in range(1, rows):
            block = jnp.where(index == k, across[k], block)
        return block

    blocks = [for_row(0)] + [over_row(for_row(m), m) for m in range(1, rows)]
    others, blocks = lax.optimization_barrier((others, blocks))
    groups = [range(rows // 2), range(rows // 2, rows)]
    sides = [jnp.stack([blocks[m] for m in group]) for group in groups]
    tags = [[(m, 0) for m in group] for group in groups]

    def double(side, bit):
        sides[side] = jnp.concatenate([sides[side], over_col(sides[side], bit)])
        tags[side] = tags[side] + [(m, c ^ bit) for m, c in tags[side]]

    bit = share // 2
    while bit > 4:
        double(0, bit)
        double(1, bit)
        bit //= 2
    double(0, 2)
    double(1, 4)
    late = jnp.concatenate([over_col(sides[0], 4), over_col(sides[1], 2)])
    late_tags = [(m, c ^ 4) for m, c in tags[0]] + [(m, c ^ 2) for m, c in tags[1]]
    m_held = [jnp.concatenate(sides), late]
    tags = [tags[0] + tags[1], late_tags]
    m_held += [over_col(x, 1) for x in m_held]
    tags += [[(m, c ^ 1) for m, c in ts] for ts in tags]
    wanted, width = merge_factor.shape[0] * rows, sub_vectors.shape[1]
    each = wanted // (rows * cols)
    merged = pl.pallas_call(
        functools.partial(merge_kernel, rows, cols, tags),
        out_shape=jax.ShapeDtypeStruct((wanted, width), jnp.float32),
        in_specs=[VMEM] + [VMEM] * len(m_held),
        out_specs=VMEM,
        compiler_params=limit(8),
        cost_estimate=cost([sub_vectors], 2 * wanted * sub_vectors.size),
        name="merge",
    )(sub_vectors, *m_held)
    per = GROUPS // COLOURS
    colours = pl.pallas_call(
        order_kernel,
        out_shape=[jax.ShapeDtypeStruct((1, per) + piece, dtype)] * COLOURS,
        in_specs=[SMEM, VMEM] + [VMEM] * len(others),
        out_specs=[VMEM] * COLOURS,
        compiler_params=limit(4),
        cost_estimate=cost([slices]),
        name="order",
    )(owners, slices, *others)
    colours = list(colours)
    links = [
        (HALF, lambda v: over_row(v, 1)),
        (2, lambda v: over_col(v, 2)),
        (4, lambda v: over_col(v, 4)),
    ]
    masks = [[0] for _ in range(COLOURS)]
    for step in range(2):
        for k in range(COLOURS):
            mask, send = links[(k + step) % 3]
            colours[k] = jnp.concatenate([colours[k], send(colours[k])])
            masks[k] = masks[k] + [m ^ mask for m in masks[k]]
    state = lax.all_to_all(merged.reshape(rows * cols, each, width), ("row", "col"), 0, 0)
    last_round = []
    for k in range(COLOURS):
        mask, send = links[(k + 2) % 3]
        last_round.append(send(colours[k]))
        masks[k] = [masks[k], [m ^ mask for m in masks[k]]]
        masks[k] += [[m ^ 1 for m in ms] for ms in masks[k]]
    bases, factors = [], []
    for k in range(COLOURS):
        held = [colours[k], last_round[k], over_col(colours[k], 1), over_col(last_round[k], 1)]
        whole = pl.pallas_call(
            functools.partial(assemble_kernel, masks[k]),
            out_shape=[
                jax.ShapeDtypeStruct((per, group_rows, reflect), dtype),
                jax.ShapeDtypeStruct((per, reflect, reflect), dtype),
            ],
            in_specs=[VMEM] * len(held),
            out_specs=[VMEM, VMEM],
            compiler_params=limit(4),
            cost_estimate=cost(held),
            name="assemble",
        )(*held)
        bases.append(whole[0])
        factors.append(whole[1])
    return pl.pallas_call(
        functools.partial(chain_kernel, cols),
        out_shape=jax.ShapeDtypeStruct((each, cols * width), jnp.bfloat16),
        in_specs=[SMEM, VMEM] + [VMEM] * (2 * COLOURS),
        out_specs=VMEM,
        compiler_params=limit(4),
        cost_estimate=cost(bases, 2 * GROUPS * 64 * group_rows * reflect),
        name="chain",
    )(offsets, state, *bases, *factors)


def solution(mesh):
    rows, cols = mesh.shape["row"], mesh.shape["col"]
    in_specs = (
        P("row", "col"),
        P("row", "col"),
        P("col", None, None),
        P("col", None, None),
        P(),
        P(),
    )
    out_specs = P(("row", "col"), None)
    return jax.shard_map(
        functools.partial(local, rows, cols),
        mesh=mesh,
        in_specs=in_specs,
        out_specs=out_specs,
        check_vma=False,
    )
```

```python
import functools

import jax
import jax.numpy as jnp
from jax import lax
from jax.experimental import pallas as pl
from jax.experimental.pallas import tpu as pltpu
from jax.sharding import PartitionSpec as P

GROUPS = 6
COLOURS = 3
CHAINS = ((0, 1, 2),)
HALF = 8
SLICES = 2 * HALF
VMEM = pl.BlockSpec(memory_space=pltpu.VMEM)
SMEM = pl.BlockSpec(memory_space=pltpu.SMEM)
HBM = pl.BlockSpec(memory_space=pltpu.HBM)


def limit(mib):
    return pltpu.CompilerParams(vmem_limit_bytes=mib * 1024 * 1024)


def cost(arrays, flops=0):
    size = sum(a.size * a.dtype.itemsize for a in arrays)
    return pl.CostEstimate(flops=flops, bytes_accessed=size, transcendentals=0)


def slice_index():
    row, col = lax.axis_index("row"), lax.axis_index("col")
    return lax.rem(row, 2) * HALF + lax.rem(col, HALF)


def aligned(index, size):
    return pl.ds(pl.multiple_of(index * size, size), size)


def pack_kernel(basis, factor, out, sems):
    at = aligned(lax.rem(lax.axis_index("row"), 2), HALF)
    pv = basis.shape[1]
    copies = [
        pltpu.make_async_copy(basis.at[at], out.at[:, :pv, :], sems.at[0]),
        pltpu.make_async_copy(factor.at[at], out.at[:, pv:, :], sems.at[1]),
    ]
    for copy in copies:
        copy.start()
    for copy in copies:
        copy.wait()


def places(owners, group):
    half = owners[group] // HALF
    rank = jnp.int32(0)
    for before in range(group):
        rank = rank + (owners[before] // HALF == half).astype(jnp.int32)
    return half, rank


def pick_kernel(owners, held, out):
    mine = lax.axis_index("col") // HALF
    for group in range(GROUPS):
        half, rank = places(owners, group)
        rank = jnp.minimum(rank, out.shape[0] - 1)

        @pl.when(half == mine)
        def _():
            out[rank] = held[lax.rem(owners[group], HALF)]


def order_kernel(owners, held, *refs):
    others, outs = refs[:-COLOURS], refs[-COLOURS:]
    mine = lax.axis_index("col") // HALF
    each = GROUPS // COLOURS
    for group in range(GROUPS):
        half, rank = places(owners, group)
        piece = held[lax.rem(owners[group], HALF)]
        for mask, ref in enumerate(others, 1):
            other = ref[jnp.minimum(rank, ref.shape[0] - 1)]
            piece = jnp.where(jnp.bitwise_xor(half, mine) == mask, other, piece)
        outs[group // each][0, group % each] = piece


def merge_kernel(rows, cols, tags, sub, *refs):
    held, total = refs[:-1], refs[-1]
    row, col = lax.axis_index("row"), lax.axis_index("col")
    deep, tall = held[0].shape[2], held[0].shape[1]
    total[...] = jnp.zeros_like(total)
    for own_tags, ref in zip(tags, held):
        for index, (row_mask, col_mask) in enumerate(own_tags):
            j = jnp.bitwise_xor(lax.rem(col, cols // rows), col_mask)
            part = jnp.dot(ref[index], sub[aligned(j, deep), :], preferred_element_type=jnp.float32)
            at = aligned(jnp.bitwise_xor(row, row_mask), tall)
            total[at, :] = total[at, :] + part


def two_terms(x):
    high = x.astype(jnp.bfloat16)
    low = (x - high.astype(jnp.float32)).astype(jnp.bfloat16)
    return jnp.concatenate([high, low], 0)


def both(products):
    half = products.shape[0] // 2
    return products[:half] + products[half:]


def chain_kernel(cols, groups, slots, masks, first, last, offsets, start, *refs):
    held, (out, basis_all, factor_all) = refs[: len(masks)], refs[len(masks) :]
    mine = slice_index()
    pv, pt = basis_all.shape[1] // SLICES, factor_all.shape[1] // SLICES
    for slot, own_masks, ref in zip(slots, masks, held):
        to = slice(slot, slot + ref.shape[1])
        for index, mask in enumerate(own_masks):
            e = jnp.bitwise_xor(mine, mask)
            basis_all[to, aligned(e, pv), :] = ref[index, :, :pv, :]
            factor_all[to, aligned(e, pt), :] = ref[index, :, pv:, :]
    if first:
        n, each, width = start.shape
        pieces = start[...].reshape(n // cols, cols, each, width).sum(0)
        x = jnp.concatenate([pieces[c] for c in range(cols)], 1)
        x = jnp.concatenate([x] + [jnp.zeros_like(x)] * (8 // each - 1), 0)
    else:
        x = start[...]
    wide = x.shape[1]
    group_rows = basis_all.shape[1]
    before = jnp.int32(0)
    for slot, group in enumerate(groups):
        offset = offsets[group]
        x = pltpu.roll(x, lax.rem(before - offset + wide, wide), 1)
        before = offset
        block = x[:, :group_rows]
        weights = both(
            jnp.dot(two_terms(block), basis_all[slot], preferred_element_type=jnp.float32)
        )
        scaled = both(
            lax.dot_general(
                two_terms(weights), factor_all[slot], (((1,), (1,)), ((), ())),
                preferred_element_type=jnp.float32,
            )
        )
        change = both(
            lax.dot_general(
                two_terms(scaled), basis_all[slot], (((1,), (1,)), ((), ())),
                preferred_element_type=jnp.float32,
            )
        )
        x = jnp.concatenate([block - change, x[:, group_rows:]], 1)
    x = pltpu.roll(x, before, 1)
    if last:
        out[...] = x[: out.shape[0]].astype(out.dtype)
    else:
        out[...] = x


def local(rows, cols, sub_vectors, merge_factor, reflectors, wy_factors, owners, offsets):
    share = cols // rows
    halves = cols // HALF

    def over_col(x, mask):
        return lax.ppermute(x, "col", [(c, c ^ mask) for c in range(cols)])

    def over_row(x, mask):
        return lax.ppermute(x, "row", [(r, r ^ mask) for r in range(rows)])

    basis, factor = reflectors[0], wy_factors[0]
    group_rows, reflect = basis.shape
    dtype = basis.dtype
    pv, pt = group_rows // SLICES, reflect // SLICES
    piece = (pv + pt, reflect)

    packed = pl.pallas_call(
        pack_kernel,
        out_shape=jax.ShapeDtypeStruct((HALF,) + piece, dtype),
        in_specs=[HBM, HBM],
        out_specs=VMEM,
        scratch_shapes=[pltpu.SemaphoreType.DMA((2,))],
        compiler_params=limit(56),
        cost_estimate=cost([basis, factor]),
        name="pack",
    )(basis.reshape(SLICES, pv, reflect), factor.reshape(SLICES, pt, reflect))
    packed, merge_factor = lax.optimization_barrier((packed, merge_factor))
    members = [[h * HALF + c for c in range(HALF)] for h in range(halves)]
    slices = lax.all_to_all(packed, "col", 0, 0, axis_index_groups=members)

    picked = pl.pallas_call(
        pick_kernel,
        out_shape=jax.ShapeDtypeStruct((GROUPS - 1,) + piece, dtype),
        in_specs=[SMEM, VMEM],
        out_specs=VMEM,
        compiler_params=limit(4),
        cost_estimate=cost([slices]),
        name="pick",
    )(owners, slices)

    across = [merge_factor] + [over_col(merge_factor, m * share) for m in range(1, rows)]

    row, top = lax.axis_index("row"), lax.axis_index("col") // share

    def for_row(mask):
        index = top ^ row ^ mask
        block = across[0]
        for k in range(1, rows):
            block = jnp.where(index == k, across[k], block)
        return block

    blocks = [for_row(0)] + [over_row(for_row(m), m) for m in range(1, rows)]
    picked, blocks = lax.optimization_barrier((picked, blocks))
    others = [over_col(picked, m * HALF) for m in range(1, halves)]
    groups = [range(rows // 2), range(rows // 2, rows)]
    sides = [jnp.stack([blocks[m] for m in group]) for group in groups]
    tags = [[(m, 0) for m in group] for group in groups]

    def double(side, bit):
        sides[side] = jnp.concatenate([sides[side], over_col(sides[side], bit)])
        tags[side] = tags[side] + [(m, c ^ bit) for m, c in tags[side]]

    bit = share // 2
    while bit > 4:
        double(0, bit)
        double(1, bit)
        bit //= 2
    double(0, 2)
    double(1, 4)
    others, sides = lax.optimization_barrier((others, sides))
    late = jnp.concatenate([over_col(sides[0], 4), over_col(sides[1], 2)])
    late_tags = [(m, c ^ 4) for m, c in tags[0]] + [(m, c ^ 2) for m, c in tags[1]]
    m_held = [jnp.concatenate(sides), late]
    tags = [tags[0] + tags[1], late_tags]
    m_held += [over_col(x, 1) for x in m_held]
    tags += [[(m, c ^ 1) for m, c in ts] for ts in tags]
    wanted, width = merge_factor.shape[0] * rows, sub_vectors.shape[1]
    each = wanted // (rows * cols)
    merged = pl.pallas_call(
        functools.partial(merge_kernel, rows, cols, tags),
        out_shape=jax.ShapeDtypeStruct((wanted, width), jnp.float32),
        in_specs=[VMEM] + [VMEM] * len(m_held),
        out_specs=VMEM,
        compiler_params=limit(8),
        cost_estimate=cost([sub_vectors], 2 * wanted * sub_vectors.size),
        name="merge",
    )(sub_vectors, *m_held)
    per = GROUPS // COLOURS
    colours = pl.pallas_call(
        order_kernel,
        out_shape=[jax.ShapeDtypeStruct((1, per) + piece, dtype)] * COLOURS,
        in_specs=[SMEM, VMEM] + [VMEM] * len(others),
        out_specs=[VMEM] * COLOURS,
        compiler_params=limit(4),
        cost_estimate=cost([slices]),
        name="order",
    )(owners, slices, *others)
    colours = list(colours)
    links = [
        (HALF, lambda v: over_row(v, 1)),
        (2, lambda v: over_col(v, 2)),
        (4, lambda v: over_col(v, 4)),
    ]
    masks = [[0] for _ in range(COLOURS)]
    for step in range(2):
        for k in range(COLOURS):
            mask, send = links[(k + step) % 3]
            colours[k] = jnp.concatenate([colours[k], send(colours[k])])
            masks[k] = masks[k] + [m ^ mask for m in masks[k]]
    state = lax.all_to_all(merged.reshape(rows * cols, each, width), ("row", "col"), 0, 0)
    colours[0], state = lax.optimization_barrier((colours[0], state))
    last_round = []
    for k in range(COLOURS):
        mask, send = links[(k + 2) % 3]
        last_round.append(send(colours[k]))
        masks[k] = [masks[k], [m ^ mask for m in masks[k]]]
        masks[k] += [[m ^ 1 for m in ms] for ms in masks[k]]
    held = []
    for k in range(COLOURS):
        held.append([colours[k], last_round[k], over_col(colours[k], 1), over_col(last_round[k], 1)])

    wide = cols * width
    for members in CHAINS:
        first, last = members[0] == 0, members[-1] == COLOURS - 1
        groups = range(members[0] * per, (members[-1] + 1) * per)
        arrays = [x for k in members for x in held[k]]
        slots = [per * i for i, k in enumerate(members) for _ in held[k]]
        state = pl.pallas_call(
            functools.partial(
                chain_kernel, cols, groups, slots, sum((masks[k] for k in members), []), first, last
            ),
            out_shape=jax.ShapeDtypeStruct(
                (each, wide) if last else (8, wide), jnp.bfloat16 if last else jnp.float32
            ),
            in_specs=[SMEM, VMEM] + [VMEM] * len(arrays),
            out_specs=VMEM,
            scratch_shapes=[
                pltpu.VMEM((len(groups), group_rows, reflect), dtype),
                pltpu.VMEM((len(groups), reflect, reflect), dtype),
            ],
            compiler_params=limit(12),
            cost_estimate=cost(arrays, 2 * len(groups) * 64 * group_rows * reflect),
            name=f"chain{members[0]}",
        )(offsets, state, *arrays)
    return state


def solution(mesh):
    rows, cols = mesh.shape["row"], mesh.shape["col"]
    in_specs = (
        P("row", "col"),
        P("row", "col"),
        P("col", None, None),
        P("col", None, None),
        P(),
        P(),
    )
    out_specs = P(("row", "col"), None)
    return jax.shard_map(
        functools.partial(local, rows, cols),
        mesh=mesh,
        in_specs=in_specs,
        out_specs=out_specs,
        check_vma=False,
    )
```

```python
import functools

import jax
import jax.numpy as jnp
from jax import lax
from jax.experimental import pallas as pl
from jax.experimental.pallas import tpu as pltpu
from jax.sharding import PartitionSpec as P

GROUPS = 6
COLOURS = 3
CHAINS = ((0, 1, 2),)
HEAD = 16
HALF = 8
SLICES = 2 * HALF
VMEM = pl.BlockSpec(memory_space=pltpu.VMEM)
SMEM = pl.BlockSpec(memory_space=pltpu.SMEM)
HBM = pl.BlockSpec(memory_space=pltpu.HBM)


def limit(mib):
    return pltpu.CompilerParams(vmem_limit_bytes=mib * 1024 * 1024)


def cost(arrays, flops=0):
    size = sum(a.size * a.dtype.itemsize for a in arrays)
    return pl.CostEstimate(flops=flops, bytes_accessed=size, transcendentals=0)


def slice_index():
    row, col = lax.axis_index("row"), lax.axis_index("col")
    return lax.rem(row, 2) * HALF + lax.rem(col, HALF)


def aligned(index, size):
    return pl.ds(pl.multiple_of(index * size, size), size)


def pack_kernel(basis, factor, out, sems):
    at = aligned(lax.rem(lax.axis_index("row"), 2), HALF)
    pv = basis.shape[1]
    copies = [
        pltpu.make_async_copy(basis.at[at], out.at[:, :pv, :], sems.at[0]),
        pltpu.make_async_copy(factor.at[at], out.at[:, pv:, :], sems.at[1]),
    ]
    for copy in copies:
        copy.start()
    for copy in copies:
        copy.wait()


def places(owners, group):
    half = owners[group] // HALF
    rank = jnp.int32(0)
    for before in range(group):
        rank = rank + (owners[before] // HALF == half).astype(jnp.int32)
    return half, rank


def pick_kernel(owners, held, out):
    mine = lax.axis_index("col") // HALF
    for group in range(GROUPS):
        half, rank = places(owners, group)
        rank = jnp.minimum(rank, out.shape[0] - 1)

        @pl.when(half == mine)
        def _():
            out[rank] = held[lax.rem(owners[group], HALF)]


def order_kernel(owners, held, *refs):
    others, outs = refs[:-COLOURS], refs[-COLOURS:]
    mine = lax.axis_index("col") // HALF
    each = GROUPS // COLOURS
    for group in range(GROUPS):
        half, rank = places(owners, group)
        piece = held[lax.rem(owners[group], HALF)]
        tall = piece.shape[0]
        for mask in range(1, len(others) // 2 + 1):
            head, tail = others[2 * mask - 2 : 2 * mask]
            at = jnp.clip(rank * tall - HEAD, 0, tail.shape[0] - tall)
            other = tail[pl.ds(pl.multiple_of(at, HEAD), tall), :]
            first = jnp.concatenate([head[...], tail[: tall - HEAD, :]], 0)
            other = jnp.where(rank == 0, first, other)
            piece = jnp.where(jnp.bitwise_xor(half, mine) == mask, other, piece)
        outs[group // each][0, group % each] = piece


def merge_kernel(rows, cols, tags, sub, *refs):
    held, total = refs[:-1], refs[-1]
    row, col = lax.axis_index("row"), lax.axis_index("col")
    deep, tall = held[0].shape[2], held[0].shape[1]
    total[...] = jnp.zeros_like(total)
    for own_tags, ref in zip(tags, held):
        for index, (row_mask, col_mask) in enumerate(own_tags):
            j = jnp.bitwise_xor(lax.rem(col, cols // rows), col_mask)
            part = jnp.dot(ref[index], sub[aligned(j, deep), :], preferred_element_type=jnp.float32)
            at = aligned(jnp.bitwise_xor(row, row_mask), tall)
            total[at, :] = total[at, :] + part


def two_terms(x):
    high = x.astype(jnp.bfloat16)
    low = (x - high.astype(jnp.float32)).astype(jnp.bfloat16)
    return jnp.concatenate([high, low], 0)


def both(products):
    half = products.shape[0] // 2
    return products[:half] + products[half:]


def chain_kernel(cols, groups, slots, masks, first, last, offsets, start, *refs):
    held, (out, basis_all, factor_all) = refs[: len(masks)], refs[len(masks) :]
    mine = slice_index()
    pv, pt = basis_all.shape[1] // SLICES, factor_all.shape[1] // SLICES
    for slot, own_masks, ref in zip(slots, masks, held):
        to = slice(slot, slot + ref.shape[1])
        for index, mask in enumerate(own_masks):
            e = jnp.bitwise_xor(mine, mask)
            basis_all[to, aligned(e, pv), :] = ref[index, :, :pv, :]
            factor_all[to, aligned(e, pt), :] = ref[index, :, pv:, :]
    if first:
        n, each, width = start.shape
        pieces = start[...].reshape(n // cols, cols, each, width).sum(0)
        x = jnp.concatenate([pieces[c] for c in range(cols)], 1)
        x = jnp.concatenate([x] + [jnp.zeros_like(x)] * (8 // each - 1), 0)
    else:
        x = start[...]
    wide = x.shape[1]
    group_rows = basis_all.shape[1]
    before = jnp.int32(0)
    for slot, group in enumerate(groups):
        offset = offsets[group]
        x = pltpu.roll(x, lax.rem(before - offset + wide, wide), 1)
        before = offset
        block = x[:, :group_rows]
        weights = both(
            jnp.dot(two_terms(block), basis_all[slot], preferred_element_type=jnp.float32)
        )
        scaled = both(
            lax.dot_general(
                two_terms(weights), factor_all[slot], (((1,), (1,)), ((), ())),
                preferred_element_type=jnp.float32,
            )
        )
        change = both(
            lax.dot_general(
                two_terms(scaled), basis_all[slot], (((1,), (1,)), ((), ())),
                preferred_element_type=jnp.float32,
            )
        )
        x = jnp.concatenate([block - change, x[:, group_rows:]], 1)
    x = pltpu.roll(x, before, 1)
    if last:
        out[...] = x[: out.shape[0]].astype(out.dtype)
    else:
        out[...] = x


def local(rows, cols, sub_vectors, merge_factor, reflectors, wy_factors, owners, offsets):
    share = cols // rows
    halves = cols // HALF

    def over_col(x, mask):
        return lax.ppermute(x, "col", [(c, c ^ mask) for c in range(cols)])

    def over_row(x, mask):
        return lax.ppermute(x, "row", [(r, r ^ mask) for r in range(rows)])

    basis, factor = reflectors[0], wy_factors[0]
    group_rows, reflect = basis.shape
    dtype = basis.dtype
    pv, pt = group_rows // SLICES, reflect // SLICES
    piece = (pv + pt, reflect)

    packed = pl.pallas_call(
        pack_kernel,
        out_shape=jax.ShapeDtypeStruct((HALF,) + piece, dtype),
        in_specs=[HBM, HBM],
        out_specs=VMEM,
        scratch_shapes=[pltpu.SemaphoreType.DMA((2,))],
        compiler_params=limit(56),
        cost_estimate=cost([basis, factor]),
        name="pack",
    )(basis.reshape(SLICES, pv, reflect), factor.reshape(SLICES, pt, reflect))
    packed, merge_factor = lax.optimization_barrier((packed, merge_factor))
    members = [[h * HALF + c for c in range(HALF)] for h in range(halves)]
    slices = lax.all_to_all(packed, "col", 0, 0, axis_index_groups=members)

    picked = pl.pallas_call(
        pick_kernel,
        out_shape=jax.ShapeDtypeStruct((GROUPS - 1,) + piece, dtype),
        in_specs=[SMEM, VMEM],
        out_specs=VMEM,
        compiler_params=limit(4),
        cost_estimate=cost([slices]),
        name="pick",
    )(owners, slices)
    picked = picked.reshape(-1, reflect)
    heads = [over_col(picked[:HEAD], m * HALF) for m in range(1, halves)]
    tails = [over_col(picked[HEAD:], m * HALF) for m in range(1, halves)]

    across = [merge_factor] + [over_col(merge_factor, m * share) for m in range(1, rows)]

    row, top = lax.axis_index("row"), lax.axis_index("col") // share

    def for_row(mask):
        index = top ^ row ^ mask
        block = across[0]
        for k in range(1, rows):
            block = jnp.where(index == k, across[k], block)
        return block

    blocks = [for_row(0)] + [over_row(for_row(m), m) for m in range(1, rows)]
    heads, blocks = lax.optimization_barrier((heads, blocks))
    others = [x for pair in zip(heads, tails) for x in pair]
    groups = [range(rows // 2), range(rows // 2, rows)]
    sides = [jnp.stack([blocks[m] for m in group]) for group in groups]
    tags = [[(m, 0) for m in group] for group in groups]

    def double(side, bit):
        sides[side] = jnp.concatenate([sides[side], over_col(sides[side], bit)])
        tags[side] = tags[side] + [(m, c ^ bit) for m, c in tags[side]]

    bit = share // 2
    while bit > 4:
        double(0, bit)
        double(1, bit)
        bit //= 2
    double(0, 2)
    double(1, 4)
    late = jnp.concatenate([over_col(sides[0], 4), over_col(sides[1], 2)])
    late_tags = [(m, c ^ 4) for m, c in tags[0]] + [(m, c ^ 2) for m, c in tags[1]]
    m_held = [jnp.concatenate(sides), late]
    tags = [tags[0] + tags[1], late_tags]
    m_held += [over_col(x, 1) for x in m_held]
    tags += [[(m, c ^ 1) for m, c in ts] for ts in tags]
    wanted, width = merge_factor.shape[0] * rows, sub_vectors.shape[1]
    each = wanted // (rows * cols)
    merged = pl.pallas_call(
        functools.partial(merge_kernel, rows, cols, tags),
        out_shape=jax.ShapeDtypeStruct((wanted, width), jnp.float32),
        in_specs=[VMEM] + [VMEM] * len(m_held),
        out_specs=VMEM,
        compiler_params=limit(8),
        cost_estimate=cost([sub_vectors], 2 * wanted * sub_vectors.size),
        name="merge",
    )(sub_vectors, *m_held)
    per = GROUPS // COLOURS
    colours = pl.pallas_call(
        order_kernel,
        out_shape=[jax.ShapeDtypeStruct((1, per) + piece, dtype)] * COLOURS,
        in_specs=[SMEM, VMEM] + [VMEM] * len(others),
        out_specs=[VMEM] * COLOURS,
        compiler_params=limit(4),
        cost_estimate=cost([slices]),
        name="order",
    )(owners, slices, *others)
    colours = list(colours)
    links = [
        (HALF, lambda v: over_row(v, 1)),
        (2, lambda v: over_col(v, 2)),
        (4, lambda v: over_col(v, 4)),
    ]
    masks = [[0] for _ in range(COLOURS)]
    for step in range(2):
        for k in range(COLOURS):
            mask, send = links[(k + step) % 3]
            colours[k] = jnp.concatenate([colours[k], send(colours[k])])
            masks[k] = masks[k] + [m ^ mask for m in masks[k]]
    state = lax.all_to_all(merged.reshape(rows * cols, each, width), ("row", "col"), 0, 0)
    last_round = []
    for k in range(COLOURS):
        mask, send = links[(k + 2) % 3]
        last_round.append(send(colours[k]))
        masks[k] = [masks[k], [m ^ mask for m in masks[k]]]
        masks[k] += [[m ^ 1 for m in ms] for ms in masks[k]]
    last_round, state = lax.optimization_barrier((last_round, state))
    held = []
    for k in range(COLOURS):
        held.append([colours[k], last_round[k], over_col(colours[k], 1), over_col(last_round[k], 1)])

    wide = cols * width
    for members in CHAINS:
        first, last = members[0] == 0, members[-1] == COLOURS - 1
        groups = range(members[0] * per, (members[-1] + 1) * per)
        arrays = [x for k in members for x in held[k]]
        slots = [per * i for i, k in enumerate(members) for _ in held[k]]
        state = pl.pallas_call(
            functools.partial(
                chain_kernel, cols, groups, slots, sum((masks[k] for k in members), []), first, last
            ),
            out_shape=jax.ShapeDtypeStruct(
                (each, wide) if last else (8, wide), jnp.bfloat16 if last else jnp.float32
            ),
            in_specs=[SMEM, VMEM] + [VMEM] * len(arrays),
            out_specs=VMEM,
            scratch_shapes=[
                pltpu.VMEM((len(groups), group_rows, reflect), dtype),
                pltpu.VMEM((len(groups), reflect, reflect), dtype),
            ],
            compiler_params=limit(12),
            cost_estimate=cost(arrays, 2 * len(groups) * 64 * group_rows * reflect),
            name=f"chain{members[0]}",
        )(offsets, state, *arrays)
    return state


def solution(mesh):
    rows, cols = mesh.shape["row"], mesh.shape["col"]
    in_specs = (
        P("row", "col"),
        P("row", "col"),
        P("col", None, None),
        P("col", None, None),
        P(),
        P(),
    )
    out_specs = P(("row", "col"), None)
    return jax.shard_map(
        functools.partial(local, rows, cols),
        mesh=mesh,
        in_specs=in_specs,
        out_specs=out_specs,
        check_vma=False,
    )
```

```python
import functools

import jax
import jax.numpy as jnp
from jax import lax
from jax.experimental import pallas as pl
from jax.experimental.pallas import tpu as pltpu
from jax.sharding import PartitionSpec as P

GROUPS = 6
COLOURS = 3
CHAINS = ((0, 1, 2),)
HALF = 8
SLICES = 2 * HALF
VMEM = pl.BlockSpec(memory_space=pltpu.VMEM)
SMEM = pl.BlockSpec(memory_space=pltpu.SMEM)
HBM = pl.BlockSpec(memory_space=pltpu.HBM)


def limit(mib):
    return pltpu.CompilerParams(vmem_limit_bytes=mib * 1024 * 1024)


def cost(arrays, flops=0):
    size = sum(a.size * a.dtype.itemsize for a in arrays)
    return pl.CostEstimate(flops=flops, bytes_accessed=size, transcendentals=0)


def slice_index():
    row, col = lax.axis_index("row"), lax.axis_index("col")
    return lax.rem(row, 2) * HALF + lax.rem(col, HALF)


def aligned(index, size):
    return pl.ds(pl.multiple_of(index * size, size), size)


def pack_kernel(basis, factor, out, sems):
    at = aligned(lax.rem(lax.axis_index("row"), 2), HALF)
    pv = basis.shape[1]
    copies = [
        pltpu.make_async_copy(basis.at[at], out.at[:, :pv, :], sems.at[0]),
        pltpu.make_async_copy(factor.at[at], out.at[:, pv:, :], sems.at[1]),
    ]
    for copy in copies:
        copy.start()
    for copy in copies:
        copy.wait()


def places(owners, group):
    half = owners[group] // HALF
    rank = jnp.int32(0)
    for before in range(group):
        rank = rank + (owners[before] // HALF == half).astype(jnp.int32)
    return half, rank


def pick_kernel(owners, held, out):
    mine = lax.axis_index("col") // HALF
    for group in range(GROUPS):
        half, rank = places(owners, group)
        rank = jnp.minimum(rank, out.shape[0] - 1)

        @pl.when(half == mine)
        def _():
            out[rank] = held[lax.rem(owners[group], HALF)]


def order_kernel(owners, held, *refs):
    others, outs = refs[:-COLOURS], refs[-COLOURS:]
    mine = lax.axis_index("col") // HALF
    each = GROUPS // COLOURS
    for group in range(GROUPS):
        half, rank = places(owners, group)
        piece = held[lax.rem(owners[group], HALF)]
        for mask in range(1, len(others) // 2 + 1):
            head, tail = others[2 * mask - 2 : 2 * mask]
            other = tail[jnp.clip(rank - 1, 0, tail.shape[0] - 1)]
            other = jnp.where(rank == 0, head[0], other)
            piece = jnp.where(jnp.bitwise_xor(half, mine) == mask, other, piece)
        outs[group // each][0, group % each] = piece


def merge_kernel(rows, cols, tags, sub, *refs):
    held, total = refs[:-1], refs[-1]
    row, col = lax.axis_index("row"), lax.axis_index("col")
    deep, tall = held[0].shape[2], held[0].shape[1]
    total[...] = jnp.zeros_like(total)
    for own_tags, ref in zip(tags, held):
        for index, (row_mask, col_mask) in enumerate(own_tags):
            j = jnp.bitwise_xor(lax.rem(col, cols // rows), col_mask)
            part = jnp.dot(ref[index], sub[aligned(j, deep), :], preferred_element_type=jnp.float32)
            at = aligned(jnp.bitwise_xor(row, row_mask), tall)
            total[at, :] = total[at, :] + part


def two_terms(x):
    high = x.astype(jnp.bfloat16)
    low = (x - high.astype(jnp.float32)).astype(jnp.bfloat16)
    return jnp.concatenate([high, low], 0)


def both(products):
    half = products.shape[0] // 2
    return products[:half] + products[half:]


def chain_kernel(cols, groups, slots, masks, first, last, offsets, start, *refs):
    held, (out, basis_all, factor_all) = refs[: len(masks)], refs[len(masks) :]
    mine = slice_index()
    pv, pt = basis_all.shape[1] // SLICES, factor_all.shape[1] // SLICES
    for slot, own_masks, ref in zip(slots, masks, held):
        to = slice(slot, slot + ref.shape[1])
        for index, mask in enumerate(own_masks):
            e = jnp.bitwise_xor(mine, mask)
            basis_all[to, aligned(e, pv), :] = ref[index, :, :pv, :]
            factor_all[to, aligned(e, pt), :] = ref[index, :, pv:, :]
    if first:
        n, each, width = start.shape
        pieces = start[...].reshape(n // cols, cols, each, width).sum(0)
        x = jnp.concatenate([pieces[c] for c in range(cols)], 1)
        x = jnp.concatenate([x] + [jnp.zeros_like(x)] * (8 // each - 1), 0)
    else:
        x = start[...]
    wide = x.shape[1]
    group_rows = basis_all.shape[1]
    before = jnp.int32(0)
    for slot, group in enumerate(groups):
        offset = offsets[group]
        x = pltpu.roll(x, lax.rem(before - offset + wide, wide), 1)
        before = offset
        block = x[:, :group_rows]
        weights = both(
            jnp.dot(two_terms(block), basis_all[slot], preferred_element_type=jnp.float32)
        )
        scaled = both(
            lax.dot_general(
                two_terms(weights), factor_all[slot], (((1,), (1,)), ((), ())),
                preferred_element_type=jnp.float32,
            )
        )
        change = both(
            lax.dot_general(
                two_terms(scaled), basis_all[slot], (((1,), (1,)), ((), ())),
                preferred_element_type=jnp.float32,
            )
        )
        x = jnp.concatenate([block - change, x[:, group_rows:]], 1)
    x = pltpu.roll(x, before, 1)
    if last:
        out[...] = x[: out.shape[0]].astype(out.dtype)
    else:
        out[...] = x


def local(rows, cols, sub_vectors, merge_factor, reflectors, wy_factors, owners, offsets):
    share = cols // rows
    halves = cols // HALF

    def over_col(x, mask):
        return lax.ppermute(x, "col", [(c, c ^ mask) for c in range(cols)])

    def over_row(x, mask):
        return lax.ppermute(x, "row", [(r, r ^ mask) for r in range(rows)])

    basis, factor = reflectors[0], wy_factors[0]
    group_rows, reflect = basis.shape
    dtype = basis.dtype
    pv, pt = group_rows // SLICES, reflect // SLICES
    piece = (pv + pt, reflect)

    across = [merge_factor] + [over_col(merge_factor, m * share) for m in range(1, rows)]

    packed = pl.pallas_call(
        pack_kernel,
        out_shape=jax.ShapeDtypeStruct((HALF,) + piece, dtype),
        in_specs=[HBM, HBM],
        out_specs=VMEM,
        scratch_shapes=[pltpu.SemaphoreType.DMA((2,))],
        compiler_params=limit(56),
        cost_estimate=cost([basis, factor]),
        name="pack",
    )(basis.reshape(SLICES, pv, reflect), factor.reshape(SLICES, pt, reflect))
    members = [[h * HALF + c for c in range(HALF)] for h in range(halves)]
    slices = lax.all_to_all(packed, "col", 0, 0, axis_index_groups=members)

    row, top = lax.axis_index("row"), lax.axis_index("col") // share

    def for_row(mask):
        index = top ^ row ^ mask
        block = across[0]
        for k in range(1, rows):
            block = jnp.where(index == k, across[k], block)
        return block

    blocks = [for_row(0)] + [over_row(for_row(m), m) for m in range(1, rows)]
    groups = [range(rows // 2), range(rows // 2, rows)]
    sides = [jnp.stack([blocks[m] for m in group]) for group in groups]
    tags = [[(m, 0) for m in group] for group in groups]

    def double(side, bit):
        sides[side] = jnp.concatenate([sides[side], over_col(sides[side], bit)])
        tags[side] = tags[side] + [(m, c ^ bit) for m, c in tags[side]]

    bit = share // 2
    while bit > 4:
        double(0, bit)
        double(1, bit)
        bit //= 2
    double(0, 2)
    double(1, 4)
    slices, sides = lax.optimization_barrier((slices, sides))

    picked = pl.pallas_call(
        pick_kernel,
        out_shape=jax.ShapeDtypeStruct((GROUPS - 1,) + piece, dtype),
        in_specs=[SMEM, VMEM],
        out_specs=VMEM,
        compiler_params=limit(4),
        cost_estimate=cost([slices]),
        name="pick",
    )(owners, slices)
    heads = [over_col(picked[:1], m * HALF) for m in range(1, halves)]
    tails = [over_col(picked[1:], m * HALF) for m in range(1, halves)]
    heads, sides = lax.optimization_barrier((heads, sides))
    others = [x for pair in zip(heads, tails) for x in pair]
    late = jnp.concatenate([over_col(sides[0], 4), over_col(sides[1], 2)])
    late_tags = [(m, c ^ 4) for m, c in tags[0]] + [(m, c ^ 2) for m, c in tags[1]]
    m_held = [jnp.concatenate(sides), late]
    tags = [tags[0] + tags[1], late_tags]
    m_held += [over_col(x, 1) for x in m_held]
    tags += [[(m, c ^ 1) for m, c in ts] for ts in tags]
    wanted, width = merge_factor.shape[0] * rows, sub_vectors.shape[1]
    each = wanted // (rows * cols)
    merged = pl.pallas_call(
        functools.partial(merge_kernel, rows, cols, tags),
        out_shape=jax.ShapeDtypeStruct((wanted, width), jnp.float32),
        in_specs=[VMEM] + [VMEM] * len(m_held),
        out_specs=VMEM,
        compiler_params=limit(8),
        cost_estimate=cost([sub_vectors], 2 * wanted * sub_vectors.size),
        name="merge",
    )(sub_vectors, *m_held)
    per = GROUPS // COLOURS
    colours = pl.pallas_call(
        order_kernel,
        out_shape=[jax.ShapeDtypeStruct((1, per) + piece, dtype)] * COLOURS,
        in_specs=[SMEM, VMEM] + [VMEM] * len(others),
        out_specs=[VMEM] * COLOURS,
        compiler_params=limit(4),
        cost_estimate=cost([slices]),
        name="order",
    )(owners, slices, *others)
    colours = list(colours)
    links = [
        (HALF, lambda v: over_row(v, 1)),
        (2, lambda v: over_col(v, 2)),
        (4, lambda v: over_col(v, 4)),
    ]
    masks = [[0] for _ in range(COLOURS)]
    for step in range(2):
        for k in range(COLOURS):
            mask, send = links[(k + step) % 3]
            colours[k] = jnp.concatenate([colours[k], send(colours[k])])
            masks[k] = masks[k] + [m ^ mask for m in masks[k]]
    state = lax.all_to_all(merged.reshape(rows * cols, each, width), ("row", "col"), 0, 0)
    colours, state = lax.optimization_barrier((colours, state))
    last_round = []
    for k in range(COLOURS):
        mask, send = links[(k + 2) % 3]
        last_round.append(send(colours[k]))
        masks[k] = [masks[k], [m ^ mask for m in masks[k]]]
        masks[k] += [[m ^ 1 for m in ms] for ms in masks[k]]
    held = []
    for k in range(COLOURS):
        held.append([colours[k], last_round[k], over_col(colours[k], 1), over_col(last_round[k], 1)])

    wide = cols * width
    for members in CHAINS:
        first, last = members[0] == 0, members[-1] == COLOURS - 1
        groups = range(members[0] * per, (members[-1] + 1) * per)
        arrays = [x for k in members for x in held[k]]
        slots = [per * i for i, k in enumerate(members) for _ in held[k]]
        state = pl.pallas_call(
            functools.partial(
                chain_kernel, cols, groups, slots, sum((masks[k] for k in members), []), first, last
            ),
            out_shape=jax.ShapeDtypeStruct(
                (each, wide) if last else (8, wide), jnp.bfloat16 if last else jnp.float32
            ),
            in_specs=[SMEM, VMEM] + [VMEM] * len(arrays),
            out_specs=VMEM,
            scratch_shapes=[
                pltpu.VMEM((len(groups), group_rows, reflect), dtype),
                pltpu.VMEM((len(groups), reflect, reflect), dtype),
            ],
            compiler_params=limit(12),
            cost_estimate=cost(arrays, 2 * len(groups) * 64 * group_rows * reflect),
            name=f"chain{members[0]}",
        )(offsets, state, *arrays)
    return state


def solution(mesh):
    rows, cols = mesh.shape["row"], mesh.shape["col"]
    in_specs = (
        P("row", "col"),
        P("row", "col"),
        P("col", None, None),
        P("col", None, None),
        P(),
        P(),
    )
    out_specs = P(("row", "col"), None)
    return jax.shard_map(
        functools.partial(local, rows, cols),
        mesh=mesh,
        in_specs=in_specs,
        out_specs=out_specs,
        check_vma=False,
    )
```

```python
import functools

import jax
import jax.numpy as jnp
from jax import lax
from jax.experimental import pallas as pl
from jax.experimental.pallas import tpu as pltpu
from jax.sharding import PartitionSpec as P

GROUPS = 6
COLOURS = 3
CHAINS = ((0, 1, 2),)
HALF = 8
SLICES = 2 * HALF
VMEM = pl.BlockSpec(memory_space=pltpu.VMEM)
SMEM = pl.BlockSpec(memory_space=pltpu.SMEM)
HBM = pl.BlockSpec(memory_space=pltpu.HBM)


def limit(mib):
    return pltpu.CompilerParams(vmem_limit_bytes=mib * 1024 * 1024)


def cost(arrays, flops=0):
    size = sum(a.size * a.dtype.itemsize for a in arrays)
    return pl.CostEstimate(flops=flops, bytes_accessed=size, transcendentals=0)


def slice_index():
    row, col = lax.axis_index("row"), lax.axis_index("col")
    return lax.rem(row, 2) * HALF + lax.rem(col, HALF)


def aligned(index, size):
    return pl.ds(pl.multiple_of(index * size, size), size)


def pack_kernel(basis, factor, out, sems):
    at = aligned(lax.rem(lax.axis_index("row"), 2), HALF)
    pv = basis.shape[1]
    copies = [
        pltpu.make_async_copy(basis.at[at], out.at[:, :pv, :], sems.at[0]),
        pltpu.make_async_copy(factor.at[at], out.at[:, pv:, :], sems.at[1]),
    ]
    for copy in copies:
        copy.start()
    for copy in copies:
        copy.wait()


def places(owners, group):
    half = owners[group] // HALF
    rank = jnp.int32(0)
    for before in range(group):
        rank = rank + (owners[before] // HALF == half).astype(jnp.int32)
    return half, rank


def pick_kernel(owners, held, out):
    mine = lax.axis_index("col") // HALF
    for group in range(GROUPS):
        half, rank = places(owners, group)
        rank = jnp.minimum(rank, out.shape[0] - 1)

        @pl.when(half == mine)
        def _():
            out[rank] = held[lax.rem(owners[group], HALF)]


def order_kernel(owners, held, *refs):
    others, outs = refs[:-COLOURS], refs[-COLOURS:]
    mine = lax.axis_index("col") // HALF
    each = GROUPS // COLOURS
    for group in range(GROUPS):
        half, rank = places(owners, group)
        piece = held[lax.rem(owners[group], HALF)]
        for mask in range(1, len(others) // 2 + 1):
            head, tail = others[2 * mask - 2 : 2 * mask]
            other = tail[jnp.clip(rank - 1, 0, tail.shape[0] - 1)]
            other = jnp.where(rank == 0, head[0], other)
            piece = jnp.where(jnp.bitwise_xor(half, mine) == mask, other, piece)
        outs[group // each][0, group % each] = piece


def merge_kernel(rows, cols, tags, sub, *refs):
    held, total = refs[:-1], refs[-1]
    row, col = lax.axis_index("row"), lax.axis_index("col")
    deep, tall = held[0].shape[2], held[0].shape[1]
    total[...] = jnp.zeros_like(total)
    for own_tags, ref in zip(tags, held):
        for index, (row_mask, col_mask) in enumerate(own_tags):
            j = jnp.bitwise_xor(lax.rem(col, cols // rows), col_mask)
            part = jnp.dot(ref[index], sub[aligned(j, deep), :], preferred_element_type=jnp.float32)
            at = aligned(jnp.bitwise_xor(row, row_mask), tall)
            total[at, :] = total[at, :] + part


def two_terms(x):
    high = x.astype(jnp.bfloat16)
    low = (x - high.astype(jnp.float32)).astype(jnp.bfloat16)
    return jnp.concatenate([high, low], 0)


def both(products):
    half = products.shape[0] // 2
    return products[:half] + products[half:]


def chain_kernel(cols, groups, slots, masks, first, last, offsets, start, *refs):
    held, (out, basis_all, factor_all) = refs[: len(masks)], refs[len(masks) :]
    mine = slice_index()
    pv, pt = basis_all.shape[1] // SLICES, factor_all.shape[1] // SLICES
    for slot, own_masks, ref in zip(slots, masks, held):
        to = slice(slot, slot + ref.shape[1])
        for index, mask in enumerate(own_masks):
            e = jnp.bitwise_xor(mine, mask)
            basis_all[to, aligned(e, pv), :] = ref[index, :, :pv, :]
            factor_all[to, aligned(e, pt), :] = ref[index, :, pv:, :]
    if first:
        n, each, width = start.shape
        pieces = start[...].reshape(n // cols, cols, each, width).sum(0)
        x = jnp.concatenate([pieces[c] for c in range(cols)], 1)
        x = jnp.concatenate([x] + [jnp.zeros_like(x)] * (8 // each - 1), 0)
    else:
        x = start[...]
    wide = x.shape[1]
    group_rows = basis_all.shape[1]
    before = jnp.int32(0)
    for slot, group in enumerate(groups):
        offset = offsets[group]
        x = pltpu.roll(x, lax.rem(before - offset + wide, wide), 1)
        before = offset
        block = x[:, :group_rows]
        weights = both(
            jnp.dot(two_terms(block), basis_all[slot], preferred_element_type=jnp.float32)
        )
        scaled = both(
            lax.dot_general(
                two_terms(weights), factor_all[slot], (((1,), (1,)), ((), ())),
                preferred_element_type=jnp.float32,
            )
        )
        change = both(
            lax.dot_general(
                two_terms(scaled), basis_all[slot], (((1,), (1,)), ((), ())),
                preferred_element_type=jnp.float32,
            )
        )
        x = jnp.concatenate([block - change, x[:, group_rows:]], 1)
    x = pltpu.roll(x, before, 1)
    if last:
        out[...] = x[: out.shape[0]].astype(out.dtype)
    else:
        out[...] = x


def local(rows, cols, sub_vectors, merge_factor, reflectors, wy_factors, owners, offsets):
    share = cols // rows
    halves = cols // HALF

    def over_col(x, mask):
        return lax.ppermute(x, "col", [(c, c ^ mask) for c in range(cols)])

    def over_row(x, mask):
        return lax.ppermute(x, "row", [(r, r ^ mask) for r in range(rows)])

    basis, factor = reflectors[0], wy_factors[0]
    group_rows, reflect = basis.shape
    dtype = basis.dtype
    pv, pt = group_rows // SLICES, reflect // SLICES
    piece = (pv + pt, reflect)

    across = [merge_factor] + [over_col(merge_factor, m * share) for m in range(1, rows)]

    packed = pl.pallas_call(
        pack_kernel,
        out_shape=jax.ShapeDtypeStruct((HALF,) + piece, dtype),
        in_specs=[HBM, HBM],
        out_specs=VMEM,
        scratch_shapes=[pltpu.SemaphoreType.DMA((2,))],
        compiler_params=limit(56),
        cost_estimate=cost([basis, factor]),
        name="pack",
    )(basis.reshape(SLICES, pv, reflect), factor.reshape(SLICES, pt, reflect))
    members = [[h * HALF + c for c in range(HALF)] for h in range(halves)]
    slices = lax.all_to_all(packed, "col", 0, 0, axis_index_groups=members)

    row, top = lax.axis_index("row"), lax.axis_index("col") // share

    def for_row(mask):
        index = top ^ row ^ mask
        block = across[0]
        for k in range(1, rows):
            block = jnp.where(index == k, across[k], block)
        return block

    blocks = [for_row(0)] + [over_row(for_row(m), m) for m in range(1, rows)]
    groups = [range(rows // 2), range(rows // 2, rows)]
    sides = [jnp.stack([blocks[m] for m in group]) for group in groups]
    tags = [[(m, 0) for m in group] for group in groups]

    def double(side, bit):
        sides[side] = jnp.concatenate([sides[side], over_col(sides[side], bit)])
        tags[side] = tags[side] + [(m, c ^ bit) for m, c in tags[side]]

    bit = share // 2
    while bit > 4:
        double(0, bit)
        double(1, bit)
        bit //= 2
    double(0, 2)
    double(1, 4)
    slices, sides = lax.optimization_barrier((slices, sides))

    picked = pl.pallas_call(
        pick_kernel,
        out_shape=jax.ShapeDtypeStruct((GROUPS - 1,) + piece, dtype),
        in_specs=[SMEM, VMEM],
        out_specs=VMEM,
        compiler_params=limit(4),
        cost_estimate=cost([slices]),
        name="pick",
    )(owners, slices)
    heads = [over_col(picked[:1], m * HALF) for m in range(1, halves)]
    tails = [over_col(picked[1:], m * HALF) for m in range(1, halves)]
    heads, sides = lax.optimization_barrier((heads, sides))
    others = [x for pair in zip(heads, tails) for x in pair]
    late = jnp.concatenate([over_col(sides[0], 4), over_col(sides[1], 2)])
    late_tags = [(m, c ^ 4) for m, c in tags[0]] + [(m, c ^ 2) for m, c in tags[1]]
    m_held = [jnp.concatenate(sides), late]
    tags = [tags[0] + tags[1], late_tags]
    m_held += [over_col(x, 1) for x in m_held]
    tags += [[(m, c ^ 1) for m, c in ts] for ts in tags]
    wanted, width = merge_factor.shape[0] * rows, sub_vectors.shape[1]
    each = wanted // (rows * cols)
    merged = pl.pallas_call(
        functools.partial(merge_kernel, rows, cols, tags),
        out_shape=jax.ShapeDtypeStruct((wanted, width), jnp.float32),
        in_specs=[VMEM] + [VMEM] * len(m_held),
        out_specs=VMEM,
        compiler_params=limit(8),
        cost_estimate=cost([sub_vectors], 2 * wanted * sub_vectors.size),
        name="merge",
    )(sub_vectors, *m_held)
    per = GROUPS // COLOURS
    colours = pl.pallas_call(
        order_kernel,
        out_shape=[jax.ShapeDtypeStruct((1, per) + piece, dtype)] * COLOURS,
        in_specs=[SMEM, VMEM] + [VMEM] * len(others),
        out_specs=[VMEM] * COLOURS,
        compiler_params=limit(4),
        cost_estimate=cost([slices]),
        name="order",
    )(owners, slices, *others)
    colours = list(colours)
    links = [
        (HALF, lambda v: over_row(v, 1)),
        (2, lambda v: over_col(v, 2)),
        (4, lambda v: over_col(v, 4)),
    ]
    masks = [[0] for _ in range(COLOURS)]
    for step in range(2):
        for k in range(COLOURS):
            mask, send = links[(k + step) % 3]
            colours[k] = jnp.concatenate([colours[k], send(colours[k])])
            masks[k] = masks[k] + [m ^ mask for m in masks[k]]
    state = lax.all_to_all(merged.reshape(rows * cols, each, width), ("row", "col"), 0, 0)
    last_round = []
    for k in range(COLOURS):
        mask, send = links[(k + 2) % 3]
        last_round.append(send(colours[k]))
        masks[k] = [masks[k], [m ^ mask for m in masks[k]]]
        masks[k] += [[m ^ 1 for m in ms] for ms in masks[k]]
    last_round, state = lax.optimization_barrier((last_round, state))
    held = []
    for k in range(COLOURS):
        held.append([colours[k], last_round[k], over_col(colours[k], 1), over_col(last_round[k], 1)])

    wide = cols * width
    for members in CHAINS:
        first, last = members[0] == 0, members[-1] == COLOURS - 1
        groups = range(members[0] * per, (members[-1] + 1) * per)
        arrays = [x for k in members for x in held[k]]
        slots = [per * i for i, k in enumerate(members) for _ in held[k]]
        state = pl.pallas_call(
            functools.partial(
                chain_kernel, cols, groups, slots, sum((masks[k] for k in members), []), first, last
            ),
            out_shape=jax.ShapeDtypeStruct(
                (each, wide) if last else (8, wide), jnp.bfloat16 if last else jnp.float32
            ),
            in_specs=[SMEM, VMEM] + [VMEM] * len(arrays),
            out_specs=VMEM,
            scratch_shapes=[
                pltpu.VMEM((len(groups), group_rows, reflect), dtype),
                pltpu.VMEM((len(groups), reflect, reflect), dtype),
            ],
            compiler_params=limit(12),
            cost_estimate=cost(arrays, 2 * len(groups) * 64 * group_rows * reflect),
            name=f"chain{members[0]}",
        )(offsets, state, *arrays)
    return state


def solution(mesh):
    rows, cols = mesh.shape["row"], mesh.shape["col"]
    in_specs = (
        P("row", "col"),
        P("row", "col"),
        P("col", None, None),
        P("col", None, None),
        P(),
        P(),
    )
    out_specs = P(("row", "col"), None)
    return jax.shard_map(
        functools.partial(local, rows, cols),
        mesh=mesh,
        in_specs=in_specs,
        out_specs=out_specs,
        check_vma=False,
    )
```

```python
import functools

import jax
import jax.numpy as jnp
from jax import lax
from jax.experimental import pallas as pl
from jax.experimental.pallas import tpu as pltpu
from jax.sharding import PartitionSpec as P

GROUPS = 6
COLOURS = 3
CHAINS = ((0, 1, 2),)
HALF = 8
SLICES = 2 * HALF
VMEM = pl.BlockSpec(memory_space=pltpu.VMEM)
SMEM = pl.BlockSpec(memory_space=pltpu.SMEM)
HBM = pl.BlockSpec(memory_space=pltpu.HBM)


def limit(mib):
    return pltpu.CompilerParams(vmem_limit_bytes=mib * 1024 * 1024)


def cost(arrays, flops=0):
    size = sum(a.size * a.dtype.itemsize for a in arrays)
    return pl.CostEstimate(flops=flops, bytes_accessed=size, transcendentals=0)


def slice_index():
    row, col = lax.axis_index("row"), lax.axis_index("col")
    return lax.rem(row, 2) * HALF + lax.rem(col, HALF)


def aligned(index, size):
    return pl.ds(pl.multiple_of(index * size, size), size)


def pack_kernel(basis, factor, out, sems):
    at = aligned(lax.rem(lax.axis_index("row"), 2), HALF)
    pv = basis.shape[1]
    copies = [
        pltpu.make_async_copy(basis.at[at], out.at[:, :pv, :], sems.at[0]),
        pltpu.make_async_copy(factor.at[at], out.at[:, pv:, :], sems.at[1]),
    ]
    for copy in copies:
        copy.start()
    for copy in copies:
        copy.wait()


def places(owners, group):
    half = owners[group] // HALF
    rank = jnp.int32(0)
    for before in range(group):
        rank = rank + (owners[before] // HALF == half).astype(jnp.int32)
    return half, rank


def pick_kernel(owners, held, out):
    mine = lax.axis_index("col") // HALF
    for group in range(GROUPS):
        half, rank = places(owners, group)
        rank = jnp.minimum(rank, out.shape[0] - 1)

        @pl.when(half == mine)
        def _():
            out[rank] = held[lax.rem(owners[group], HALF)]


def order_kernel(owners, held, *refs):
    others, outs = refs[:-COLOURS], refs[-COLOURS:]
    mine = lax.axis_index("col") // HALF
    each = GROUPS // COLOURS
    for group in range(GROUPS):
        half, rank = places(owners, group)
        piece = held[lax.rem(owners[group], HALF)]
        for mask in range(1, len(others) // 2 + 1):
            head, tail = others[2 * mask - 2 : 2 * mask]
            other = tail[jnp.clip(rank - 1, 0, tail.shape[0] - 1)]
            other = jnp.where(rank == 0, head[0], other)
            piece = jnp.where(jnp.bitwise_xor(half, mine) == mask, other, piece)
        outs[group // each][0, group % each] = piece


def merge_kernel(rows, cols, tags, sub, *refs):
    held, total = refs[:-1], refs[-1]
    row, col = lax.axis_index("row"), lax.axis_index("col")
    deep, tall = held[0].shape[2], held[0].shape[1]
    total[...] = jnp.zeros_like(total)
    for own_tags, ref in zip(tags, held):
        for index, (row_mask, col_mask) in enumerate(own_tags):
            j = jnp.bitwise_xor(lax.rem(col, cols // rows), col_mask)
            part = jnp.dot(ref[index], sub[aligned(j, deep), :], preferred_element_type=jnp.float32)
            at = aligned(jnp.bitwise_xor(row, row_mask), tall)
            total[at, :] = total[at, :] + part


def two_terms(x):
    high = x.astype(jnp.bfloat16)
    low = (x - high.astype(jnp.float32)).astype(jnp.bfloat16)
    return jnp.concatenate([high, low], 0)


def both(products):
    half = products.shape[0] // 2
    return products[:half] + products[half:]


def chain_kernel(cols, groups, slots, masks, first, last, offsets, start, *refs):
    held, (out, basis_all, factor_all) = refs[: len(masks)], refs[len(masks) :]
    mine = slice_index()
    pv, pt = basis_all.shape[1] // SLICES, factor_all.shape[1] // SLICES
    for slot, own_masks, ref in zip(slots, masks, held):
        to = slice(slot, slot + ref.shape[1])
        for index, mask in enumerate(own_masks):
            e = jnp.bitwise_xor(mine, mask)
            basis_all[to, aligned(e, pv), :] = ref[index, :, :pv, :]
            factor_all[to, aligned(e, pt), :] = ref[index, :, pv:, :]
    if first:
        n, each, width = start.shape
        pieces = start[...].reshape(n // cols, cols, each, width).sum(0)
        x = jnp.concatenate([pieces[c] for c in range(cols)], 1)
        x = jnp.concatenate([x] + [jnp.zeros_like(x)] * (8 // each - 1), 0)
    else:
        x = start[...]
    wide = x.shape[1]
    group_rows = basis_all.shape[1]
    before = jnp.int32(0)
    for slot, group in enumerate(groups):
        offset = offsets[group]
        x = pltpu.roll(x, lax.rem(before - offset + wide, wide), 1)
        before = offset
        block = x[:, :group_rows]
        weights = both(
            jnp.dot(two_terms(block), basis_all[slot], preferred_element_type=jnp.float32)
        )
        scaled = both(
            lax.dot_general(
                two_terms(weights), factor_all[slot], (((1,), (1,)), ((), ())),
                preferred_element_type=jnp.float32,
            )
        )
        change = both(
            lax.dot_general(
                two_terms(scaled), basis_all[slot], (((1,), (1,)), ((), ())),
                preferred_element_type=jnp.float32,
            )
        )
        x = jnp.concatenate([block - change, x[:, group_rows:]], 1)
    x = pltpu.roll(x, before, 1)
    if last:
        out[...] = x[: out.shape[0]].astype(out.dtype)
    else:
        out[...] = x


def local(rows, cols, sub_vectors, merge_factor, reflectors, wy_factors, owners, offsets):
    share = cols // rows
    halves = cols // HALF

    def over_col(x, mask):
        return lax.ppermute(x, "col", [(c, c ^ mask) for c in range(cols)])

    def over_row(x, mask):
        return lax.ppermute(x, "row", [(r, r ^ mask) for r in range(rows)])

    basis, factor = reflectors[0], wy_factors[0]
    group_rows, reflect = basis.shape
    dtype = basis.dtype
    pv, pt = group_rows // SLICES, reflect // SLICES
    piece = (pv + pt, reflect)

    across = [merge_factor] + [over_col(merge_factor, m * share) for m in range(1, rows)]

    packed = pl.pallas_call(
        pack_kernel,
        out_shape=jax.ShapeDtypeStruct((HALF,) + piece, dtype),
        in_specs=[HBM, HBM],
        out_specs=VMEM,
        scratch_shapes=[pltpu.SemaphoreType.DMA((2,))],
        compiler_params=limit(56),
        cost_estimate=cost([basis, factor]),
        name="pack",
    )(basis.reshape(SLICES, pv, reflect), factor.reshape(SLICES, pt, reflect))
    members = [[h * HALF + c for c in range(HALF)] for h in range(halves)]
    slices = lax.all_to_all(packed, "col", 0, 0, axis_index_groups=members)

    row, top = lax.axis_index("row"), lax.axis_index("col") // share

    def for_row(mask):
        index = top ^ row ^ mask
        block = across[0]
        for k in range(1, rows):
            block = jnp.where(index == k, across[k], block)
        return block

    blocks = [for_row(0)] + [over_row(for_row(m), m) for m in range(1, rows)]
    groups = [range(rows // 2), range(rows // 2, rows)]
    sides = [jnp.stack([blocks[m] for m in group]) for group in groups]
    tags = [[(m, 0) for m in group] for group in groups]

    def double(side, bit):
        sides[side] = jnp.concatenate([sides[side], over_col(sides[side], bit)])
        tags[side] = tags[side] + [(m, c ^ bit) for m, c in tags[side]]

    bit = share // 2
    while bit > 4:
        double(0, bit)
        double(1, bit)
        bit //= 2
    double(0, 2)
    double(1, 4)
    slices, sides = lax.optimization_barrier((slices, sides))

    picked = pl.pallas_call(
        pick_kernel,
        out_shape=jax.ShapeDtypeStruct((GROUPS - 1,) + piece, dtype),
        in_specs=[SMEM, VMEM],
        out_specs=VMEM,
        compiler_params=limit(4),
        cost_estimate=cost([slices]),
        name="pick",
    )(owners, slices)
    heads = [over_col(picked[:1], m * HALF) for m in range(1, halves)]
    tails = [over_col(picked[1:], m * HALF) for m in range(1, halves)]
    heads, sides = lax.optimization_barrier((heads, sides))
    others = [x for pair in zip(heads, tails) for x in pair]
    late = jnp.concatenate([over_col(sides[0], 4), over_col(sides[1], 2)])
    late_tags = [(m, c ^ 4) for m, c in tags[0]] + [(m, c ^ 2) for m, c in tags[1]]
    m_held = [jnp.concatenate(sides), late]
    tags = [tags[0] + tags[1], late_tags]
    m_held += [over_col(x, 1) for x in m_held]
    tags += [[(m, c ^ 1) for m, c in ts] for ts in tags]
    wanted, width = merge_factor.shape[0] * rows, sub_vectors.shape[1]
    each = wanted // (rows * cols)
    merged = pl.pallas_call(
        functools.partial(merge_kernel, rows, cols, tags),
        out_shape=jax.ShapeDtypeStruct((wanted, width), jnp.float32),
        in_specs=[VMEM] + [VMEM] * len(m_held),
        out_specs=VMEM,
        compiler_params=limit(8),
        cost_estimate=cost([sub_vectors], 2 * wanted * sub_vectors.size),
        name="merge",
    )(sub_vectors, *m_held)
    per = GROUPS // COLOURS
    colours = pl.pallas_call(
        order_kernel,
        out_shape=[jax.ShapeDtypeStruct((1, per) + piece, dtype)] * COLOURS,
        in_specs=[SMEM, VMEM] + [VMEM] * len(others),
        out_specs=[VMEM] * COLOURS,
        compiler_params=limit(4),
        cost_estimate=cost([slices]),
        name="order",
    )(owners, slices, *others)
    colours = list(colours)
    links = [
        (HALF, lambda v: over_row(v, 1)),
        (2, lambda v: over_col(v, 2)),
        (4, lambda v: over_col(v, 4)),
    ]
    masks = [[0] for _ in range(COLOURS)]
    for step in range(2):
        for k in range(COLOURS):
            mask, send = links[(k + step) % 3]
            colours[k] = jnp.concatenate([colours[k], send(colours[k])])
            masks[k] = masks[k] + [m ^ mask for m in masks[k]]
        if step == 0:
            colours = list(lax.optimization_barrier(colours))
    state = lax.all_to_all(merged.reshape(rows * cols, each, width), ("row", "col"), 0, 0)
    last_round = []
    for k in range(COLOURS):
        mask, send = links[(k + 2) % 3]
        last_round.append(send(colours[k]))
        masks[k] = [masks[k], [m ^ mask for m in masks[k]]]
        masks[k] += [[m ^ 1 for m in ms] for ms in masks[k]]
    last_round, state = lax.optimization_barrier((last_round, state))
    held = []
    for k in range(COLOURS):
        held.append([colours[k], last_round[k], over_col(colours[k], 1), over_col(last_round[k], 1)])

    wide = cols * width
    for members in CHAINS:
        first, last = members[0] == 0, members[-1] == COLOURS - 1
        groups = range(members[0] * per, (members[-1] + 1) * per)
        arrays = [x for k in members for x in held[k]]
        slots = [per * i for i, k in enumerate(members) for _ in held[k]]
        state = pl.pallas_call(
            functools.partial(
                chain_kernel, cols, groups, slots, sum((masks[k] for k in members), []), first, last
            ),
            out_shape=jax.ShapeDtypeStruct(
                (each, wide) if last else (8, wide), jnp.bfloat16 if last else jnp.float32
            ),
            in_specs=[SMEM, VMEM] + [VMEM] * len(arrays),
            out_specs=VMEM,
            scratch_shapes=[
                pltpu.VMEM((len(groups), group_rows, reflect), dtype),
                pltpu.VMEM((len(groups), reflect, reflect), dtype),
            ],
            compiler_params=limit(12),
            cost_estimate=cost(arrays, 2 * len(groups) * 64 * group_rows * reflect),
            name=f"chain{members[0]}",
        )(offsets, state, *arrays)
    return state


def solution(mesh):
    rows, cols = mesh.shape["row"], mesh.shape["col"]
    in_specs = (
        P("row", "col"),
        P("row", "col"),
        P("col", None, None),
        P("col", None, None),
        P(),
        P(),
    )
    out_specs = P(("row", "col"), None)
    return jax.shard_map(
        functools.partial(local, rows, cols),
        mesh=mesh,
        in_specs=in_specs,
        out_specs=out_specs,
        check_vma=False,
    )
```

```python
import functools

import jax
import jax.numpy as jnp
from jax import lax
from jax.experimental import pallas as pl
from jax.experimental.pallas import tpu as pltpu
from jax.sharding import PartitionSpec as P

GROUPS = 6
COLOURS = 3
CHAINS = ((0, 1, 2),)
HALF = 8
SLICES = 2 * HALF
VMEM = pl.BlockSpec(memory_space=pltpu.VMEM)
SMEM = pl.BlockSpec(memory_space=pltpu.SMEM)
HBM = pl.BlockSpec(memory_space=pltpu.HBM)


def limit(mib):
    return pltpu.CompilerParams(vmem_limit_bytes=mib * 1024 * 1024)


def cost(arrays, flops=0):
    size = sum(a.size * a.dtype.itemsize for a in arrays)
    return pl.CostEstimate(flops=flops, bytes_accessed=size, transcendentals=0)


def slice_index():
    row, col = lax.axis_index("row"), lax.axis_index("col")
    return lax.rem(row, 2) * HALF + lax.rem(col, HALF)


def aligned(index, size):
    return pl.ds(pl.multiple_of(index * size, size), size)


def pack_kernel(basis, factor, out, sems):
    at = aligned(lax.rem(lax.axis_index("row"), 2), HALF)
    pv = basis.shape[1]
    copies = [
        pltpu.make_async_copy(basis.at[at], out.at[:, :pv, :], sems.at[0]),
        pltpu.make_async_copy(factor.at[at], out.at[:, pv:, :], sems.at[1]),
    ]
    for copy in copies:
        copy.start()
    for copy in copies:
        copy.wait()


def places(owners, group):
    half = owners[group] // HALF
    rank = jnp.int32(0)
    for before in range(group):
        rank = rank + (owners[before] // HALF == half).astype(jnp.int32)
    return half, rank


def pick_kernel(owners, held, out):
    mine = lax.axis_index("col") // HALF
    for group in range(GROUPS):
        half, rank = places(owners, group)
        rank = jnp.minimum(rank, out.shape[0] - 1)

        @pl.when(half == mine)
        def _():
            out[rank] = held[lax.rem(owners[group], HALF)]


def order_kernel(owners, held, *refs):
    others, outs = refs[:-COLOURS], refs[-COLOURS:]
    mine = lax.axis_index("col") // HALF
    each = GROUPS // COLOURS
    for group in range(GROUPS):
        half, rank = places(owners, group)
        piece = held[lax.rem(owners[group], HALF)]
        for mask in range(1, len(others) // 2 + 1):
            head, tail = others[2 * mask - 2 : 2 * mask]
            other = tail[jnp.clip(rank - 1, 0, tail.shape[0] - 1)]
            other = jnp.where(rank == 0, head[0], other)
            piece = jnp.where(jnp.bitwise_xor(half, mine) == mask, other, piece)
        outs[group // each][0, group % each] = piece


def merge_kernel(rows, cols, tags, sub, *refs):
    held, total = refs[:-1], refs[-1]
    row, col = lax.axis_index("row"), lax.axis_index("col")
    deep, tall = held[0].shape[2], held[0].shape[1]
    total[...] = jnp.zeros_like(total)
    for own_tags, ref in zip(tags, held):
        for index, (row_mask, col_mask) in enumerate(own_tags):
            j = jnp.bitwise_xor(lax.rem(col, cols // rows), col_mask)
            part = jnp.dot(ref[index], sub[aligned(j, deep), :], preferred_element_type=jnp.float32)
            at = aligned(jnp.bitwise_xor(row, row_mask), tall)
            total[at, :] = total[at, :] + part


def two_terms(x):
    high = x.astype(jnp.bfloat16)
    low = (x - high.astype(jnp.float32)).astype(jnp.bfloat16)
    return jnp.concatenate([high, low], 0)


def both(products):
    half = products.shape[0] // 2
    return products[:half] + products[half:]


def chain_kernel(cols, groups, slots, masks, first, last, offsets, start, *refs):
    held, (out, basis_all, factor_all) = refs[: len(masks)], refs[len(masks) :]
    mine = slice_index()
    pv, pt = basis_all.shape[1] // SLICES, factor_all.shape[1] // SLICES
    for slot, own_masks, ref in zip(slots, masks, held):
        to = slice(slot, slot + ref.shape[1])
        for index, mask in enumerate(own_masks):
            e = jnp.bitwise_xor(mine, mask)
            basis_all[to, aligned(e, pv), :] = ref[index, :, :pv, :]
            factor_all[to, aligned(e, pt), :] = ref[index, :, pv:, :]
    if first:
        n, each, width = start.shape
        pieces = start[...].reshape(n // cols, cols, each, width).sum(0)
        x = jnp.concatenate([pieces[c] for c in range(cols)], 1)
        x = jnp.concatenate([x] + [jnp.zeros_like(x)] * (8 // each - 1), 0)
    else:
        x = start[...]
    wide = x.shape[1]
    group_rows = basis_all.shape[1]
    before = jnp.int32(0)
    for slot, group in enumerate(groups):
        offset = offsets[group]
        x = pltpu.roll(x, lax.rem(before - offset + wide, wide), 1)
        before = offset
        block = x[:, :group_rows]
        weights = both(
            jnp.dot(two_terms(block), basis_all[slot], preferred_element_type=jnp.float32)
        )
        scaled = both(
            lax.dot_general(
                two_terms(weights), factor_all[slot], (((1,), (1,)), ((), ())),
                preferred_element_type=jnp.float32,
            )
        )
        change = both(
            lax.dot_general(
                two_terms(scaled), basis_all[slot], (((1,), (1,)), ((), ())),
                preferred_element_type=jnp.float32,
            )
        )
        x = jnp.concatenate([block - change, x[:, group_rows:]], 1)
    x = pltpu.roll(x, before, 1)
    if last:
        out[...] = x[: out.shape[0]].astype(out.dtype)
    else:
        out[...] = x


def local(rows, cols, sub_vectors, merge_factor, reflectors, wy_factors, owners, offsets):
    share = cols // rows
    halves = cols // HALF

    def over_col(x, mask):
        return lax.ppermute(x, "col", [(c, c ^ mask) for c in range(cols)])

    def over_row(x, mask):
        return lax.ppermute(x, "row", [(r, r ^ mask) for r in range(rows)])

    basis, factor = reflectors[0], wy_factors[0]
    group_rows, reflect = basis.shape
    dtype = basis.dtype
    pv, pt = group_rows // SLICES, reflect // SLICES
    piece = (pv + pt, reflect)

    across = [merge_factor] + [over_col(merge_factor, m * share) for m in range(1, rows)]

    packed = pl.pallas_call(
        pack_kernel,
        out_shape=jax.ShapeDtypeStruct((HALF,) + piece, dtype),
        in_specs=[HBM, HBM],
        out_specs=VMEM,
        scratch_shapes=[pltpu.SemaphoreType.DMA((2,))],
        compiler_params=limit(56),
        cost_estimate=cost([basis, factor]),
        name="pack",
    )(basis.reshape(SLICES, pv, reflect), factor.reshape(SLICES, pt, reflect))
    members = [[h * HALF + c for c in range(HALF)] for h in range(halves)]
    slices = lax.all_to_all(packed, "col", 0, 0, axis_index_groups=members)

    row, top = lax.axis_index("row"), lax.axis_index("col") // share

    def for_row(mask):
        index = top ^ row ^ mask
        block = across[0]
        for k in range(1, rows):
            block = jnp.where(index == k, across[k], block)
        return block

    blocks = [for_row(0)] + [over_row(for_row(m), m) for m in range(1, rows)]
    groups = [range(rows // 2), range(rows // 2, rows)]
    sides = [jnp.stack([blocks[m] for m in group]) for group in groups]
    tags = [[(m, 0) for m in group] for group in groups]

    def double(side, bit):
        sides[side] = jnp.concatenate([sides[side], over_col(sides[side], bit)])
        tags[side] = tags[side] + [(m, c ^ bit) for m, c in tags[side]]

    bit = share // 2
    while bit > 4:
        double(0, bit)
        double(1, bit)
        bit //= 2
    double(0, 2)
    double(1, 4)
    slices, sides = lax.optimization_barrier((slices, sides))

    picked = pl.pallas_call(
        pick_kernel,
        out_shape=jax.ShapeDtypeStruct((GROUPS - 1,) + piece, dtype),
        in_specs=[SMEM, VMEM],
        out_specs=VMEM,
        compiler_params=limit(4),
        cost_estimate=cost([slices]),
        name="pick",
    )(owners, slices)
    heads = [over_col(picked[:1], m * HALF) for m in range(1, halves)]
    tails = [over_col(picked[1:], m * HALF) for m in range(1, halves)]
    heads, sides = lax.optimization_barrier((heads, sides))
    others = [x for pair in zip(heads, tails) for x in pair]
    late = jnp.concatenate([over_col(sides[0], 4), over_col(sides[1], 2)])
    late_tags = [(m, c ^ 4) for m, c in tags[0]] + [(m, c ^ 2) for m, c in tags[1]]
    m_held = [jnp.concatenate(sides), late]
    tags = [tags[0] + tags[1], late_tags]
    m_held += [over_col(x, 1) for x in m_held]
    tags += [[(m, c ^ 1) for m, c in ts] for ts in tags]
    wanted, width = merge_factor.shape[0] * rows, sub_vectors.shape[1]
    each = wanted // (rows * cols)
    merged = pl.pallas_call(
        functools.partial(merge_kernel, rows, cols, tags),
        out_shape=jax.ShapeDtypeStruct((wanted, width), jnp.float32),
        in_specs=[VMEM] + [VMEM] * len(m_held),
        out_specs=VMEM,
        compiler_params=limit(8),
        cost_estimate=cost([sub_vectors], 2 * wanted * sub_vectors.size),
        name="merge",
    )(sub_vectors, *m_held)
    per = GROUPS // COLOURS
    colours = pl.pallas_call(
        order_kernel,
        out_shape=[jax.ShapeDtypeStruct((1, per) + piece, dtype)] * COLOURS,
        in_specs=[SMEM, VMEM] + [VMEM] * len(others),
        out_specs=[VMEM] * COLOURS,
        compiler_params=limit(4),
        cost_estimate=cost([slices]),
        name="order",
    )(owners, slices, *others)
    colours = list(colours)
    links = [
        (HALF, lambda v: over_row(v, 1)),
        (2, lambda v: over_col(v, 2)),
        (4, lambda v: over_col(v, 4)),
    ]
    masks = [[0] for _ in range(COLOURS)]
    for step in range(2):
        for k in range(COLOURS):
            mask, send = links[(k + step) % 3]
            colours[k] = jnp.concatenate([colours[k], send(colours[k])])
            masks[k] = masks[k] + [m ^ mask for m in masks[k]]
        if step == 0:
            colours, merged = lax.optimization_barrier((colours, merged))
    state = lax.all_to_all(merged.reshape(rows * cols, each, width), ("row", "col"), 0, 0)
    last_round = []
    for k in range(COLOURS):
        mask, send = links[(k + 2) % 3]
        last_round.append(send(colours[k]))
        masks[k] = [masks[k], [m ^ mask for m in masks[k]]]
        masks[k] += [[m ^ 1 for m in ms] for ms in masks[k]]
    last_round, state = lax.optimization_barrier((last_round, state))
    held = []
    for k in range(COLOURS):
        held.append([colours[k], last_round[k], over_col(colours[k], 1), over_col(last_round[k], 1)])

    wide = cols * width
    for members in CHAINS:
        first, last = members[0] == 0, members[-1] == COLOURS - 1
        groups = range(members[0] * per, (members[-1] + 1) * per)
        arrays = [x for k in members for x in held[k]]
        slots = [per * i for i, k in enumerate(members) for _ in held[k]]
        state = pl.pallas_call(
            functools.partial(
                chain_kernel, cols, groups, slots, sum((masks[k] for k in members), []), first, last
            ),
            out_shape=jax.ShapeDtypeStruct(
                (each, wide) if last else (8, wide), jnp.bfloat16 if last else jnp.float32
            ),
            in_specs=[SMEM, VMEM] + [VMEM] * len(arrays),
            out_specs=VMEM,
            scratch_shapes=[
                pltpu.VMEM((len(groups), group_rows, reflect), dtype),
                pltpu.VMEM((len(groups), reflect, reflect), dtype),
            ],
            compiler_params=limit(12),
            cost_estimate=cost(arrays, 2 * len(groups) * 64 * group_rows * reflect),
            name=f"chain{members[0]}",
        )(offsets, state, *arrays)
    return state


def solution(mesh):
    rows, cols = mesh.shape["row"], mesh.shape["col"]
    in_specs = (
        P("row", "col"),
        P("row", "col"),
        P("col", None, None),
        P("col", None, None),
        P(),
        P(),
    )
    out_specs = P(("row", "col"), None)
    return jax.shard_map(
        functools.partial(local, rows, cols),
        mesh=mesh,
        in_specs=in_specs,
        out_specs=out_specs,
        check_vma=False,
    )
```

```python
import functools

import jax
import jax.numpy as jnp
from jax import lax
from jax.experimental import pallas as pl
from jax.experimental.pallas import tpu as pltpu
from jax.sharding import PartitionSpec as P

GROUPS = 6
COLOURS = 3
CHAINS = ((0,), (1, 2))
HALF = 8
SLICES = 2 * HALF
VMEM = pl.BlockSpec(memory_space=pltpu.VMEM)
SMEM = pl.BlockSpec(memory_space=pltpu.SMEM)
HBM = pl.BlockSpec(memory_space=pltpu.HBM)


def limit(mib):
    return pltpu.CompilerParams(vmem_limit_bytes=mib * 1024 * 1024)


def cost(arrays, flops=0):
    size = sum(a.size * a.dtype.itemsize for a in arrays)
    return pl.CostEstimate(flops=flops, bytes_accessed=size, transcendentals=0)


def slice_index():
    row, col = lax.axis_index("row"), lax.axis_index("col")
    return lax.rem(row, 2) * HALF + lax.rem(col, HALF)


def aligned(index, size):
    return pl.ds(pl.multiple_of(index * size, size), size)


def pack_kernel(basis, factor, out, sems):
    at = aligned(lax.rem(lax.axis_index("row"), 2), HALF)
    pv = basis.shape[1]
    copies = [
        pltpu.make_async_copy(basis.at[at], out.at[:, :pv, :], sems.at[0]),
        pltpu.make_async_copy(factor.at[at], out.at[:, pv:, :], sems.at[1]),
    ]
    for copy in copies:
        copy.start()
    for copy in copies:
        copy.wait()


def places(owners, group):
    half = owners[group] // HALF
    rank = jnp.int32(0)
    for before in range(group):
        rank = rank + (owners[before] // HALF == half).astype(jnp.int32)
    return half, rank


def pick_kernel(owners, held, out):
    mine = lax.axis_index("col") // HALF
    for group in range(GROUPS):
        half, rank = places(owners, group)
        rank = jnp.minimum(rank, out.shape[0] - 1)

        @pl.when(half == mine)
        def _():
            out[rank] = held[lax.rem(owners[group], HALF)]


def order_kernel(owners, held, *refs):
    others, outs = refs[:-COLOURS], refs[-COLOURS:]
    mine = lax.axis_index("col") // HALF
    each = GROUPS // COLOURS
    for group in range(GROUPS):
        half, rank = places(owners, group)
        piece = held[lax.rem(owners[group], HALF)]
        for mask in range(1, len(others) // 2 + 1):
            head, tail = others[2 * mask - 2 : 2 * mask]
            other = tail[jnp.clip(rank - 1, 0, tail.shape[0] - 1)]
            other = jnp.where(rank == 0, head[0], other)
            piece = jnp.where(jnp.bitwise_xor(half, mine) == mask, other, piece)
        outs[group // each][0, group % each] = piece


def merge_kernel(rows, cols, tags, sub, *refs):
    held, total = refs[:-1], refs[-1]
    row, col = lax.axis_index("row"), lax.axis_index("col")
    deep, tall = held[0].shape[2], held[0].shape[1]
    total[...] = jnp.zeros_like(total)
    for own_tags, ref in zip(tags, held):
        for index, (row_mask, col_mask) in enumerate(own_tags):
            j = jnp.bitwise_xor(lax.rem(col, cols // rows), col_mask)
            part = jnp.dot(ref[index], sub[aligned(j, deep), :], preferred_element_type=jnp.float32)
            at = aligned(jnp.bitwise_xor(row, row_mask), tall)
            total[at, :] = total[at, :] + part


def two_terms(x):
    high = x.astype(jnp.bfloat16)
    low = (x - high.astype(jnp.float32)).astype(jnp.bfloat16)
    return jnp.concatenate([high, low], 0)


def both(products):
    half = products.shape[0] // 2
    return products[:half] + products[half:]


def chain_kernel(cols, groups, slots, masks, first, last, offsets, start, *refs):
    held, (out, basis_all, factor_all) = refs[: len(masks)], refs[len(masks) :]
    mine = slice_index()
    pv, pt = basis_all.shape[1] // SLICES, factor_all.shape[1] // SLICES
    for slot, own_masks, ref in zip(slots, masks, held):
        to = slice(slot, slot + ref.shape[1])
        for index, mask in enumerate(own_masks):
            e = jnp.bitwise_xor(mine, mask)
            basis_all[to, aligned(e, pv), :] = ref[index, :, :pv, :]
            factor_all[to, aligned(e, pt), :] = ref[index, :, pv:, :]
    if first:
        n, each, width = start.shape
        pieces = start[...].reshape(n // cols, cols, each, width).sum(0)
        x = jnp.concatenate([pieces[c] for c in range(cols)], 1)
        x = jnp.concatenate([x] + [jnp.zeros_like(x)] * (8 // each - 1), 0)
    else:
        x = start[...]
    wide = x.shape[1]
    group_rows = basis_all.shape[1]
    before = jnp.int32(0)
    for slot, group in enumerate(groups):
        offset = offsets[group]
        x = pltpu.roll(x, lax.rem(before - offset + wide, wide), 1)
        before = offset
        block = x[:, :group_rows]
        weights = both(
            jnp.dot(two_terms(block), basis_all[slot], preferred_element_type=jnp.float32)
        )
        scaled = both(
            lax.dot_general(
                two_terms(weights), factor_all[slot], (((1,), (1,)), ((), ())),
                preferred_element_type=jnp.float32,
            )
        )
        change = both(
            lax.dot_general(
                two_terms(scaled), basis_all[slot], (((1,), (1,)), ((), ())),
                preferred_element_type=jnp.float32,
            )
        )
        x = jnp.concatenate([block - change, x[:, group_rows:]], 1)
    x = pltpu.roll(x, before, 1)
    if last:
        out[...] = x[: out.shape[0]].astype(out.dtype)
    else:
        out[...] = x


def local(rows, cols, sub_vectors, merge_factor, reflectors, wy_factors, owners, offsets):
    share = cols // rows
    halves = cols // HALF

    def over_col(x, mask):
        return lax.ppermute(x, "col", [(c, c ^ mask) for c in range(cols)])

    def over_row(x, mask):
        return lax.ppermute(x, "row", [(r, r ^ mask) for r in range(rows)])

    basis, factor = reflectors[0], wy_factors[0]
    group_rows, reflect = basis.shape
    dtype = basis.dtype
    pv, pt = group_rows // SLICES, reflect // SLICES
    piece = (pv + pt, reflect)

    across = [merge_factor] + [over_col(merge_factor, m * share) for m in range(1, rows)]

    packed = pl.pallas_call(
        pack_kernel,
        out_shape=jax.ShapeDtypeStruct((HALF,) + piece, dtype),
        in_specs=[HBM, HBM],
        out_specs=VMEM,
        scratch_shapes=[pltpu.SemaphoreType.DMA((2,))],
        compiler_params=limit(56),
        cost_estimate=cost([basis, factor]),
        name="pack",
    )(basis.reshape(SLICES, pv, reflect), factor.reshape(SLICES, pt, reflect))
    members = [[h * HALF + c for c in range(HALF)] for h in range(halves)]
    slices = lax.all_to_all(packed, "col", 0, 0, axis_index_groups=members)

    row, top = lax.axis_index("row"), lax.axis_index("col") // share

    def for_row(mask):
        index = top ^ row ^ mask
        block = across[0]
        for k in range(1, rows):
            block = jnp.where(index == k, across[k], block)
        return block

    blocks = [for_row(0)] + [over_row(for_row(m), m) for m in range(1, rows)]
    groups = [range(rows // 2), range(rows // 2, rows)]
    sides = [jnp.stack([blocks[m] for m in group]) for group in groups]
    tags = [[(m, 0) for m in group] for group in groups]

    def double(side, bit):
        sides[side] = jnp.concatenate([sides[side], over_col(sides[side], bit)])
        tags[side] = tags[side] + [(m, c ^ bit) for m, c in tags[side]]

    bit = share // 2
    while bit > 4:
        double(0, bit)
        double(1, bit)
        bit //= 2
    double(0, 2)
    double(1, 4)
    slices, sides = lax.optimization_barrier((slices, sides))

    picked = pl.pallas_call(
        pick_kernel,
        out_shape=jax.ShapeDtypeStruct((GROUPS - 1,) + piece, dtype),
        in_specs=[SMEM, VMEM],
        out_specs=VMEM,
        compiler_params=limit(4),
        cost_estimate=cost([slices]),
        name="pick",
    )(owners, slices)
    heads = [over_col(picked[:1], m * HALF) for m in range(1, halves)]
    tails = [over_col(picked[1:], m * HALF) for m in range(1, halves)]
    heads, sides = lax.optimization_barrier((heads, sides))
    others = [x for pair in zip(heads, tails) for x in pair]
    late = jnp.concatenate([over_col(sides[0], 4), over_col(sides[1], 2)])
    late_tags = [(m, c ^ 4) for m, c in tags[0]] + [(m, c ^ 2) for m, c in tags[1]]
    m_held = [jnp.concatenate(sides), late]
    tags = [tags[0] + tags[1], late_tags]
    m_held += [over_col(x, 1) for x in m_held]
    tags += [[(m, c ^ 1) for m, c in ts] for ts in tags]
    wanted, width = merge_factor.shape[0] * rows, sub_vectors.shape[1]
    each = wanted // (rows * cols)
    merged = pl.pallas_call(
        functools.partial(merge_kernel, rows, cols, tags),
        out_shape=jax.ShapeDtypeStruct((wanted, width), jnp.float32),
        in_specs=[VMEM] + [VMEM] * len(m_held),
        out_specs=VMEM,
        compiler_params=limit(8),
        cost_estimate=cost([sub_vectors], 2 * wanted * sub_vectors.size),
        name="merge",
    )(sub_vectors, *m_held)
    per = GROUPS // COLOURS
    colours = pl.pallas_call(
        order_kernel,
        out_shape=[jax.ShapeDtypeStruct((1, per) + piece, dtype)] * COLOURS,
        in_specs=[SMEM, VMEM] + [VMEM] * len(others),
        out_specs=[VMEM] * COLOURS,
        compiler_params=limit(4),
        cost_estimate=cost([slices]),
        name="order",
    )(owners, slices, *others)
    colours = list(colours)
    links = [
        (HALF, lambda v: over_row(v, 1)),
        (2, lambda v: over_col(v, 2)),
        (4, lambda v: over_col(v, 4)),
    ]
    masks = [[0] for _ in range(COLOURS)]
    for step in range(2):
        for k in range(COLOURS):
            mask, send = links[(k + step) % 3]
            colours[k] = jnp.concatenate([colours[k], send(colours[k])])
            masks[k] = masks[k] + [m ^ mask for m in masks[k]]
    state = lax.all_to_all(merged.reshape(rows * cols, each, width), ("row", "col"), 0, 0)
    last_round = []
    for k in range(COLOURS):
        mask, send = links[(k + 2) % 3]
        last_round.append(send(colours[k]))
        masks[k] = [masks[k], [m ^ mask for m in masks[k]]]
        masks[k] += [[m ^ 1 for m in ms] for ms in masks[k]]
    last_round, state = lax.optimization_barrier((last_round, state))
    held = []
    for k in range(COLOURS):
        held.append([colours[k], last_round[k], over_col(colours[k], 1), over_col(last_round[k], 1)])

    wide = cols * width
    for members in CHAINS:
        first, last = members[0] == 0, members[-1] == COLOURS - 1
        groups = range(members[0] * per, (members[-1] + 1) * per)
        arrays = [x for k in members for x in held[k]]
        slots = [per * i for i, k in enumerate(members) for _ in held[k]]
        state = pl.pallas_call(
            functools.partial(
                chain_kernel, cols, groups, slots, sum((masks[k] for k in members), []), first, last
            ),
            out_shape=jax.ShapeDtypeStruct(
                (each, wide) if last else (8, wide), jnp.bfloat16 if last else jnp.float32
            ),
            in_specs=[SMEM, VMEM] + [VMEM] * len(arrays),
            out_specs=VMEM,
            scratch_shapes=[
                pltpu.VMEM((len(groups), group_rows, reflect), dtype),
                pltpu.VMEM((len(groups), reflect, reflect), dtype),
            ],
            compiler_params=limit(12),
            cost_estimate=cost(arrays, 2 * len(groups) * 64 * group_rows * reflect),
            name=f"chain{members[0]}",
        )(offsets, state, *arrays)
    return state


def solution(mesh):
    rows, cols = mesh.shape["row"], mesh.shape["col"]
    in_specs = (
        P("row", "col"),
        P("row", "col"),
        P("col", None, None),
        P("col", None, None),
        P(),
        P(),
    )
    out_specs = P(("row", "col"), None)
    return jax.shard_map(
        functools.partial(local, rows, cols),
        mesh=mesh,
        in_specs=in_specs,
        out_specs=out_specs,
        check_vma=False,
    )
```

```python
import functools

import jax
import jax.numpy as jnp
from jax import lax
from jax.experimental import pallas as pl
from jax.experimental.pallas import tpu as pltpu
from jax.sharding import PartitionSpec as P

GROUPS = 6
COLOURS = 3
CHAINS = ((0,), (1, 2))
HALF = 8
SLICES = 2 * HALF
VMEM = pl.BlockSpec(memory_space=pltpu.VMEM)
SMEM = pl.BlockSpec(memory_space=pltpu.SMEM)
HBM = pl.BlockSpec(memory_space=pltpu.HBM)


def limit(mib):
    return pltpu.CompilerParams(vmem_limit_bytes=mib * 1024 * 1024)


def cost(arrays, flops=0):
    size = sum(a.size * a.dtype.itemsize for a in arrays)
    return pl.CostEstimate(flops=flops, bytes_accessed=size, transcendentals=0)


def slice_index():
    row, col = lax.axis_index("row"), lax.axis_index("col")
    return lax.rem(row, 2) * HALF + lax.rem(col, HALF)


def aligned(index, size):
    return pl.ds(pl.multiple_of(index * size, size), size)


def pack_kernel(basis, factor, out, sems):
    at = aligned(lax.rem(lax.axis_index("row"), 2), HALF)
    pv = basis.shape[1]
    copies = [
        pltpu.make_async_copy(basis.at[at], out.at[:, :pv, :], sems.at[0]),
        pltpu.make_async_copy(factor.at[at], out.at[:, pv:, :], sems.at[1]),
    ]
    for copy in copies:
        copy.start()
    for copy in copies:
        copy.wait()


def places(owners, group):
    half = owners[group] // HALF
    rank = jnp.int32(0)
    for before in range(group):
        rank = rank + (owners[before] // HALF == half).astype(jnp.int32)
    return half, rank


def pick_kernel(owners, held, out):
    mine = lax.axis_index("col") // HALF
    for group in range(GROUPS):
        half, rank = places(owners, group)
        rank = jnp.minimum(rank, out.shape[0] - 1)

        @pl.when(half == mine)
        def _():
            out[rank] = held[lax.rem(owners[group], HALF)]


def order_kernel(owners, held, *refs):
    others, outs = refs[:-COLOURS], refs[-COLOURS:]
    mine = lax.axis_index("col") // HALF
    each = GROUPS // COLOURS
    for group in range(GROUPS):
        half, rank = places(owners, group)
        piece = held[lax.rem(owners[group], HALF)]
        for mask in range(1, len(others) // 2 + 1):
            head, tail = others[2 * mask - 2 : 2 * mask]
            other = tail[jnp.clip(rank - 1, 0, tail.shape[0] - 1)]
            other = jnp.where(rank == 0, head[0], other)
            piece = jnp.where(jnp.bitwise_xor(half, mine) == mask, other, piece)
        outs[group // each][0, group % each] = piece


def merge_kernel(rows, cols, tags, sub, *refs):
    held, total = refs[:-1], refs[-1]
    row, col = lax.axis_index("row"), lax.axis_index("col")
    deep, tall = held[0].shape[2], held[0].shape[1]
    total[...] = jnp.zeros_like(total)
    for own_tags, ref in zip(tags, held):
        for index, (row_mask, col_mask) in enumerate(own_tags):
            j = jnp.bitwise_xor(lax.rem(col, cols // rows), col_mask)
            part = jnp.dot(ref[index], sub[aligned(j, deep), :], preferred_element_type=jnp.float32)
            at = aligned(jnp.bitwise_xor(row, row_mask), tall)
            total[at, :] = total[at, :] + part


def two_terms(x):
    high = x.astype(jnp.bfloat16)
    low = (x - high.astype(jnp.float32)).astype(jnp.bfloat16)
    return jnp.concatenate([high, low], 0)


def both(products):
    half = products.shape[0] // 2
    return products[:half] + products[half:]


def chain_kernel(cols, groups, slots, masks, first, last, offsets, start, *refs):
    held, (out, basis_all, factor_all) = refs[: len(masks)], refs[len(masks) :]
    mine = slice_index()
    pv, pt = basis_all.shape[1] // SLICES, factor_all.shape[1] // SLICES
    for slot, own_masks, ref in zip(slots, masks, held):
        to = slice(slot, slot + ref.shape[1])
        for index, mask in enumerate(own_masks):
            e = jnp.bitwise_xor(mine, mask)
            basis_all[to, aligned(e, pv), :] = ref[index, :, :pv, :]
            factor_all[to, aligned(e, pt), :] = ref[index, :, pv:, :]
    if first:
        n, each, width = start.shape
        pieces = start[...].reshape(n // cols, cols, each, width).sum(0)
        x = jnp.concatenate([pieces[c] for c in range(cols)], 1)
        x = jnp.concatenate([x] + [jnp.zeros_like(x)] * (8 // each - 1), 0)
    else:
        x = start[...]
    wide = x.shape[1]
    group_rows = basis_all.shape[1]
    before = jnp.int32(0)
    for slot, group in enumerate(groups):
        offset = offsets[group]
        x = pltpu.roll(x, lax.rem(before - offset + wide, wide), 1)
        before = offset
        block = x[:, :group_rows]
        weights = both(
            jnp.dot(two_terms(block), basis_all[slot], preferred_element_type=jnp.float32)
        )
        scaled = both(
            lax.dot_general(
                two_terms(weights), factor_all[slot], (((1,), (1,)), ((), ())),
                preferred_element_type=jnp.float32,
            )
        )
        change = both(
            lax.dot_general(
                two_terms(scaled), basis_all[slot], (((1,), (1,)), ((), ())),
                preferred_element_type=jnp.float32,
            )
        )
        x = jnp.concatenate([block - change, x[:, group_rows:]], 1)
    x = pltpu.roll(x, before, 1)
    if last:
        out[...] = x[: out.shape[0]].astype(out.dtype)
    else:
        out[...] = x


def local(rows, cols, sub_vectors, merge_factor, reflectors, wy_factors, owners, offsets):
    share = cols // rows
    halves = cols // HALF

    def over_col(x, mask):
        return lax.ppermute(x, "col", [(c, c ^ mask) for c in range(cols)])

    def over_row(x, mask):
        return lax.ppermute(x, "row", [(r, r ^ mask) for r in range(rows)])

    basis, factor = reflectors[0], wy_factors[0]
    group_rows, reflect = basis.shape
    dtype = basis.dtype
    pv, pt = group_rows // SLICES, reflect // SLICES
    piece = (pv + pt, reflect)

    across = [merge_factor] + [over_col(merge_factor, m * share) for m in range(1, rows)]

    packed = pl.pallas_call(
        pack_kernel,
        out_shape=jax.ShapeDtypeStruct((HALF,) + piece, dtype),
        in_specs=[HBM, HBM],
        out_specs=VMEM,
        scratch_shapes=[pltpu.SemaphoreType.DMA((2,))],
        compiler_params=limit(56),
        cost_estimate=cost([basis, factor]),
        name="pack",
    )(basis.reshape(SLICES, pv, reflect), factor.reshape(SLICES, pt, reflect))
    members = [[h * HALF + c for c in range(HALF)] for h in range(halves)]
    slices = lax.all_to_all(packed, "col", 0, 0, axis_index_groups=members)

    row, top = lax.axis_index("row"), lax.axis_index("col") // share

    def for_row(mask):
        index = top ^ row ^ mask
        block = across[0]
        for k in range(1, rows):
            block = jnp.where(index == k, across[k], block)
        return block

    blocks = [for_row(0)] + [over_row(for_row(m), m) for m in range(1, rows)]
    groups = [range(rows // 2), range(rows // 2, rows)]
    sides = [jnp.stack([blocks[m] for m in group]) for group in groups]
    tags = [[(m, 0) for m in group] for group in groups]

    def double(side, bit):
        sides[side] = jnp.concatenate([sides[side], over_col(sides[side], bit)])
        tags[side] = tags[side] + [(m, c ^ bit) for m, c in tags[side]]

    bit = share // 2
    while bit > 4:
        double(0, bit)
        double(1, bit)
        bit //= 2
    double(0, 2)
    double(1, 4)
    slices, sides = lax.optimization_barrier((slices, sides))

    picked = pl.pallas_call(
        pick_kernel,
        out_shape=jax.ShapeDtypeStruct((GROUPS - 1,) + piece, dtype),
        in_specs=[SMEM, VMEM],
        out_specs=VMEM,
        compiler_params=limit(4),
        cost_estimate=cost([slices]),
        name="pick",
    )(owners, slices)
    heads = [over_col(picked[:1], m * HALF) for m in range(1, halves)]
    tails = [over_col(picked[1:], m * HALF) for m in range(1, halves)]
    heads, sides = lax.optimization_barrier((heads, sides))
    others = [x for pair in zip(heads, tails) for x in pair]
    late = jnp.concatenate([over_col(sides[0], 4), over_col(sides[1], 2)])
    late_tags = [(m, c ^ 4) for m, c in tags[0]] + [(m, c ^ 2) for m, c in tags[1]]
    m_held = [jnp.concatenate(sides), late]
    tags = [tags[0] + tags[1], late_tags]
    m_held += [over_col(x, 1) for x in m_held]
    tags += [[(m, c ^ 1) for m, c in ts] for ts in tags]
    wanted, width = merge_factor.shape[0] * rows, sub_vectors.shape[1]
    each = wanted // (rows * cols)
    merged = pl.pallas_call(
        functools.partial(merge_kernel, rows, cols, tags),
        out_shape=jax.ShapeDtypeStruct((wanted, width), jnp.float32),
        in_specs=[VMEM] + [VMEM] * len(m_held),
        out_specs=VMEM,
        compiler_params=limit(8),
        cost_estimate=cost([sub_vectors], 2 * wanted * sub_vectors.size),
        name="merge",
    )(sub_vectors, *m_held)
    per = GROUPS // COLOURS
    colours = pl.pallas_call(
        order_kernel,
        out_shape=[jax.ShapeDtypeStruct((1, per) + piece, dtype)] * COLOURS,
        in_specs=[SMEM, VMEM] + [VMEM] * len(others),
        out_specs=[VMEM] * COLOURS,
        compiler_params=limit(4),
        cost_estimate=cost([slices]),
        name="order",
    )(owners, slices, *others)
    colours = list(colours)
    links = [
        (HALF, lambda v: over_row(v, 1)),
        (2, lambda v: over_col(v, 2)),
        (4, lambda v: over_col(v, 4)),
    ]
    masks = [[0] for _ in range(COLOURS)]
    for step in range(2):
        for k in range(COLOURS):
            mask, send = links[(k + step) % 3]
            colours[k] = jnp.concatenate([colours[k], send(colours[k])])
            masks[k] = masks[k] + [m ^ mask for m in masks[k]]
    state = lax.all_to_all(merged.reshape(rows * cols, each, width), ("row", "col"), 0, 0)
    last_round = []
    for k in range(COLOURS):
        mask, send = links[(k + 2) % 3]
        last_round.append(send(colours[k]))
        masks[k] = [masks[k], [m ^ mask for m in masks[k]]]
        masks[k] += [[m ^ 1 for m in ms] for ms in masks[k]]
    last_round[0], state = lax.optimization_barrier((last_round[0], state))
    held = []
    for k in range(COLOURS):
        held.append([colours[k], last_round[k], over_col(colours[k], 1), over_col(last_round[k], 1)])

    wide = cols * width
    for members in CHAINS:
        first, last = members[0] == 0, members[-1] == COLOURS - 1
        groups = range(members[0] * per, (members[-1] + 1) * per)
        arrays = [x for k in members for x in held[k]]
        slots = [per * i for i, k in enumerate(members) for _ in held[k]]
        state = pl.pallas_call(
            functools.partial(
                chain_kernel, cols, groups, slots, sum((masks[k] for k in members), []), first, last
            ),
            out_shape=jax.ShapeDtypeStruct(
                (each, wide) if last else (8, wide), jnp.bfloat16 if last else jnp.float32
            ),
            in_specs=[SMEM, VMEM] + [VMEM] * len(arrays),
            out_specs=VMEM,
            scratch_shapes=[
                pltpu.VMEM((len(groups), group_rows, reflect), dtype),
                pltpu.VMEM((len(groups), reflect, reflect), dtype),
            ],
            compiler_params=limit(12),
            cost_estimate=cost(arrays, 2 * len(groups) * 64 * group_rows * reflect),
            name=f"chain{members[0]}",
        )(offsets, state, *arrays)
    return state


def solution(mesh):
    rows, cols = mesh.shape["row"], mesh.shape["col"]
    in_specs = (
        P("row", "col"),
        P("row", "col"),
        P("col", None, None),
        P("col", None, None),
        P(),
        P(),
    )
    out_specs = P(("row", "col"), None)
    return jax.shard_map(
        functools.partial(local, rows, cols),
        mesh=mesh,
        in_specs=in_specs,
        out_specs=out_specs,
        check_vma=False,
    )
```

```python
import functools

import jax
import jax.numpy as jnp
from jax import lax
from jax.experimental import pallas as pl
from jax.experimental.pallas import tpu as pltpu
from jax.sharding import PartitionSpec as P

GROUPS = 6
COLOURS = 3
CHAINS = ((0,), (1, 2))
HALF = 8
SLICES = 2 * HALF
VMEM = pl.BlockSpec(memory_space=pltpu.VMEM)
SMEM = pl.BlockSpec(memory_space=pltpu.SMEM)
HBM = pl.BlockSpec(memory_space=pltpu.HBM)


def limit(mib):
    return pltpu.CompilerParams(vmem_limit_bytes=mib * 1024 * 1024)


def cost(arrays, flops=0):
    size = sum(a.size * a.dtype.itemsize for a in arrays)
    return pl.CostEstimate(flops=flops, bytes_accessed=size, transcendentals=0)


def slice_index():
    row, col = lax.axis_index("row"), lax.axis_index("col")
    return lax.rem(row, 2) * HALF + lax.rem(col, HALF)


def aligned(index, size):
    return pl.ds(pl.multiple_of(index * size, size), size)


def pack_kernel(basis, factor, out, sems):
    at = aligned(lax.rem(lax.axis_index("row"), 2), HALF)
    pv = basis.shape[1]
    copies = [
        pltpu.make_async_copy(basis.at[at], out.at[:, :pv, :], sems.at[0]),
        pltpu.make_async_copy(factor.at[at], out.at[:, pv:, :], sems.at[1]),
    ]
    for copy in copies:
        copy.start()
    for copy in copies:
        copy.wait()


def places(owners, group):
    half = owners[group] // HALF
    rank = jnp.int32(0)
    for before in range(group):
        rank = rank + (owners[before] // HALF == half).astype(jnp.int32)
    return half, rank


def pick_kernel(owners, held, out):
    mine = lax.axis_index("col") // HALF
    for group in range(GROUPS):
        half, rank = places(owners, group)
        rank = jnp.minimum(rank, out.shape[0] - 1)

        @pl.when(half == mine)
        def _():
            out[rank] = held[lax.rem(owners[group], HALF)]


def order_kernel(owners, held, *refs):
    others, outs = refs[:-COLOURS], refs[-COLOURS:]
    mine = lax.axis_index("col") // HALF
    each = GROUPS // COLOURS
    for group in range(GROUPS):
        half, rank = places(owners, group)
        piece = held[lax.rem(owners[group], HALF)]
        for mask, ref in enumerate(others, 1):
            other = ref[jnp.minimum(rank, ref.shape[0] - 1)]
            piece = jnp.where(jnp.bitwise_xor(half, mine) == mask, other, piece)
        outs[group // each][0, group % each] = piece


def merge_kernel(rows, cols, tags, sub, *refs):
    held, total = refs[:-1], refs[-1]
    row, col = lax.axis_index("row"), lax.axis_index("col")
    deep, tall = held[0].shape[2], held[0].shape[1]
    total[...] = jnp.zeros_like(total)
    for own_tags, ref in zip(tags, held):
        for index, (row_mask, col_mask) in enumerate(own_tags):
            j = jnp.bitwise_xor(lax.rem(col, cols // rows), col_mask)
            part = jnp.dot(ref[index], sub[aligned(j, deep), :], preferred_element_type=jnp.float32)
            at = aligned(jnp.bitwise_xor(row, row_mask), tall)
            total[at, :] = total[at, :] + part


def two_terms(x):
    high = x.astype(jnp.bfloat16)
    low = (x - high.astype(jnp.float32)).astype(jnp.bfloat16)
    return jnp.concatenate([high, low], 0)


def both(products):
    half = products.shape[0] // 2
    return products[:half] + products[half:]


def chain_kernel(cols, groups, slots, masks, first, last, offsets, start, *refs):
    held, (out, basis_all, factor_all) = refs[: len(masks)], refs[len(masks) :]
    mine = slice_index()
    pv, pt = basis_all.shape[1] // SLICES, factor_all.shape[1] // SLICES
    for slot, own_masks, ref in zip(slots, masks, held):
        to = slice(slot, slot + ref.shape[1])
        for index, mask in enumerate(own_masks):
            e = jnp.bitwise_xor(mine, mask)
            basis_all[to, aligned(e, pv), :] = ref[index, :, :pv, :]
            factor_all[to, aligned(e, pt), :] = ref[index, :, pv:, :]
    if first:
        n, each, width = start.shape
        pieces = start[...].reshape(n // cols, cols, each, width).sum(0)
        x = jnp.concatenate([pieces[c] for c in range(cols)], 1)
        x = jnp.concatenate([x] + [jnp.zeros_like(x)] * (8 // each - 1), 0)
    else:
        x = start[...]
    wide = x.shape[1]
    group_rows = basis_all.shape[1]
    before = jnp.int32(0)
    for slot, group in enumerate(groups):
        offset = offsets[group]
        x = pltpu.roll(x, lax.rem(before - offset + wide, wide), 1)
        before = offset
        block = x[:, :group_rows]
        weights = both(
            jnp.dot(two_terms(block), basis_all[slot], preferred_element_type=jnp.float32)
        )
        scaled = both(
            lax.dot_general(
                two_terms(weights), factor_all[slot], (((1,), (1,)), ((), ())),
                preferred_element_type=jnp.float32,
            )
        )
        change = both(
            lax.dot_general(
                two_terms(scaled), basis_all[slot], (((1,), (1,)), ((), ())),
                preferred_element_type=jnp.float32,
            )
        )
        x = jnp.concatenate([block - change, x[:, group_rows:]], 1)
    x = pltpu.roll(x, before, 1)
    if last:
        out[...] = x[: out.shape[0]].astype(out.dtype)
    else:
        out[...] = x


def local(rows, cols, sub_vectors, merge_factor, reflectors, wy_factors, owners, offsets):
    share = cols // rows
    halves = cols // HALF

    def over_col(x, mask):
        return lax.ppermute(x, "col", [(c, c ^ mask) for c in range(cols)])

    def over_row(x, mask):
        return lax.ppermute(x, "row", [(r, r ^ mask) for r in range(rows)])

    basis, factor = reflectors[0], wy_factors[0]
    group_rows, reflect = basis.shape
    dtype = basis.dtype
    pv, pt = group_rows // SLICES, reflect // SLICES
    piece = (pv + pt, reflect)

    across = [merge_factor] + [over_col(merge_factor, m * share) for m in range(1, rows)]

    packed = pl.pallas_call(
        pack_kernel,
        out_shape=jax.ShapeDtypeStruct((HALF,) + piece, dtype),
        in_specs=[HBM, HBM],
        out_specs=VMEM,
        scratch_shapes=[pltpu.SemaphoreType.DMA((2,))],
        compiler_params=limit(56),
        cost_estimate=cost([basis, factor]),
        name="pack",
    )(basis.reshape(SLICES, pv, reflect), factor.reshape(SLICES, pt, reflect))
    members = [[h * HALF + c for c in range(HALF)] for h in range(halves)]
    slices = lax.all_to_all(packed, "col", 0, 0, axis_index_groups=members)

    row, top = lax.axis_index("row"), lax.axis_index("col") // share

    def for_row(mask):
        index = top ^ row ^ mask
        block = across[0]
        for k in range(1, rows):
            block = jnp.where(index == k, across[k], block)
        return block

    blocks = [for_row(0)] + [over_row(for_row(m), m) for m in range(1, rows)]
    groups = [range(rows // 2), range(rows // 2, rows)]
    sides = [jnp.stack([blocks[m] for m in group]) for group in groups]
    tags = [[(m, 0) for m in group] for group in groups]

    def double(side, bit):
        sides[side] = jnp.concatenate([sides[side], over_col(sides[side], bit)])
        tags[side] = tags[side] + [(m, c ^ bit) for m, c in tags[side]]

    bit = share // 2
    while bit > 4:
        double(0, bit)
        double(1, bit)
        bit //= 2
    double(0, 2)
    double(1, 4)
    slices, sides = lax.optimization_barrier((slices, sides))

    picked = pl.pallas_call(
        pick_kernel,
        out_shape=jax.ShapeDtypeStruct((GROUPS - 1,) + piece, dtype),
        in_specs=[SMEM, VMEM],
        out_specs=VMEM,
        compiler_params=limit(4),
        cost_estimate=cost([slices]),
        name="pick",
    )(owners, slices)
    others = [over_col(picked, m * HALF) for m in range(1, halves)]
    others, sides = lax.optimization_barrier((others, sides))
    late = jnp.concatenate([over_col(sides[0], 4), over_col(sides[1], 2)])
    late_tags = [(m, c ^ 4) for m, c in tags[0]] + [(m, c ^ 2) for m, c in tags[1]]
    m_held = [jnp.concatenate(sides), late]
    tags = [tags[0] + tags[1], late_tags]
    m_held += [over_col(x, 1) for x in m_held]
    tags += [[(m, c ^ 1) for m, c in ts] for ts in tags]
    wanted, width = merge_factor.shape[0] * rows, sub_vectors.shape[1]
    each = wanted // (rows * cols)
    merged = pl.pallas_call(
        functools.partial(merge_kernel, rows, cols, tags),
        out_shape=jax.ShapeDtypeStruct((wanted, width), jnp.float32),
        in_specs=[VMEM] + [VMEM] * len(m_held),
        out_specs=VMEM,
        compiler_params=limit(8),
        cost_estimate=cost([sub_vectors], 2 * wanted * sub_vectors.size),
        name="merge",
    )(sub_vectors, *m_held)
    per = GROUPS // COLOURS
    colours = pl.pallas_call(
        order_kernel,
        out_shape=[jax.ShapeDtypeStruct((1, per) + piece, dtype)] * COLOURS,
        in_specs=[SMEM, VMEM] + [VMEM] * len(others),
        out_specs=[VMEM] * COLOURS,
        compiler_params=limit(4),
        cost_estimate=cost([slices]),
        name="order",
    )(owners, slices, *others)
    colours = list(colours)
    links = [
        (HALF, lambda v: over_row(v, 1)),
        (2, lambda v: over_col(v, 2)),
        (4, lambda v: over_col(v, 4)),
    ]
    masks = [[0] for _ in range(COLOURS)]
    for step in range(2):
        for k in range(COLOURS):
            mask, send = links[(k + step) % 3]
            colours[k] = jnp.concatenate([colours[k], send(colours[k])])
            masks[k] = masks[k] + [m ^ mask for m in masks[k]]
    state = lax.all_to_all(merged.reshape(rows * cols, each, width), ("row", "col"), 0, 0)
    last_round = []
    for k in range(COLOURS):
        mask, send = links[(k + 2) % 3]
        last_round.append(send(colours[k]))
        masks[k] = [masks[k], [m ^ mask for m in masks[k]]]
        masks[k] += [[m ^ 1 for m in ms] for ms in masks[k]]
    last_round, state = lax.optimization_barrier((last_round, state))
    held = []
    for k in range(COLOURS):
        held.append([colours[k], last_round[k], over_col(colours[k], 1), over_col(last_round[k], 1)])

    wide = cols * width
    for members in CHAINS:
        first, last = members[0] == 0, members[-1] == COLOURS - 1
        groups = range(members[0] * per, (members[-1] + 1) * per)
        arrays = [x for k in members for x in held[k]]
        slots = [per * i for i, k in enumerate(members) for _ in held[k]]
        state = pl.pallas_call(
            functools.partial(
                chain_kernel, cols, groups, slots, sum((masks[k] for k in members), []), first, last
            ),
            out_shape=jax.ShapeDtypeStruct(
                (each, wide) if last else (8, wide), jnp.bfloat16 if last else jnp.float32
            ),
            in_specs=[SMEM, VMEM] + [VMEM] * len(arrays),
            out_specs=VMEM,
            scratch_shapes=[
                pltpu.VMEM((len(groups), group_rows, reflect), dtype),
                pltpu.VMEM((len(groups), reflect, reflect), dtype),
            ],
            compiler_params=limit(12),
            cost_estimate=cost(arrays, 2 * len(groups) * 64 * group_rows * reflect),
            name=f"chain{members[0]}",
        )(offsets, state, *arrays)
    return state


def solution(mesh):
    rows, cols = mesh.shape["row"], mesh.shape["col"]
    in_specs = (
        P("row", "col"),
        P("row", "col"),
        P("col", None, None),
        P("col", None, None),
        P(),
        P(),
    )
    out_specs = P(("row", "col"), None)
    return jax.shard_map(
        functools.partial(local, rows, cols),
        mesh=mesh,
        in_specs=in_specs,
        out_specs=out_specs,
        check_vma=False,
    )
```

```python
import functools

import jax
import jax.numpy as jnp
from jax import lax
from jax.experimental import pallas as pl
from jax.experimental.pallas import tpu as pltpu
from jax.sharding import PartitionSpec as P

GROUPS = 6
COLOURS = 3
CHAINS = ((0,), (1, 2))
HALF = 8
SLICES = 2 * HALF
VMEM = pl.BlockSpec(memory_space=pltpu.VMEM)
SMEM = pl.BlockSpec(memory_space=pltpu.SMEM)
HBM = pl.BlockSpec(memory_space=pltpu.HBM)


def limit(mib):
    return pltpu.CompilerParams(vmem_limit_bytes=mib * 1024 * 1024)


def cost(arrays, flops=0):
    size = sum(a.size * a.dtype.itemsize for a in arrays)
    return pl.CostEstimate(flops=flops, bytes_accessed=size, transcendentals=0)


def slice_index():
    row, col = lax.axis_index("row"), lax.axis_index("col")
    return lax.rem(row, 2) * HALF + lax.rem(col, HALF)


def aligned(index, size):
    return pl.ds(pl.multiple_of(index * size, size), size)


def pack_kernel(basis, factor, out, sems):
    at = aligned(lax.rem(lax.axis_index("row"), 2), HALF)
    pv = basis.shape[1]
    start = lax.rem(lax.axis_index("row"), 2) * HALF
    step = HALF // 4
    copies = [
        pltpu.make_async_copy(
            basis.at[pl.ds(start + k * step, step)],
            out.at[k * step : (k + 1) * step, :pv, :],
            sems.at[k],
        )
        for k in range(4)
    ]
    copies.append(pltpu.make_async_copy(factor.at[at], out.at[:, pv:, :], sems.at[4]))
    for copy in copies:
        copy.start()
    for copy in copies:
        copy.wait()


def places(owners, group):
    half = owners[group] // HALF
    rank = jnp.int32(0)
    for before in range(group):
        rank = rank + (owners[before] // HALF == half).astype(jnp.int32)
    return half, rank


def pick_kernel(owners, held, out):
    mine = lax.axis_index("col") // HALF
    for group in range(GROUPS):
        half, rank = places(owners, group)
        rank = jnp.minimum(rank, out.shape[0] - 1)

        @pl.when(half == mine)
        def _():
            out[rank] = held[lax.rem(owners[group], HALF)]


def order_kernel(owners, held, *refs):
    others, outs = refs[:-COLOURS], refs[-COLOURS:]
    mine = lax.axis_index("col") // HALF
    each = GROUPS // COLOURS
    for group in range(GROUPS):
        half, rank = places(owners, group)
        piece = held[lax.rem(owners[group], HALF)]
        for mask in range(1, len(others) // 2 + 1):
            head, tail = others[2 * mask - 2 : 2 * mask]
            other = tail[jnp.clip(rank - 1, 0, tail.shape[0] - 1)]
            other = jnp.where(rank == 0, head[0], other)
            piece = jnp.where(jnp.bitwise_xor(half, mine) == mask, other, piece)
        outs[group // each][0, group % each] = piece


def merge_kernel(rows, cols, tags, sub, *refs):
    held, total = refs[:-1], refs[-1]
    row, col = lax.axis_index("row"), lax.axis_index("col")
    deep, tall = held[0].shape[2], held[0].shape[1]
    total[...] = jnp.zeros_like(total)
    for own_tags, ref in zip(tags, held):
        for index, (row_mask, col_mask) in enumerate(own_tags):
            j = jnp.bitwise_xor(lax.rem(col, cols // rows), col_mask)
            part = jnp.dot(ref[index], sub[aligned(j, deep), :], preferred_element_type=jnp.float32)
            at = aligned(jnp.bitwise_xor(row, row_mask), tall)
            total[at, :] = total[at, :] + part


def two_terms(x):
    high = x.astype(jnp.bfloat16)
    low = (x - high.astype(jnp.float32)).astype(jnp.bfloat16)
    return jnp.concatenate([high, low], 0)


def both(products):
    half = products.shape[0] // 2
    return products[:half] + products[half:]


def chain_kernel(cols, groups, slots, masks, first, last, offsets, start, *refs):
    held, (out, basis_all, factor_all) = refs[: len(masks)], refs[len(masks) :]
    mine = slice_index()
    pv, pt = basis_all.shape[1] // SLICES, factor_all.shape[1] // SLICES
    for slot, own_masks, ref in zip(slots, masks, held):
        to = slice(slot, slot + ref.shape[1])
        for index, mask in enumerate(own_masks):
            e = jnp.bitwise_xor(mine, mask)
            basis_all[to, aligned(e, pv), :] = ref[index, :, :pv, :]
            factor_all[to, aligned(e, pt), :] = ref[index, :, pv:, :]
    if first:
        n, each, width = start.shape
        pieces = start[...].reshape(n // cols, cols, each, width).sum(0)
        x = jnp.concatenate([pieces[c] for c in range(cols)], 1)
        x = jnp.concatenate([x] + [jnp.zeros_like(x)] * (8 // each - 1), 0)
    else:
        x = start[...]
    wide = x.shape[1]
    group_rows = basis_all.shape[1]
    before = jnp.int32(0)
    for slot, group in enumerate(groups):
        offset = offsets[group]
        x = pltpu.roll(x, lax.rem(before - offset + wide, wide), 1)
        before = offset
        block = x[:, :group_rows]
        weights = both(
            jnp.dot(two_terms(block), basis_all[slot], preferred_element_type=jnp.float32)
        )
        scaled = both(
            lax.dot_general(
                two_terms(weights), factor_all[slot], (((1,), (1,)), ((), ())),
                preferred_element_type=jnp.float32,
            )
        )
        change = both(
            lax.dot_general(
                two_terms(scaled), basis_all[slot], (((1,), (1,)), ((), ())),
                preferred_element_type=jnp.float32,
            )
        )
        x = jnp.concatenate([block - change, x[:, group_rows:]], 1)
    x = pltpu.roll(x, before, 1)
    if last:
        out[...] = x[: out.shape[0]].astype(out.dtype)
    else:
        out[...] = x


def local(rows, cols, sub_vectors, merge_factor, reflectors, wy_factors, owners, offsets):
    share = cols // rows
    halves = cols // HALF

    def over_col(x, mask):
        return lax.ppermute(x, "col", [(c, c ^ mask) for c in range(cols)])

    def over_row(x, mask):
        return lax.ppermute(x, "row", [(r, r ^ mask) for r in range(rows)])

    basis, factor = reflectors[0], wy_factors[0]
    group_rows, reflect = basis.shape
    dtype = basis.dtype
    pv, pt = group_rows // SLICES, reflect // SLICES
    piece = (pv + pt, reflect)

    across = [merge_factor] + [over_col(merge_factor, m * share) for m in range(1, rows)]

    packed = pl.pallas_call(
        pack_kernel,
        out_shape=jax.ShapeDtypeStruct((HALF,) + piece, dtype),
        in_specs=[HBM, HBM],
        out_specs=VMEM,
        scratch_shapes=[pltpu.SemaphoreType.DMA((5,))],
        compiler_params=limit(56),
        cost_estimate=cost([basis, factor]),
        name="pack",
    )(basis.reshape(SLICES, pv, reflect), factor.reshape(SLICES, pt, reflect))
    members = [[h * HALF + c for c in range(HALF)] for h in range(halves)]
    slices = lax.all_to_all(packed, "col", 0, 0, axis_index_groups=members)

    row, top = lax.axis_index("row"), lax.axis_index("col") // share

    def for_row(mask):
        index = top ^ row ^ mask
        block = across[0]
        for k in range(1, rows):
            block = jnp.where(index == k, across[k], block)
        return block

    blocks = [for_row(0)] + [over_row(for_row(m), m) for m in range(1, rows)]
    groups = [range(rows // 2), range(rows // 2, rows)]
    sides = [jnp.stack([blocks[m] for m in group]) for group in groups]
    tags = [[(m, 0) for m in group] for group in groups]

    def double(side, bit):
        sides[side] = jnp.concatenate([sides[side], over_col(sides[side], bit)])
        tags[side] = tags[side] + [(m, c ^ bit) for m, c in tags[side]]

    bit = share // 2
    while bit > 4:
        double(0, bit)
        double(1, bit)
        bit //= 2
    double(0, 2)
    double(1, 4)
    slices, sides = lax.optimization_barrier((slices, sides))

    picked = pl.pallas_call(
        pick_kernel,
        out_shape=jax.ShapeDtypeStruct((GROUPS - 1,) + piece, dtype),
        in_specs=[SMEM, VMEM],
        out_specs=VMEM,
        compiler_params=limit(4),
        cost_estimate=cost([slices]),
        name="pick",
    )(owners, slices)
    heads = [over_col(picked[:1], m * HALF) for m in range(1, halves)]
    tails = [over_col(picked[1:], m * HALF) for m in range(1, halves)]
    heads, sides = lax.optimization_barrier((heads, sides))
    others = [x for pair in zip(heads, tails) for x in pair]
    late = jnp.concatenate([over_col(sides[0], 4), over_col(sides[1], 2)])
    late_tags = [(m, c ^ 4) for m, c in tags[0]] + [(m, c ^ 2) for m, c in tags[1]]
    m_held = [jnp.concatenate(sides), late]
    tags = [tags[0] + tags[1], late_tags]
    m_held += [over_col(x, 1) for x in m_held]
    tags += [[(m, c ^ 1) for m, c in ts] for ts in tags]
    wanted, width = merge_factor.shape[0] * rows, sub_vectors.shape[1]
    each = wanted // (rows * cols)
    merged = pl.pallas_call(
        functools.partial(merge_kernel, rows, cols, tags),
        out_shape=jax.ShapeDtypeStruct((wanted, width), jnp.float32),
        in_specs=[VMEM] + [VMEM] * len(m_held),
        out_specs=VMEM,
        compiler_params=limit(8),
        cost_estimate=cost([sub_vectors], 2 * wanted * sub_vectors.size),
        name="merge",
    )(sub_vectors, *m_held)
    per = GROUPS // COLOURS
    colours = pl.pallas_call(
        order_kernel,
        out_shape=[jax.ShapeDtypeStruct((1, per) + piece, dtype)] * COLOURS,
        in_specs=[SMEM, VMEM] + [VMEM] * len(others),
        out_specs=[VMEM] * COLOURS,
        compiler_params=limit(4),
        cost_estimate=cost([slices]),
        name="order",
    )(owners, slices, *others)
    colours = list(colours)
    links = [
        (HALF, lambda v: over_row(v, 1)),
        (2, lambda v: over_col(v, 2)),
        (4, lambda v: over_col(v, 4)),
    ]
    masks = [[0] for _ in range(COLOURS)]
    for step in range(2):
        for k in range(COLOURS):
            mask, send = links[(k + step) % 3]
            colours[k] = jnp.concatenate([colours[k], send(colours[k])])
            masks[k] = masks[k] + [m ^ mask for m in masks[k]]
    state = lax.all_to_all(merged.reshape(rows * cols, each, width), ("row", "col"), 0, 0)
    last_round = []
    for k in range(COLOURS):
        mask, send = links[(k + 2) % 3]
        last_round.append(send(colours[k]))
        masks[k] = [masks[k], [m ^ mask for m in masks[k]]]
        masks[k] += [[m ^ 1 for m in ms] for ms in masks[k]]
    last_round, state = lax.optimization_barrier((last_round, state))
    held = []
    for k in range(COLOURS):
        held.append([colours[k], last_round[k], over_col(colours[k], 1), over_col(last_round[k], 1)])

    wide = cols * width
    for members in CHAINS:
        first, last = members[0] == 0, members[-1] == COLOURS - 1
        groups = range(members[0] * per, (members[-1] + 1) * per)
        arrays = [x for k in members for x in held[k]]
        slots = [per * i for i, k in enumerate(members) for _ in held[k]]
        state = pl.pallas_call(
            functools.partial(
                chain_kernel, cols, groups, slots, sum((masks[k] for k in members), []), first, last
            ),
            out_shape=jax.ShapeDtypeStruct(
                (each, wide) if last else (8, wide), jnp.bfloat16 if last else jnp.float32
            ),
            in_specs=[SMEM, VMEM] + [VMEM] * len(arrays),
            out_specs=VMEM,
            scratch_shapes=[
                pltpu.VMEM((len(groups), group_rows, reflect), dtype),
                pltpu.VMEM((len(groups), reflect, reflect), dtype),
            ],
            compiler_params=limit(12),
            cost_estimate=cost(arrays, 2 * len(groups) * 64 * group_rows * reflect),
            name=f"chain{members[0]}",
        )(offsets, state, *arrays)
    return state


def solution(mesh):
    rows, cols = mesh.shape["row"], mesh.shape["col"]
    in_specs = (
        P("row", "col"),
        P("row", "col"),
        P("col", None, None),
        P("col", None, None),
        P(),
        P(),
    )
    out_specs = P(("row", "col"), None)
    return jax.shard_map(
        functools.partial(local, rows, cols),
        mesh=mesh,
        in_specs=in_specs,
        out_specs=out_specs,
        check_vma=False,
    )
```
